256 devices in a mesh: row: 32 (over y, z), col: 8 (over x, core).
Axes of the slice: x: 4, y: 4, z: 8, core: 2. Of those that a mesh axis runs over, the one named last changes fastest.
Arguments:
- lower: bfloat16 [8, 32, 512, 1, 8, 512], P(None, 'row', None, None, 'col'), may hold values from -0.125 to 0.125
- slab: float32 [8, 32, 512, 128], P(None, 'row'), may hold values from -6 to 6
- inverses: float32 [1, 8, 512, 512], P(None, 'col'), may hold values from -0.12374368670764582 to 2, as said below
Outputs:
- reduced: float32 [8, 32, 512, 128], P('col', 'row')
The draws below stay inside these ranges and needn't reach their ends.
Inputs may be any that keep to these rules, and one draw needn't show every extreme that they name: `inverses`: each block is lower triangular with a positive diagonal.
All inputs are finite; a program needn't handle non-finite values.
Results may differ from the reference program's by a relative error of at most 0.0075.
Values may be sent and summed in bfloat16 or wider, within the bound.
A program may use at most 64 MiB of HBM per device.

```python
import math
import jax
import jax.numpy as jnp
from jax import lax

B = 512
W = 128
RB_DEV = 8
SC_DEV = 1
N_ROW = 32
N_COL = 8


def draw_inverses(key, part):
    key = jax.random.fold_in(key, 7)
    key_diag, key_below = jax.random.split(key)
    full_shape = (SC_DEV, N_COL, B, B)
    row_index = lax.broadcasted_iota(jnp.int32, full_shape, 2)
    col_index = lax.broadcasted_iota(jnp.int32, full_shape, 3)
    spread = 0.7 / math.sqrt(B)
    diagonal = jnp.exp(jax.random.uniform(key_diag, full_shape, jnp.float32, math.log(1.0), math.log(2.0)))
    below = jnp.clip(jax.random.normal(key_below, full_shape, jnp.float32), -4.0, 4.0)
    return jnp.where(row_index == col_index, diagonal, jnp.where(row_index > col_index, below * spread, jnp.float32(0)))


def block_scale(own_key, dims, cuts, least, top_value):
    gain = 1.0
    for dim, parts in cuts:
        steps = jax.random.uniform(jax.random.fold_in(jax.random.fold_in(own_key, 6), dim), (parts,), jnp.float32, least / len(cuts), top_value / len(cuts))
        gain = gain * jnp.repeat(jnp.exp(steps), dims[dim] // parts).reshape((-1,) + (1,) * (len(dims) - 1 - dim))
    return gain


def normal_values(own_key, shape, scale, reach, shards=(), kind=jnp.bfloat16):
    array = scale * jax.random.normal(own_key, shape, jnp.float32)
    if shards:
        array = array * block_scale(own_key, shape, shards, -0.22, 0.18)
    return jnp.clip(array, -reach, reach).astype(kind)


def setup_inputs(seed: int = 0) -> dict:
    keys = jax.random.split(jax.random.key(seed), 4)
    return {
        "lower": normal_values(keys[0], (RB_DEV, N_ROW, B, SC_DEV, N_COL, B), (SC_DEV * N_COL * B // 2) ** -0.5, 0.125, ((1, 32), (4, 8))),
        "slab": normal_values(keys[1], (RB_DEV, N_ROW, B, W), 1.0, 6.0, ((1, 32),), jnp.float32),
        "inverses": draw_inverses(jax.random.fold_in(keys[3], 71), 0),
    }


def reference(lower, slab, inverses):
    block_count = RB_DEV * N_ROW
    step_count = SC_DEV * N_COL
    panel_blocks = lower.reshape(block_count, B, step_count, B)
    right_side = slab.reshape(block_count, B, W)
    inverse_blocks = inverses.reshape(step_count, B, B)
    block_ids = jnp.arange(block_count)
    accumulated = jnp.zeros((block_count, B, W), jnp.float32)
    solved = []
    for step_index in range(step_count):
        residue = right_side[step_index] - accumulated[step_index]
        x_now = jnp.dot(inverse_blocks[step_index], residue, precision=lax.Precision.HIGHEST, preferred_element_type=jnp.float32)
        solved.append(x_now)
        x_low = x_now.astype(jnp.bfloat16)
        column = panel_blocks[:, :, step_index, :].reshape(block_count * B, B).astype(jnp.float32)
        update = jnp.dot(column, x_low.astype(jnp.float32), preferred_element_type=jnp.float32).reshape(block_count, B, W)
        accumulated = accumulated + jnp.where((block_ids > step_index)[:, None, None], update, jnp.float32(0))
    result = right_side - accumulated
    result = result.at[:step_count].set(jnp.stack(solved))
    return result.reshape(RB_DEV, N_ROW, B, W)
```

```python
import jax
import jax.numpy as jnp
from jax import lax
from jax.experimental import pallas as pl
from jax.experimental.pallas import tpu as pltpu
from jax.sharding import PartitionSpec as P

MESH = pl.DeviceIdType.MESH
F32 = jnp.float32
BF16 = jnp.bfloat16

N_Z, N_Y, N_X = 8, 4, 4
SOLVE_0 = (0, 0)
SOLVE_1 = (1, 0)
SOLVE_23 = (2, 1)
SOLVE_47 = (6, 4)
INVERSE_SENDS = (
    ((1, 1), SOLVE_1, 0),
    ((10, 2), SOLVE_23, 0),
    ((26, 3), SOLVE_23, 1),
    ((6, 5), SOLVE_47, 1),
    ((14, 6), SOLVE_47, 2),
    ((30, 7), SOLVE_47, 3),
)
BLOCK_SENDS = (
    ((3, 1), SOLVE_23, 0),
    ((3, 2), SOLVE_23, 1),
    ((5, 4), SOLVE_47, 0),
    ((6, 5), SOLVE_47, 1),
    ((7, 4), SOLVE_47, 2),
    ((7, 5), SOLVE_47, 3),
    ((7, 6), SOLVE_47, 4),
)


def special_pairs():
    pairs = {(s, t) for s, t, _ in INVERSE_SENDS} | {(s, t) for s, t, _ in BLOCK_SENDS}
    pairs |= {(SOLVE_1, (z, 1)) for z in range(N_Z)}
    pairs |= {((3, 0), SOLVE_23)}
    pairs |= {(SOLVE_23, (2, c)) for c in (2, 3)}
    pairs |= {(SOLVE_23, (r, c)) for c in (2, 3) for r in range(4, 8)}
    pairs |= {((r, c), SOLVE_47) for c in (1, 3) for r in range(4, 8)}
    pairs |= {(SOLVE_47, (6, c)) for c in (5, 6, 7)}
    pairs |= {(SOLVE_47, (r, 0)) for r in range(4, 8)}
    return sorted({tuple(sorted(p)) for p in pairs})


def kernel(
    lower, slab, inverses, out,
    panel, inv, inv_parts, blocks, right, right_own, x_own, x_stage, x_full, x_in,
    acc_f, acc_b, stage_f, stage_b, pair_out, pair_in, sums, cross_in,
    load_sem, send_sem, x_sem, x_in_sem, inv_sem, block_sem, acc_f_sem, acc_b_sem, pair_sem, cross_sem,
):
    row = lax.axis_index("row")
    col = lax.axis_index("col")
    y, z = row // N_Z, row % N_Z
    x, core = col // 2, col % 2
    half = panel.shape[1] // 2
    quarter = half // 2
    width = x_own.shape[1]

    def here(device):
        return (row == device[0]) & (col == device[1])

    def plane_row(r0, r1):
        return (row >= r0) & (row < r1)

    root_z = jnp.where(col < 2, col, jnp.where(col < 4, 2, 6))
    sibling = (row, col + 1 - 2 * core)
    pending = []

    def remote(src, dst, s, recv, device):
        return pltpu.make_async_remote_copy(
            src_ref=src, dst_ref=dst, send_sem=send_sem.at[s], recv_sem=recv, device_id=device, device_id_type=MESH
        )

    def send(when, src, dst, s, recv, device):
        remote(src, dst, s, recv, device).start()
        pending.append((when, s, src.shape, src.dtype))

    def arrived(dst, recv):
        remote(dst, dst, 0, recv, sibling).wait_recv()

    load_first = pltpu.make_async_copy(lower.at[0], panel.at[0], load_sem.at[0])
    load_rest = pltpu.make_async_copy(lower.at[pl.ds(1, 7)], panel.at[pl.ds(1, 7)], load_sem.at[1])
    load_inv = pltpu.make_async_copy(inverses, inv, load_sem.at[2])
    load_right = pltpu.make_async_copy(slab.at[0], right, load_sem.at[3])
    load_own = pltpu.make_async_copy(slab.at[col], right_own, load_sem.at[4])
    load_inv.start()
    load_right.start()
    load_first.start()
    load_rest.start()
    load_own.start()

    def clear_slot(slot):
        inv_parts[slot] = jnp.zeros(inv_parts.shape[1:], BF16)

    @pl.when(here(SOLVE_1))
    def _():
        clear_slot(0)

    @pl.when(here(SOLVE_23))
    def _():
        clear_slot(0)
        clear_slot(1)

    @pl.when(here(SOLVE_47))
    def _():
        clear_slot(1)
        clear_slot(2)
        clear_slot(3)

    barrier = pltpu.get_barrier_semaphore()

    def greet(device):
        pl.semaphore_signal(barrier, inc=1, device_id=device, device_id_type=MESH)

    greet(sibling)
    for d in range(1, N_X):
        greet((row, (x + d) % N_X * 2 + core))
    count = jnp.int32(N_X)
    is_root = z == root_z

    @pl.when(is_root)
    def _():
        for d in range(1, N_Z):
            greet((y * N_Z + (z + d) % N_Z, col))

    @pl.when(jnp.logical_not(is_root))
    def _():
        greet((y * N_Z + root_z, col))

    count += jnp.where(is_root, N_Z - 1, 1)

    @pl.when(is_root & (y == 0))
    def _():
        for d in range(1, N_Y):
            greet((d * N_Z + z, col))

    @pl.when(is_root & (y != 0))
    def _():
        greet((z, col))

    count += jnp.where(is_root, jnp.where(y == 0, N_Y - 1, 1), 0)
    partners = {}
    for a, b in special_pairs():
        partners.setdefault(a, []).append(b)
        partners.setdefault(b, []).append(a)
    for device, others in partners.items():
        count += jnp.where(here(device), len(others), 0)

        @pl.when(here(device))
        def _(others=others):
            for other in others:
                greet(other)

    pl.semaphore_wait(barrier, count)

    def split_inverse(slot):
        value = inv[...]
        high = value.astype(BF16)
        inv_parts[slot, 0] = high
        inv_parts[slot, 1] = (value - high.astype(F32)).astype(BF16)

    for source, solver, slot in BLOCK_SENDS:

        @pl.when(here(source))
        def _(source=source, solver=solver, slot=slot):
            send(source, lower.at[0], blocks.at[slot], 0, block_sem.at[slot], solver)

    def part(slot, piece, b):
        return inv_parts.at[slot, piece, pl.ds(b * quarter, quarter), pl.ds(0, (b + 1) * quarter)]

    is_source = here(INVERSE_SENDS[0][0])
    for source, _, _ in INVERSE_SENDS[1:]:
        is_source |= here(source)

    @pl.when(is_source)
    def _():
        load_inv.wait()
        split_inverse(0)

    for source, solver, slot in INVERSE_SENDS:

        @pl.when(here(source))
        def _(source=source, solver=solver, slot=slot):
            for piece in range(2):
                for b in range(4):
                    s = 1 + piece * 4 + b
                    send(source, part(0, piece, b), part(slot, piece, b), s, inv_sem.at[slot, piece, b], solver)

    def inverse_arrived(slot):
        for piece in range(2):
            for b in range(4):
                arrived(part(slot, piece, b), inv_sem.at[slot, piece, b])

    def solve(slot, total):
        high = total.astype(BF16)
        low = (total - high.astype(F32)).astype(BF16)
        both = jnp.concatenate([high, low], axis=1)

        def times(rows, depth):
            a = inv_parts[slot, 0, rows, :depth]
            b = inv_parts[slot, 1, rows, :depth]
            return jnp.dot(a, both[:depth], preferred_element_type=F32) + jnp.dot(
                b, both[:depth], preferred_element_type=F32
            )

        whole = jnp.concatenate([times(slice(0, half), half), times(slice(half, 2 * half), 2 * half)], axis=0)
        return whole[:, :width] + whole[:, width:]

    def product(block, value):
        return jnp.dot(block, value, preferred_element_type=F32)

    @pl.when(here(SOLVE_0))
    def _():
        load_inv.wait()
        split_inverse(0)
        load_right.wait()
        value = solve(0, right[...])
        x_own[...] = value.astype(BF16)
        x_full[0] = value

    column_root = [SOLVE_0, (1, 1), (2, 2), (2, 3), SOLVE_47, (6, 5), (6, 6), (6, 7)]
    in_plane = [(1, 2, 3, 4, 5, 6, 7), (), (0, 1, 3), (0, 1, 3)] + [(2, 1, 3, 0, 4, 7, 5)] * 4

    def spread_from_root(c):
        when = column_root[c]
        root_row = column_root[c][0]
        for i, target in enumerate(in_plane[c][:1]):
            send(when, x_own, x_own, 9 + i, x_sem, (target, c))
        for d in (2, 1, 3):
            send(when, x_own, x_own, 15 + d, x_sem, (d * N_Z + root_row, c))
        for i, target in enumerate(in_plane[c]):
            if i > 0:
                send(when, x_own, x_own, 9 + i, x_sem, (target, c))

    @pl.when(here(SOLVE_0))
    def _():
        spread_from_root(0)

    @pl.when(here(SOLVE_1))
    def _():
        load_right.wait()
        load_first.wait()
        inverse_arrived(0)
        arrived(x_own, x_sem)
        value = solve(0, right[...] - product(panel[0], x_own[...]))
        x_stage[0] = value.astype(BF16)
        x_full[0] = value
        for i, target in enumerate((2, 3, 1, 4, 5, 6, 7, 0)):
            send(SOLVE_1, x_stage.at[0], x_own, 9 + i, x_sem, (target, 1))

    def rows_of(c, r0, r1):
        return plane_row(r0, r1) & (col == c)

    @pl.when(rows_of(0, 2, 8))
    def _():
        load_right.wait()
        load_first.wait()
        arrived(x_own, x_sem)
        stage_f[...] = right[...] - product(panel[0], x_own[...])

    @pl.when(here((3, 0)))
    def _():
        send((3, 0), stage_f, acc_f.at[1], 19, acc_f_sem.at[1], SOLVE_23)

    to_sibling = rows_of(0, 2, 8) & (row != 3)

    @pl.when(to_sibling)
    def _():
        send(to_sibling, stage_f, acc_f.at[0], 19, acc_f_sem.at[0], sibling)

    for r in range(4, 8):

        @pl.when(here((r, 1)))
        def _(r=r):
            load_right.wait()
            load_first.wait()
            arrived(x_own, x_sem)
            arrived(acc_f.at[0], acc_f_sem.at[0])
            stage_f[...] = acc_f[0] - product(panel[0], x_own[...])
            send((r, 1), stage_f, acc_f.at[r - 2], 19, acc_f_sem.at[r - 2], SOLVE_47)

    @pl.when(here(SOLVE_23))
    def _():
        when = SOLVE_23
        load_right.wait()
        load_first.wait()
        arrived(acc_f.at[0], acc_f_sem.at[0])
        arrived(x_own, x_sem)
        total = acc_f[0] - product(panel[0], x_own[...])
        inverse_arrived(0)
        value = solve(0, total)
        x_stage[0] = value.astype(BF16)
        x_full[0] = value
        for i, r in enumerate((4, 5, 7, 6)):
            send(when, x_stage.at[0], x_own, 20 + i, x_sem, (r, 2))
        arrived(blocks.at[0], block_sem.at[0])
        arrived(acc_f.at[1], acc_f_sem.at[1])
        stage_f[...] = acc_f[1] - product(blocks[0], x_own[...])
        arrived(blocks.at[1], block_sem.at[1])
        total = stage_f[...] - product(blocks[1], x_stage[0])
        inverse_arrived(1)
        value = solve(1, total)
        x_stage[1] = value.astype(BF16)
        x_full[1] = value
        for i, r in enumerate((4, 5, 7, 6)):
            send(when, x_stage.at[1], x_own, 24 + i, x_sem, (r, 3))
        send(when, x_stage.at[0], x_own, 28, x_sem, (2, 2))
        send(when, x_stage.at[1], x_own, 29, x_sem, (2, 3))
        send(when, x_full.at[0], x_in, 30, x_in_sem, (2, 0))
        send(when, x_full.at[1], x_in, 31, x_in_sem, (3, 0))

    low_rows = rows_of(2, 4, 8)

    @pl.when(low_rows)
    def _():
        load_first.wait()
        arrived(x_own, x_sem)
        stage_f[...] = product(panel[0], x_own[...])
        send(low_rows, stage_f, acc_f.at[0], 19, acc_f_sem.at[0], sibling)

    for r in range(4, 8):

        @pl.when(here((r, 3)))
        def _(r=r):
            load_first.wait()
            arrived(acc_f.at[0], acc_f_sem.at[0])
            arrived(x_own, x_sem)
            stage_b[...] = (acc_f[0] + product(panel[0], x_own[...])).astype(BF16)
            send((r, 3), stage_b, acc_b.at[r - 4], 19, acc_b_sem.at[r - 4], SOLVE_47)

    @pl.when(here(SOLVE_47))
    def _():
        when = SOLVE_47
        load_inv.wait()
        split_inverse(0)
        load_first.wait()
        load_right.wait()
        place = {(1, 0): blocks.at[0], (2, 0): panel.at[0], (2, 1): blocks.at[1]}
        place |= {(3, 0): blocks.at[2], (3, 1): blocks.at[3], (3, 2): blocks.at[4]}
        for slot in range(5):
            arrived(blocks.at[slot], block_sem.at[slot])
        for slot in range(1, 4):
            inverse_arrived(slot)
        for q in range(4):
            arrived(acc_f.at[q + 2], acc_f_sem.at[q + 2])
            for j in range(q - 1):
                acc_f[q + 2] -= product(place[q, j][...], x_stage[j])
            total = acc_f[q + 2]
            if q > 0:
                total -= product(place[q, q - 1][...], x_stage[q - 1])
            arrived(acc_b.at[q], acc_b_sem.at[q])
            total -= acc_b[q].astype(F32)
            value = solve(q, total)
            x_stage[q] = value.astype(BF16)
            x_full[q] = value
            if q == 0:
                x_own[...] = x_stage[0]
            else:
                send(when, x_stage.at[q], x_own, 20 + q, x_sem, (6, 4 + q))
        spread_from_root(4)
        for q in range(4):
            send(when, x_full.at[q], x_in, 24 + q, x_in_sem, (4 + q, 0))

    waited = rows_of(0, 0, 8) | (plane_row(4, 8) & (col < 4)) | here(SOLVE_23) | here(SOLVE_47)

    @pl.when(jnp.logical_not(waited))
    def _():
        arrived(x_own, x_sem)

    for c in (1, 2, 3, 5, 6, 7):

        @pl.when(here(column_root[c]))
        def _(c=c):
            spread_from_root(c)

    relay = is_root & (y != 0)
    peers = [(i, (y * N_Z + (z + d) % N_Z, col)) for i, d in enumerate((4, 3, 5, 2, 6, 1, 7))]

    @pl.when(relay)
    def _():
        for i, peer in peers:
            send(relay, x_own, x_own, 9 + i, x_sem, peer)

    always = row >= 0
    waited_first = (plane_row(2, 8) & (col < 4)) | here(SOLVE_1) | here(SOLVE_47)
    waited_first = waited_first & jnp.logical_not((col > 1) & (row < 4)) & jnp.logical_not(here((2, 1)))
    waited_first = waited_first & jnp.logical_not(here((3, 1))) | here(SOLVE_23)

    @pl.when(jnp.logical_not(waited_first))
    def _():
        load_first.wait()

    load_rest.wait()
    value = x_own[...]
    for i in range(4):
        pair_out[i] = product(panel[2 * i + 1 - core], value).astype(BF16)
    send(always, pair_out, pair_in, 32, pair_sem, sibling)
    for i in range(4):
        sums[i] = product(panel[2 * i + core], value).astype(BF16)
    arrived(pair_in, pair_sem)
    for i in range(4):
        sums[i] = (sums[i].astype(F32) + pair_in[i].astype(F32)).astype(BF16)
    for d in (2, 1, 3):
        owner = (x + d) % N_X
        send(always, sums.at[owner], cross_in.at[d - 1], 32 + d, cross_sem.at[d - 1], (row, owner * 2 + core))

    load_own.wait()
    total = right_own[...] - sums[x].astype(F32)
    for d in range(3):
        arrived(cross_in.at[d], cross_sem.at[d])
        total -= cross_in[d].astype(F32)
    out[...] = total

    solved = plane_row(0, 8) & (col == 0)

    @pl.when(solved & (row < 2))
    def _():
        out[...] = x_full[0]

    @pl.when(solved & (row >= 2))
    def _():
        arrived(x_in, x_in_sem)
        out[...] = x_in[...]

    @pl.when(jnp.logical_not(is_source | here(SOLVE_0) | here(SOLVE_47)))
    def _():
        load_inv.wait()

    read_right = plane_row(2, 8) & (col == 0) | plane_row(4, 8) & (col == 1)
    read_right = read_right | here(SOLVE_0) | here(SOLVE_1) | here(SOLVE_23) | here(SOLVE_47)

    @pl.when(jnp.logical_not(read_right))
    def _():
        load_right.wait()

    buffers = [x_own, stage_f, pair_out]

    def same_size(shape, dtype):
        for buffer in buffers:
            if buffer.shape == shape and buffer.dtype == dtype:
                return buffer
        if shape == panel.shape[1:]:
            return panel.at[0]
        return part(0, 0, shape[1] // quarter - 1)

    for when, s, shape, dtype in pending:

        @pl.when(when if not isinstance(when, tuple) else here(when))
        def _(s=s, shape=shape, dtype=dtype):
            ref = same_size(shape, dtype)
            remote(ref, ref, s, x_sem, sibling).wait_send()


def body(lower, slab, inverses):
    row_blocks, _, order, _, _, _ = lower.shape
    width = slab.shape[3]
    vmem = pltpu.VMEM
    dma = pltpu.SemaphoreType.DMA
    scratch = [
        vmem((row_blocks, order, order), BF16),
        vmem((order, order), F32),
        vmem((4, 2, order, order), BF16),
        vmem((5, order, order), BF16),
        vmem((order, width), F32),
        vmem((order, width), F32),
        vmem((order, width), BF16),
        vmem((4, order, width), BF16),
        vmem((4, order, width), F32),
        vmem((order, width), F32),
        vmem((6, order, width), F32),
        vmem((4, order, width), BF16),
        vmem((order, width), F32),
        vmem((order, width), BF16),
        vmem((4, order, width), BF16),
        vmem((4, order, width), BF16),
        vmem((4, order, width), BF16),
        vmem((3, order, width), BF16),
        dma((5,)),
        dma((36,)),
        dma,
        dma,
        dma((4, 2, 4)),
        dma((5,)),
        dma((6,)),
        dma((4,)),
        dma,
        dma((3,)),
    ]
    result = pl.pallas_call(
        kernel,
        name="window_solve",
        out_shape=jax.ShapeDtypeStruct((order, width), F32),
        in_specs=[pl.BlockSpec(memory_space=pl.ANY)] * 3,
        out_specs=pl.BlockSpec(memory_space=pltpu.VMEM),
        scratch_shapes=scratch,
        compiler_params=pltpu.CompilerParams(
            collective_id=0, has_side_effects=True, vmem_limit_bytes=40 << 20
        ),
    )(
        lower.reshape(row_blocks, order, order),
        slab.reshape(row_blocks, order, width),
        inverses.reshape(order, order),
    )
    return result.reshape(1, 1, order, width)


def solution(mesh):
    in_specs = (
        P(None, "row", None, None, "col", None),
        P(None, "row", None, None),
        P(None, "col", None, None),
    )
    out_specs = P("col", "row", None, None)
    return jax.shard_map(body, mesh=mesh, in_specs=in_specs, out_specs=out_specs, check_vma=False)
```

```python
import jax
import jax.numpy as jnp
from jax import lax
from jax.experimental import pallas as pl
from jax.experimental.pallas import tpu as pltpu
from jax.sharding import PartitionSpec as P

MESH = pl.DeviceIdType.MESH
F32 = jnp.float32
BF16 = jnp.bfloat16

N_Z, N_Y, N_X = 8, 4, 4
SOLVE_0 = (0, 0)
SOLVE_1 = (1, 0)
SOLVE_23 = (2, 1)
SOLVE_47 = (6, 4)
INVERSE_SENDS = (
    ((1, 1), SOLVE_1, 0),
    ((10, 2), SOLVE_23, 0),
    ((26, 3), SOLVE_23, 1),
    ((6, 5), SOLVE_47, 1),
    ((14, 6), SOLVE_47, 2),
    ((30, 7), SOLVE_47, 3),
)
BLOCK_SENDS = (
    ((3, 1), SOLVE_23, 0),
    ((3, 2), SOLVE_23, 1),
    ((5, 4), SOLVE_47, 0),
    ((6, 5), SOLVE_47, 1),
    ((7, 4), SOLVE_47, 2),
    ((7, 5), SOLVE_47, 3),
    ((7, 6), SOLVE_47, 4),
)


def special_pairs():
    pairs = {(s, t) for s, t, _ in INVERSE_SENDS} | {(s, t) for s, t, _ in BLOCK_SENDS}
    pairs |= {(SOLVE_1, (z, 1)) for z in range(N_Z)}
    pairs |= {((3, 0), SOLVE_23)}
    pairs |= {(SOLVE_23, (r, c)) for c in (2, 3) for r in (4, 5, 7)}
    pairs |= {((7, c), (6, c)) for c in (2, 3)}
    pairs |= {(SOLVE_23, (2, c)) for c in range(8) if c != 1}
    pairs |= {(SOLVE_47, (6, c)) for c in range(8) if c != 4}
    pairs |= {((r, c), SOLVE_47) for c in (1, 3) for r in range(4, 8)}
    pairs |= {(SOLVE_47, (r, 0)) for r in range(4, 8)}
    return sorted({tuple(sorted(p)) for p in pairs})


def kernel(
    lower, slab, inverses, out,
    panel, inv, inv_parts, blocks, right, right_own, x_own, x_stage, x_full, x_in,
    acc_f, acc_b, stage_f, stage_b, relays, pair_out, pair_in, sums, cross_in,
    load_sem, send_sem, x_sem, x_in_sem, relay_sem, inv_sem, block_sem, acc_f_sem, acc_b_sem, pair_sem, cross_sem,
):
    row = lax.axis_index("row")
    col = lax.axis_index("col")
    y, z = row // N_Z, row % N_Z
    x, core = col // 2, col % 2
    half = panel.shape[1] // 2
    quarter = half // 2
    width = x_own.shape[1]

    def here(device):
        return (row == device[0]) & (col == device[1])

    def plane_row(r0, r1):
        return (row >= r0) & (row < r1)

    root_z = col
    sibling = (row, col + 1 - 2 * core)
    pending = []

    def remote(src, dst, s, recv, device):
        return pltpu.make_async_remote_copy(
            src_ref=src, dst_ref=dst, send_sem=send_sem.at[s], recv_sem=recv, device_id=device, device_id_type=MESH
        )

    def send(when, src, dst, s, recv, device):
        remote(src, dst, s, recv, device).start()
        pending.append((when, s, src.shape, src.dtype))

    def arrived(dst, recv):
        remote(dst, dst, 0, recv, sibling).wait_recv()

    load_first = pltpu.make_async_copy(lower.at[0], panel.at[0], load_sem.at[0])
    load_rest = pltpu.make_async_copy(lower.at[pl.ds(1, 7)], panel.at[pl.ds(1, 7)], load_sem.at[1])
    load_inv = pltpu.make_async_copy(inverses, inv, load_sem.at[2])
    load_right = pltpu.make_async_copy(slab.at[0], right, load_sem.at[3])
    load_own = pltpu.make_async_copy(slab.at[col], right_own, load_sem.at[4])
    load_inv.start()
    load_right.start()
    load_first.start()
    load_rest.start()
    load_own.start()

    def clear_slot(slot):
        inv_parts[slot] = jnp.zeros(inv_parts.shape[1:], BF16)

    @pl.when(here(SOLVE_1))
    def _():
        clear_slot(0)

    @pl.when(here(SOLVE_23))
    def _():
        clear_slot(0)
        clear_slot(1)

    @pl.when(here(SOLVE_47))
    def _():
        clear_slot(1)
        clear_slot(2)
        clear_slot(3)

    barrier = pltpu.get_barrier_semaphore()

    def greet(device):
        pl.semaphore_signal(barrier, inc=1, device_id=device, device_id_type=MESH)

    greet(sibling)
    for d in range(1, N_X):
        greet((row, (x + d) % N_X * 2 + core))
    count = jnp.int32(N_X)
    is_root = (z == root_z) & (col < 2)

    @pl.when(is_root)
    def _():
        for d in range(1, N_Z):
            greet((y * N_Z + (z + d) % N_Z, col))

    @pl.when((col < 2) & (z != root_z))
    def _():
        greet((y * N_Z + root_z, col))

    count += jnp.where(is_root, N_Z - 1, jnp.where(col < 2, 1, 0))
    is_relay = (z == 2) | (z == 6)
    relay_z = jnp.where(col < 4, 2, 6)

    @pl.when(is_relay)
    def _():
        for k in range(2, 8):

            @pl.when((core == k % 2) & (z == (2 if k < 4 else 6)))
            def _(k=k):
                for d in range(1, N_Z):
                    greet((y * N_Z + (z + d) % N_Z, k))

                @pl.when(col != k)
                def _():
                    greet((row, k))

    count += jnp.where(z == 2, N_Z - 1 + jnp.where(x == 1, 0, 1), 0)
    count += jnp.where(z == 6, 2 * (N_Z - 1) + jnp.where(x >= 2, 1, 2), 0)

    @pl.when(col >= 2)
    def _():
        for q in range(N_X):

            @pl.when((z != relay_z) | (q != x))
            def _(q=q):
                greet((y * N_Z + relay_z, 2 * q + core))

    count += jnp.where(col >= 2, jnp.where(z == jnp.where(col < 4, 2, 6), N_X - 1, N_X), 0)
    in_line = is_root | is_relay

    @pl.when(in_line & (y == 0))
    def _():
        for d in range(1, N_Y):
            greet((d * N_Z + z, col))

    @pl.when(in_line & (y != 0))
    def _():
        greet((z, col))

    count += jnp.where(in_line, jnp.where(y == 0, N_Y - 1, 1), 0)
    partners = {}
    for a, b in special_pairs():
        partners.setdefault(a, []).append(b)
        partners.setdefault(b, []).append(a)
    for device, others in partners.items():
        count += jnp.where(here(device), len(others), 0)

        @pl.when(here(device))
        def _(others=others):
            for other in others:
                greet(other)

    pl.semaphore_wait(barrier, count)

    def split_inverse(slot):
        value = inv[...]
        high = value.astype(BF16)
        inv_parts[slot, 0] = high
        inv_parts[slot, 1] = (value - high.astype(F32)).astype(BF16)

    for source, solver, slot in BLOCK_SENDS:

        @pl.when(here(source))
        def _(source=source, solver=solver, slot=slot):
            send(source, lower.at[0], blocks.at[slot], 0, block_sem.at[slot], solver)

    def part(slot, piece, b):
        return inv_parts.at[slot, piece, pl.ds(b * quarter, quarter), pl.ds(0, (b + 1) * quarter)]

    is_source = here(INVERSE_SENDS[0][0])
    for source, _, _ in INVERSE_SENDS[1:]:
        is_source |= here(source)

    @pl.when(is_source)
    def _():
        load_inv.wait()
        split_inverse(0)

    for source, solver, slot in INVERSE_SENDS:

        @pl.when(here(source))
        def _(source=source, solver=solver, slot=slot):
            for piece in range(2):
                for b in range(4):
                    s = 1 + piece * 4 + b
                    send(source, part(0, piece, b), part(slot, piece, b), s, inv_sem.at[slot, piece, b], solver)

    def inverse_arrived(slot):
        for piece in range(2):
            for b in range(4):
                arrived(part(slot, piece, b), inv_sem.at[slot, piece, b])

    def solve(slot, total):
        high = total.astype(BF16)
        low = (total - high.astype(F32)).astype(BF16)
        both = jnp.concatenate([high, low], axis=1)

        def times(rows, depth):
            a = inv_parts[slot, 0, rows, :depth]
            b = inv_parts[slot, 1, rows, :depth]
            return jnp.dot(a, both[:depth], preferred_element_type=F32) + jnp.dot(
                b, both[:depth], preferred_element_type=F32
            )

        whole = jnp.concatenate([times(slice(0, half), half), times(slice(half, 2 * half), 2 * half)], axis=0)
        return whole[:, :width] + whole[:, width:]

    def product(block, value):
        return jnp.dot(block, value, preferred_element_type=F32)

    @pl.when(here(SOLVE_0))
    def _():
        load_inv.wait()
        split_inverse(0)
        load_right.wait()
        value = solve(0, right[...])
        x_own[...] = value.astype(BF16)
        x_full[0] = value

    column_root = [SOLVE_0, (1, 1)]
    in_plane = [(1, 2, 3, 4, 5, 6, 7), ()]

    def spread_from_root(c):
        when = column_root[c]
        root_row = column_root[c][0]
        for i, target in enumerate(in_plane[c][:1]):
            send(when, x_own, x_own, 9 + i, x_sem, (target, c))
        for d in (2, 1, 3):
            send(when, x_own, x_own, 15 + d, x_sem, (d * N_Z + root_row, c))
        for i, target in enumerate(in_plane[c]):
            if i > 0:
                send(when, x_own, x_own, 9 + i, x_sem, (target, c))

    @pl.when(here(SOLVE_0))
    def _():
        spread_from_root(0)

    @pl.when(here(SOLVE_1))
    def _():
        load_right.wait()
        load_first.wait()
        inverse_arrived(0)
        arrived(x_own, x_sem)
        value = solve(0, right[...] - product(panel[0], x_own[...]))
        x_stage[0] = value.astype(BF16)
        x_full[0] = value
        for i, target in enumerate((2, 3, 1, 4, 5, 6, 7, 0)):
            send(SOLVE_1, x_stage.at[0], x_own, 9 + i, x_sem, (target, 1))

    def rows_of(c, r0, r1):
        return plane_row(r0, r1) & (col == c)

    @pl.when(rows_of(0, 2, 8))
    def _():
        load_right.wait()
        load_first.wait()
        arrived(x_own, x_sem)
        stage_f[...] = right[...] - product(panel[0], x_own[...])

    @pl.when(here((3, 0)))
    def _():
        send((3, 0), stage_f, acc_f.at[1], 19, acc_f_sem.at[1], SOLVE_23)

    to_sibling = rows_of(0, 2, 8) & (row != 3)

    @pl.when(to_sibling)
    def _():
        send(to_sibling, stage_f, acc_f.at[0], 19, acc_f_sem.at[0], sibling)

    for r in range(4, 8):

        @pl.when(here((r, 1)))
        def _(r=r):
            load_right.wait()
            load_first.wait()
            arrived(x_own, x_sem)
            arrived(acc_f.at[0], acc_f_sem.at[0])
            stage_f[...] = acc_f[0] - product(panel[0], x_own[...])
            send((r, 1), stage_f, acc_f.at[r - 2], 19, acc_f_sem.at[r - 2], SOLVE_47)

    def scatter(when, slot, k, s):
        solver = SOLVE_23 if k < 4 else SOLVE_47
        for q in range(N_X):
            device = (solver[0], 2 * q + k % 2)
            if device != solver:
                rows = pl.ds(q * quarter, quarter)
                send(when, x_stage.at[slot, rows], relays.at[max(k // 2 - 2, 0)], s + q, relay_sem.at[max(k // 2 - 2, 0)], device)

    own_rows = pl.ds(pl.multiple_of(x * quarter, quarter), quarter)
    other_planes = [(d * N_Z + z, col) for d in range(1, N_Y)]
    other_z = [y * N_Z + (z + d) % N_Z for d in (4, 3, 5, 2, 6, 1, 7)]

    def relay_quarter(k):
        solver = SOLVE_23 if k < 4 else SOLVE_47
        slot = max(k // 2 - 2, 0)
        piece = relays.at[slot]
        first = 40 + 12 * slot

        place = lambda: (z == solver[0]) & (core == k % 2)

        @pl.when(place())
        def _():
            @pl.when(here(solver))
            def _():
                q = solver[1] // 2
                relays[slot] = x_stage[k - 2 if k < 4 else k - 4, q * quarter : (q + 1) * quarter]

            @pl.when(jnp.logical_not(here(solver)))
            def _():
                arrived(piece, relay_sem.at[slot])

            @pl.when(y == 0)
            def _():
                for i, device in enumerate(other_planes):
                    send(lambda: place() & (y == 0), piece, piece, first + i, relay_sem.at[slot], device)

            for i, target in enumerate(other_z):
                direct = (lambda target=target: (y != 0) | (target < 4)) if k < 4 else (lambda: True)

                @pl.when(direct())
                def _(i=i, target=target, direct=direct):
                    wanted = lambda: place() & direct()
                    send(wanted, piece, x_own.at[own_rows], first + 3 + i, x_sem, (target, k))

            @pl.when(col == k)
            def _():
                x_own[own_rows] = relays[slot]

            @pl.when(col != k)
            def _():
                send(lambda: place() & (col != k), piece, x_own.at[own_rows], first + 10, x_sem, (row, k))

    @pl.when(here(SOLVE_23))
    def _():
        when = SOLVE_23
        load_right.wait()
        load_first.wait()
        arrived(acc_f.at[0], acc_f_sem.at[0])
        arrived(x_own, x_sem)
        total = acc_f[0] - product(panel[0], x_own[...])
        inverse_arrived(0)
        value = solve(0, total)
        x_stage[0] = value.astype(BF16)
        x_full[0] = value
        for i, r in enumerate((4, 5, 7)):
            send(when, x_stage.at[0], x_own, 20 + i, x_sem, (r, 2))
        scatter(when, 0, 2, 26)
        arrived(blocks.at[0], block_sem.at[0])
        arrived(acc_f.at[1], acc_f_sem.at[1])
        stage_f[...] = acc_f[1] - product(blocks[0], x_own[...])
        arrived(blocks.at[1], block_sem.at[1])
        total = stage_f[...] - product(blocks[1], x_stage[0])
        inverse_arrived(1)
        value = solve(1, total)
        x_stage[1] = value.astype(BF16)
        x_full[1] = value
        for i, r in enumerate((4, 5, 7)):
            send(when, x_stage.at[1], x_own, 23 + i, x_sem, (r, 3))
        scatter(when, 1, 3, 29)
        send(when, x_full.at[0], x_in, 36, x_in_sem, (2, 0))
        send(when, x_full.at[1], x_in, 37, x_in_sem, (3, 0))

    low_rows = rows_of(2, 4, 8)

    def pass_on(c):
        @pl.when(row == 7)
        def _():
            send((7, c), x_own, x_own, 9, x_sem, (6, c))

    @pl.when(low_rows)
    def _():
        load_first.wait()
        arrived(x_own, x_sem)
        pass_on(2)
        stage_f[...] = product(panel[0], x_own[...])
        send(low_rows, stage_f, acc_f.at[0], 19, acc_f_sem.at[0], sibling)

    for r in range(4, 8):

        @pl.when(here((r, 3)))
        def _(r=r):
            load_first.wait()
            arrived(x_own, x_sem)
            if r == 7:
                pass_on(3)
            arrived(acc_f.at[0], acc_f_sem.at[0])
            stage_b[...] = (acc_f[0] + product(panel[0], x_own[...])).astype(BF16)
            send((r, 3), stage_b, acc_b.at[r - 4], 19, acc_b_sem.at[r - 4], SOLVE_47)

    @pl.when(here(SOLVE_47))
    def _():
        when = SOLVE_47
        load_inv.wait()
        split_inverse(0)
        load_first.wait()
        load_right.wait()
        place = {(1, 0): blocks.at[0], (2, 0): panel.at[0], (2, 1): blocks.at[1]}
        place |= {(3, 0): blocks.at[2], (3, 1): blocks.at[3], (3, 2): blocks.at[4]}
        for slot in range(5):
            arrived(blocks.at[slot], block_sem.at[slot])
        for slot in range(1, 4):
            inverse_arrived(slot)
        for q in range(4):
            arrived(acc_f.at[q + 2], acc_f_sem.at[q + 2])
            for j in range(q - 1):
                acc_f[q + 2] -= product(place[q, j][...], x_stage[j])
            total = acc_f[q + 2]
            if q > 0:
                total -= product(place[q, q - 1][...], x_stage[q - 1])
            arrived(acc_b.at[q], acc_b_sem.at[q])
            total -= acc_b[q].astype(F32)
            value = solve(q, total)
            x_stage[q] = value.astype(BF16)
            x_full[q] = value
            scatter(when, q, 4 + q, 20 + 4 * q)
        for q in range(4):
            send(when, x_full.at[q], x_in, 36 + q, x_in_sem, (4 + q, 0))

    for k in range(2, 8):
        relay_quarter(k)

    waited = rows_of(0, 0, 8) | (plane_row(4, 8) & (col < 4)) | here(SOLVE_23)

    @pl.when(jnp.logical_not(waited) & (col < 2))
    def _():
        arrived(x_own, x_sem)

    @pl.when(jnp.logical_not(waited) & (col >= 2))
    def _():
        @pl.when(z != relay_z)
        def _():
            arrived(x_own, x_sem)

        @pl.when(z == relay_z)
        def _():
            arrived(x_own.at[pl.ds(0, 3 * quarter)], x_sem)

    @pl.when(here(column_root[1]))
    def _():
        spread_from_root(1)

    relay = is_root & (y != 0)
    peers = [(i, (y * N_Z + (z + d) % N_Z, col)) for i, d in enumerate((4, 3, 5, 2, 6, 1, 7))]

    @pl.when(relay)
    def _():
        for i, peer in peers:
            send(relay, x_own, x_own, 9 + i, x_sem, peer)

    always = row >= 0
    waited_first = (plane_row(2, 8) & (col < 4)) | here(SOLVE_1) | here(SOLVE_47)
    waited_first = waited_first & jnp.logical_not((col > 1) & (row < 4)) & jnp.logical_not(here((2, 1)))
    waited_first = waited_first & jnp.logical_not(here((3, 1))) | here(SOLVE_23)

    @pl.when(jnp.logical_not(waited_first))
    def _():
        load_first.wait()

    load_rest.wait()
    value = x_own[...]
    for i in range(4):
        pair_out[i] = product(panel[2 * i + 1 - core], value).astype(BF16)
    send(always, pair_out, pair_in, 64, pair_sem, sibling)
    for i in range(4):
        sums[i] = product(panel[2 * i + core], value).astype(BF16)
    arrived(pair_in, pair_sem)
    for i in range(4):
        sums[i] = (sums[i].astype(F32) + pair_in[i].astype(F32)).astype(BF16)
    for d in (2, 1, 3):
        owner = (x + d) % N_X
        send(always, sums.at[owner], cross_in.at[d - 1], 64 + d, cross_sem.at[d - 1], (row, owner * 2 + core))

    load_own.wait()
    total = right_own[...] - sums[x].astype(F32)
    for d in range(3):
        arrived(cross_in.at[d], cross_sem.at[d])
        total -= cross_in[d].astype(F32)
    out[...] = total

    solved = plane_row(0, 8) & (col == 0)

    @pl.when(solved & (row < 2))
    def _():
        out[...] = x_full[0]

    @pl.when(solved & (row >= 2))
    def _():
        arrived(x_in, x_in_sem)
        out[...] = x_in[...]

    @pl.when(jnp.logical_not(is_source | here(SOLVE_0) | here(SOLVE_47)))
    def _():
        load_inv.wait()

    read_right = plane_row(2, 8) & (col == 0) | plane_row(4, 8) & (col == 1)
    read_right = read_right | here(SOLVE_0) | here(SOLVE_1) | here(SOLVE_23) | here(SOLVE_47)

    @pl.when(jnp.logical_not(read_right))
    def _():
        load_right.wait()

    buffers = [x_own, stage_f, pair_out, relays.at[0]]

    def same_size(shape, dtype):
        for buffer in buffers:
            if buffer.shape == shape and buffer.dtype == dtype:
                return buffer
        if shape == panel.shape[1:]:
            return panel.at[0]
        return part(0, 0, shape[1] // quarter - 1)

    for when, s, shape, dtype in pending:

        @pl.when(here(when) if isinstance(when, tuple) else when() if callable(when) else when)
        def _(s=s, shape=shape, dtype=dtype):
            ref = same_size(shape, dtype)
            remote(ref, ref, s, x_sem, sibling).wait_send()


def body(lower, slab, inverses):
    row_blocks, _, order, _, _, _ = lower.shape
    width = slab.shape[3]
    vmem = pltpu.VMEM
    dma = pltpu.SemaphoreType.DMA
    scratch = [
        vmem((row_blocks, order, order), BF16),
        vmem((order, order), F32),
        vmem((4, 2, order, order), BF16),
        vmem((5, order, order), BF16),
        vmem((order, width), F32),
        vmem((order, width), F32),
        vmem((order, width), BF16),
        vmem((4, order, width), BF16),
        vmem((4, order, width), F32),
        vmem((order, width), F32),
        vmem((6, order, width), F32),
        vmem((4, order, width), BF16),
        vmem((order, width), F32),
        vmem((order, width), BF16),
        vmem((2, order // 4, width), BF16),
        vmem((4, order, width), BF16),
        vmem((4, order, width), BF16),
        vmem((4, order, width), BF16),
        vmem((3, order, width), BF16),
        dma((5,)),
        dma((72,)),
        dma,
        dma,
        dma((2,)),
        dma((4, 2, 4)),
        dma((5,)),
        dma((6,)),
        dma((4,)),
        dma,
        dma((3,)),
    ]
    result = pl.pallas_call(
        kernel,
        name="window_solve",
        out_shape=jax.ShapeDtypeStruct((order, width), F32),
        in_specs=[pl.BlockSpec(memory_space=pltpu.HBM)] * 3,
        out_specs=pl.BlockSpec(memory_space=pltpu.VMEM),
        scratch_shapes=scratch,
        compiler_params=pltpu.CompilerParams(
            collective_id=0, has_side_effects=True, vmem_limit_bytes=60 << 20
        ),
    )(
        lower.reshape(row_blocks, order, order),
        slab.reshape(row_blocks, order, width),
        inverses.reshape(order, order),
    )
    return result.reshape(1, 1, order, width)


def solution(mesh):
    in_specs = (
        P(None, "row", None, None, "col", None),
        P(None, "row", None, None),
        P(None, "col", None, None),
    )
    out_specs = P("col", "row", None, None)
    return jax.shard_map(body, mesh=mesh, in_specs=in_specs, out_specs=out_specs, check_vma=False)
```

```python
import jax
import jax.numpy as jnp
from jax import lax
from jax.experimental import pallas as pl
from jax.experimental.pallas import tpu as pltpu
from jax.sharding import PartitionSpec as P

MESH = pl.DeviceIdType.MESH
F32 = jnp.float32
BF16 = jnp.bfloat16

N_Z, N_Y, N_X = 8, 4, 4
SOLVE_0 = (0, 0)
SOLVE_1 = (1, 0)
SOLVE_23 = (2, 1)
SOLVE_47 = (6, 4)
INVERSE_SENDS = (
    ((1, 1), SOLVE_1, 0, (0, 1)),
    ((9, 2), SOLVE_23, 0, (0,)),
    ((25, 2), SOLVE_23, 0, (1,)),
    ((12, 3), SOLVE_23, 1, (0,)),
    ((28, 3), SOLVE_23, 1, (1,)),
    ((6, 5), SOLVE_47, 1, (0, 1)),
    ((14, 6), SOLVE_47, 2, (0, 1)),
    ((30, 7), SOLVE_47, 3, (0, 1)),
)
BLOCK_SENDS = (
    ((3, 1), SOLVE_23, 0),
    ((3, 2), SOLVE_23, 1),
    ((5, 4), SOLVE_47, 0),
    ((6, 5), SOLVE_47, 1),
    ((7, 4), SOLVE_47, 2),
    ((7, 5), SOLVE_47, 3),
    ((7, 6), SOLVE_47, 4),
    *(((5, c), (4, c), 0) for c in (2, 3)),
    *(((6, c), (7, c), 0) for c in (2, 3)),
)

RIGHT_SENDS = (((3, 2), SOLVE_23), ((5, 3), (4, 3)), ((6, 3), (7, 3)))


def special_pairs():
    pairs = {(s, t) for s, t, _, _ in INVERSE_SENDS} | {(s, t) for s, t, _ in BLOCK_SENDS}
    pairs |= {(SOLVE_0, (z, 0)) for z in (1, 2, 3)} | {(SOLVE_1, (z, 1)) for z in (0, 1, 2, 4, 5)}
    pairs |= {((r, 1), (4 if r < 6 else 7, 3)) for r in range(4, 8)}
    pairs |= {((3, 0), (4, 0)), ((0, 1), (5, 0))} | {((0, 1), (r, c)) for r in (6, 7) for c in (0, 1)}
    pairs |= {((3, 0), SOLVE_23)}
    pairs |= {(SOLVE_23, (r, c)) for c in (2, 3) for r in (4, 7)}
    pairs |= {(SOLVE_23, (2, c)) for c in range(8) if c != 1}
    pairs |= {(SOLVE_47, (6, c)) for c in range(8) if c != 4}
    pairs |= {((r, 3), SOLVE_47) for r in (4, 7)} | {((r, 0), (r, 3)) for r in (4, 7)} | {((r, 1), (r, 3)) for r in (4, 7)}
    pairs |= {(SOLVE_47, (r, 0)) for r in range(4, 8)}
    return sorted({tuple(sorted(p)) for p in pairs})


def kernel(
    lower, slab, inverses, out,
    panel, inv, inv_parts, blocks, right, right_own, x_own, x_stage, x_full, x_in,
    acc_f, acc_b, stage_f, stage_b, relays, pair_out, pair_in, sums, cross_in,
    load_sem, send_sem, x_sem, x_in_sem, side_sem, go_sem, relay_sem, inv_sem, block_sem, acc_f_sem, acc_b_sem, pair_sem, cross_sem,
):
    row = lax.axis_index("row")
    col = lax.axis_index("col")
    y, z = row // N_Z, row % N_Z
    x, core = col // 2, col % 2
    half = panel.shape[1] // 2
    quarter = half // 2
    width = x_own.shape[1]

    def here(device):
        return (row == device[0]) & (col == device[1])

    def plane_row(r0, r1):
        return (row >= r0) & (row < r1)

    root_z = col
    sibling = (row, col + 1 - 2 * core)
    pending = []

    def remote(src, dst, s, recv, device):
        return pltpu.make_async_remote_copy(
            src_ref=src, dst_ref=dst, send_sem=send_sem.at[s], recv_sem=recv, device_id=device, device_id_type=MESH
        )

    def send(when, src, dst, s, recv, device):
        remote(src, dst, s, recv, device).start()
        pending.append((when, s, src.shape, src.dtype))

    def arrived(dst, recv):
        remote(dst, dst, 0, recv, sibling).wait_recv()

    load_first = pltpu.make_async_copy(lower.at[0], panel.at[0], load_sem.at[0])
    load_rest = pltpu.make_async_copy(lower.at[pl.ds(1, 7)], panel.at[pl.ds(1, 7)], load_sem.at[1])
    load_inv = pltpu.make_async_copy(inverses, inv, load_sem.at[2])
    load_right = pltpu.make_async_copy(slab.at[0], right, load_sem.at[3])
    load_own = pltpu.make_async_copy(slab.at[col], right_own, load_sem.at[4])
    load_inv.start()
    load_right.start()
    load_first.start()
    load_rest.start()
    load_own.start()

    def clear_slot(slot):
        inv_parts[slot] = jnp.zeros(inv_parts.shape[1:], BF16)

    @pl.when(here(SOLVE_1))
    def _():
        clear_slot(0)

    @pl.when(here(SOLVE_23))
    def _():
        clear_slot(0)
        clear_slot(1)

    @pl.when(here(SOLVE_47))
    def _():
        clear_slot(1)
        clear_slot(2)
        clear_slot(3)

    barrier = pltpu.get_barrier_semaphore()

    def greet(device):
        pl.semaphore_signal(barrier, inc=1, device_id=device, device_id_type=MESH)

    greet(sibling)
    for d in range(1, N_X):
        greet((row, (x + d) % N_X * 2 + core))
    count = jnp.int32(N_X)
    is_root = (z == root_z) & (col < 2)
    in_other = (col < 2) & (y != 0)

    @pl.when(is_root & in_other)
    def _():
        for d in range(1, N_Z):
            greet((y * N_Z + (z + d) % N_Z, col))

    @pl.when(jnp.logical_not(is_root) & in_other)
    def _():
        greet((y * N_Z + root_z, col))

    count += jnp.where(in_other, jnp.where(is_root, N_Z - 1, 1), 0)
    is_relay = (z == 2) | (z == 6)
    relay_z = jnp.where(col < 4, 2, 6)

    @pl.when(is_relay)
    def _():
        for k in range(2, 8):

            @pl.when((core == k % 2) & (z == (2 if k < 4 else 6)))
            def _(k=k):
                for d in range(1, N_Z):
                    greet((y * N_Z + (z + d) % N_Z, k))

                @pl.when(col != k)
                def _():
                    greet((row, k))

    count += jnp.where(z == 2, N_Z - 1 + jnp.where(x == 1, 0, 1), 0)
    count += jnp.where(z == 6, 2 * (N_Z - 1) + jnp.where(x >= 2, 1, 2), 0)

    @pl.when(col >= 2)
    def _():
        for q in range(N_X):

            @pl.when((z != relay_z) | (q != x))
            def _(q=q):
                greet((y * N_Z + relay_z, 2 * q + core))

    count += jnp.where(col >= 2, jnp.where(z == jnp.where(col < 4, 2, 6), N_X - 1, N_X), 0)
    in_line = is_root | is_relay

    @pl.when(in_line & (y == 0))
    def _():
        for d in range(1, N_Y):
            greet((d * N_Z + z, col))

    @pl.when(in_line & (y != 0))
    def _():
        greet((z, col))

    count += jnp.where(in_line, jnp.where(y == 0, N_Y - 1, 1), 0)
    partners = {}
    for a, b in special_pairs():
        partners.setdefault(a, []).append(b)
        partners.setdefault(b, []).append(a)
    for device, others in partners.items():
        count += jnp.where(here(device), len(others), 0)

        @pl.when(here(device))
        def _(others=others):
            for other in others:
                greet(other)

    pl.semaphore_wait(barrier, count)

    def split_inverse(slot):
        value = inv[...]
        high = value.astype(BF16)
        inv_parts[slot, 0] = high
        inv_parts[slot, 1] = (value - high.astype(F32)).astype(BF16)

    for source, solver, slot in BLOCK_SENDS:

        @pl.when(here(source))
        def _(source=source, solver=solver, slot=slot):
            send(source, lower.at[0], blocks.at[slot], 0, block_sem.at[slot], solver)

    for source, target in RIGHT_SENDS:

        @pl.when(here(source))
        def _(source=source, target=target):
            send(source, slab.at[0], acc_f.at[2], 1, acc_f_sem.at[2], target)

    def part(slot, piece, b):
        return inv_parts.at[slot, piece, pl.ds(b * quarter, quarter), pl.ds(0, (b + 1) * quarter)]

    is_source = here(INVERSE_SENDS[0][0])
    for source, _, _, _ in INVERSE_SENDS[1:]:
        is_source |= here(source)

    @pl.when(is_source)
    def _():
        load_inv.wait()
        split_inverse(0)

    for source, solver, slot, pieces in INVERSE_SENDS:

        @pl.when(here(source))
        def _(source=source, solver=solver, slot=slot, pieces=pieces):
            for piece in pieces:
                for b in range(4):
                    s = 1 + piece * 4 + b
                    send(source, part(0, piece, b), part(slot, piece, b), s, inv_sem.at[slot, piece, b], solver)

    def inverse_arrived(slot):
        for piece in range(2):
            for b in range(4):
                arrived(part(slot, piece, b), inv_sem.at[slot, piece, b])

    def solve(slot, total):
        high = total.astype(BF16)
        low = (total - high.astype(F32)).astype(BF16)
        both = jnp.concatenate([high, low], axis=1)

        def times(rows, depth):
            a = inv_parts[slot, 0, rows, :depth]
            b = inv_parts[slot, 1, rows, :depth]
            return jnp.dot(a, both[:depth], preferred_element_type=F32) + jnp.dot(
                b, both[:depth], preferred_element_type=F32
            )

        whole = jnp.concatenate([times(slice(0, half), half), times(slice(half, 2 * half), 2 * half)], axis=0)
        return whole[:, :width] + whole[:, width:]

    def product(block, value):
        return jnp.dot(block, value, preferred_element_type=F32)

    @pl.when(here(SOLVE_0))
    def _():
        load_inv.wait()
        split_inverse(0)
        load_right.wait()
        value = solve(0, right[...])
        x_own[...] = value.astype(BF16)
        x_full[0] = value

    column_root = [SOLVE_0, (1, 1)]
    in_plane = [(1, 3, 2), ()]

    def spread_from_root(c):
        when = column_root[c]
        root_row = column_root[c][0]
        for i, target in enumerate(in_plane[c][:1]):
            send(when, x_own, x_own, 9 + i, x_sem, (target, c))
        if c == 0:
            send(when, x_own, x_stage.at[0], 19, side_sem, (0, 1))
        for d in (2, 1, 3):
            send(when, x_own, x_own, 15 + d, x_sem, (d * N_Z + root_row, c))
        for i, target in enumerate(in_plane[c]):
            if i > 0:
                send(when, x_own, x_own, 9 + i, x_sem, (target, c))

    @pl.when(here(SOLVE_0))
    def _():
        spread_from_root(0)

    @pl.when(here(SOLVE_1))
    def _():
        load_right.wait()
        load_first.wait()
        inverse_arrived(0)
        arrived(x_own, x_sem)
        value = solve(0, right[...] - product(panel[0], x_own[...]))
        x_stage[0] = value.astype(BF16)
        x_full[0] = value
        send(SOLVE_1, x_stage.at[0], x_own, 9, x_sem, (2, 1))
        send(SOLVE_1, x_stage.at[0], x_own, 10, x_sem, (4, 1))
        for i, target in enumerate((5, 0, 1)):
            send(SOLVE_1, x_stage.at[0], x_own, 11 + i, x_sem, (target, 1))

    def rows_of(c, r0, r1):
        return plane_row(r0, r1) & (col == c)

    @pl.when(here((2, 0)))
    def _():
        load_first.wait()
        arrived(x_own, x_sem)
        stage_f[0] = product(panel[0], x_own[...])
        send((2, 0), stage_f.at[0], acc_f.at[0], 19, acc_f_sem.at[0], sibling)

    @pl.when(here((3, 0)))
    def _():
        load_first.wait()
        arrived(x_own, x_sem)
        stage_b[0] = product(panel[0], x_own[...]).astype(BF16)
        send((3, 0), stage_b.at[0], acc_b.at[0], 19, acc_b_sem.at[0], SOLVE_23)
        send((3, 0), x_own, x_own, 9, x_sem, (4, 0))

    @pl.when(here((0, 1)))
    def _():
        arrived(x_stage.at[0], side_sem)
        for i, r in enumerate((5, 6, 7)):
            send((0, 1), x_stage.at[0], x_own, 9 + i, x_sem, (r, 0))
        arrived(x_own, x_sem)
        for i, r in enumerate((6, 7)):
            send((0, 1), x_own, x_own, 12 + i, x_sem, (r, 1))

    low_0 = rows_of(0, 4, 8)
    low_1 = rows_of(1, 4, 8)

    @pl.when(low_0)
    def _():
        load_first.wait()
        arrived(x_own, x_sem)
        stage_f[0] = product(panel[0], x_own[...])
        send(low_0, stage_f.at[0], acc_f.at[0], 18, acc_f_sem.at[0], sibling)

    @pl.when(low_1)
    def _():
        load_first.wait()
        arrived(x_own, x_sem)
        arrived(acc_f.at[0], acc_f_sem.at[0])
        stage_b[0] = (acc_f[0] + product(panel[0], x_own[...])).astype(BF16)

    for r, target, slot in ((4, 4, 0), (5, 4, 1), (6, 7, 1), (7, 7, 0)):

        @pl.when(here((r, 1)))
        def _(r=r, target=target, slot=slot):
            send((r, 1), stage_b.at[0], acc_b.at[slot], 19, acc_b_sem.at[slot], (target, 3))

    def scatter(when, slot, k, s):
        solver = SOLVE_23 if k < 4 else SOLVE_47
        for q in range(N_X):
            device = (solver[0], 2 * q + k % 2)
            if device != solver:
                rows = pl.ds(q * quarter, quarter)
                send(when, x_stage.at[slot, rows], relays.at[max(k // 2 - 2, 0)], s + q, relay_sem.at[max(k // 2 - 2, 0)], device)

    own_rows = pl.ds(pl.multiple_of(x * quarter, quarter), quarter)
    other_planes = [(d * N_Z + z, col) for d in range(1, N_Y)]
    other_z = [y * N_Z + (z + d) % N_Z for d in (4, 3, 5, 2, 6, 1, 7)]

    def relay_quarter(k):
        solver = SOLVE_23 if k < 4 else SOLVE_47
        slot = max(k // 2 - 2, 0)
        piece = relays.at[slot]
        first = 40 + 12 * slot

        place = lambda: (z == solver[0]) & (core == k % 2)

        @pl.when(place())
        def _():
            @pl.when(here(solver))
            def _():
                q = solver[1] // 2
                relays[slot] = x_stage[k - 2 if k < 4 else k - 4, q * quarter : (q + 1) * quarter]

            @pl.when(jnp.logical_not(here(solver)))
            def _():
                arrived(piece, relay_sem.at[slot])

            @pl.when(y == 0)
            def _():
                for i, device in enumerate(other_planes):
                    send(lambda: place() & (y == 0), piece, piece, first + i, relay_sem.at[slot], device)

            for i, target in enumerate(other_z):
                direct = (lambda target=target: (y != 0) | ((target != 4) & (target != 7))) if k < 4 else (lambda: True)

                @pl.when(direct())
                def _(i=i, target=target, direct=direct):
                    wanted = lambda: place() & direct()
                    send(wanted, piece, x_own.at[own_rows], first + 3 + i, x_sem, (target, k))

            @pl.when(col == k)
            def _():
                x_own[own_rows] = relays[slot]

            @pl.when(col != k)
            def _():
                send(lambda: place() & (col != k), piece, x_own.at[own_rows], first + 10, x_sem, (row, k))

    @pl.when(here(SOLVE_23))
    def _():
        when = SOLVE_23
        load_right.wait()
        load_first.wait()
        arrived(acc_f.at[0], acc_f_sem.at[0])
        arrived(x_own, x_sem)
        total = right[...] - acc_f[0] - product(panel[0], x_own[...])
        inverse_arrived(0)
        value = solve(0, total)
        x_stage[0] = value.astype(BF16)
        x_full[0] = value
        for i, r in enumerate((4, 7)):
            send(when, x_stage.at[0], x_own, 20 + i, x_sem, (r, 2))
        scatter(when, 0, 2, 26)
        arrived(blocks.at[0], block_sem.at[0])
        arrived(acc_f.at[2], acc_f_sem.at[2])
        arrived(acc_b.at[0], acc_b_sem.at[0])
        stage_f[0] = acc_f[2] - acc_b[0].astype(F32) - product(blocks[0], x_own[...])
        arrived(blocks.at[1], block_sem.at[1])
        total = stage_f[0] - product(blocks[1], x_stage[0])
        inverse_arrived(1)
        value = solve(1, total)
        x_stage[1] = value.astype(BF16)
        x_full[1] = value
        for i, r in enumerate((4, 7)):
            send(when, x_stage.at[1], x_own, 23 + i, x_sem, (r, 3))
        scatter(when, 1, 3, 29)
        send(when, x_own, x_own, 33, x_sem, (3, 1))

    low_rows = (row == 4) | (row == 7)
    low_2 = low_rows & (col == 2)

    @pl.when(low_2)
    def _():
        load_first.wait()
        arrived(x_own, x_sem)
        stage_f[0] = product(panel[0], x_own[...])
        send(low_2, stage_f.at[0], acc_f.at[0], 18, acc_f_sem.at[0], sibling)
        arrived(blocks.at[0], block_sem.at[0])
        stage_f[1] = product(blocks[0], x_own[...])
        send(low_2, stage_f.at[1], acc_f.at[1], 19, acc_f_sem.at[1], sibling)

    for r, rows in ((4, (4, 5)), (7, (6, 7))):

        @pl.when(here((r, 3)))
        def _(r=r, rows=rows):
            load_first.wait()
            load_right.wait()
            for i, target in enumerate(rows):
                j = 0 if target == r else 1
                if j == 1:
                    arrived(acc_f.at[2], acc_f_sem.at[2])
                    arrived(blocks.at[0], block_sem.at[0])
                arrived(acc_b.at[j], acc_b_sem.at[j])
                arrived(acc_f.at[j], acc_f_sem.at[j])
                start = acc_f[2] if j == 1 else right[...]
                stage_f[j] = start - acc_b[j].astype(F32) - acc_f[j]
                if i == 0:
                    arrived(x_own, x_sem)
                    for c in (0, 1):
                        pl.semaphore_signal(go_sem, inc=1, device_id=(r, c), device_id_type=MESH)
                block = panel[0] if target == r else blocks[0]
                stage_b[i] = (stage_f[j] - product(block, x_own[...])).astype(BF16)
                send((r, 3), stage_b.at[i], acc_b.at[target - 4], 18 + i, acc_b_sem.at[target - 4], SOLVE_47)

    @pl.when(here(SOLVE_47))
    def _():
        when = SOLVE_47
        load_inv.wait()
        split_inverse(0)
        load_first.wait()
        load_right.wait()
        place = {(1, 0): blocks.at[0], (2, 0): panel.at[0], (2, 1): blocks.at[1]}
        place |= {(3, 0): blocks.at[2], (3, 1): blocks.at[3], (3, 2): blocks.at[4]}
        for slot in range(5):
            arrived(blocks.at[slot], block_sem.at[slot])
        for slot in range(1, 4):
            inverse_arrived(slot)
        for q in range(4):
            for j in range(q - 1):
                done = product(place[q, j][...], x_stage[j])
                acc_f[q] = done if j == 0 else acc_f[q] + done
            arrived(acc_b.at[q], acc_b_sem.at[q])
            total = acc_b[q].astype(F32)
            if q > 1:
                total -= acc_f[q]
            if q > 0:
                total -= product(place[q, q - 1][...], x_stage[q - 1])
            value = solve(q, total)
            x_stage[q] = value.astype(BF16)
            x_full[q] = value
            scatter(when, q, 4 + q, 20 + 4 * q)
            if q < 2:
                send(when, x_full.at[q], x_in, 36 + q, x_in_sem, (4 + q, 0))
        send(when, x_full.at[2], x_in, 38, x_in_sem, (6, 0))
    for k in range(2, 8):
        relay_quarter(k)

    waited = rows_of(0, 0, 8) | here((0, 1)) | low_1 | (low_rows & (col < 4)) | here(SOLVE_23)

    @pl.when(jnp.logical_not(waited) & (col < 2))
    def _():
        arrived(x_own, x_sem)

    @pl.when(jnp.logical_not(waited) & (col >= 2))
    def _():
        @pl.when(z != relay_z)
        def _():
            arrived(x_own, x_sem)

        @pl.when(z == relay_z)
        def _():
            arrived(x_own.at[pl.ds(0, 3 * quarter)], x_sem)

    @pl.when(here(column_root[1]))
    def _():
        spread_from_root(1)

    relay = is_root & (y != 0)
    peers = [(i, (y * N_Z + (z + d) % N_Z, col)) for i, d in enumerate((4, 3, 5, 2, 6, 1, 7))]

    @pl.when(relay)
    def _():
        for i, peer in peers:
            send(relay, x_own, x_own, 9 + i, x_sem, peer)

    always = row >= 0
    waited_first = rows_of(0, 2, 8) | low_1 | (low_rows & (col < 4))
    waited_first = waited_first | here(SOLVE_1) | here(SOLVE_23) | here(SOLVE_47)

    @pl.when(jnp.logical_not(waited_first))
    def _():
        load_first.wait()

    load_rest.wait()
    value = x_own[...]
    distances = (2, 1, 3, 0)
    owners = [(x + d) % N_X for d in distances]
    for j, owner in enumerate(owners):
        pair_out[j] = product(panel[2 * owner + 1 - core], value).astype(BF16)
        send(always, pair_out.at[j], pair_in.at[j], 64 + j, pair_sem.at[j], sibling)

    @pl.when(low_rows & (col < 2))
    def _():
        pl.semaphore_wait(go_sem, 1)

    for j, (d, owner) in enumerate(zip(distances, owners)):
        total = product(panel[2 * owner + core], value)
        arrived(pair_in.at[j], pair_sem.at[j])
        total = total + pair_in[j].astype(F32)
        if d > 0:
            sums[j] = total.astype(BF16)
            send(always, sums.at[j], cross_in.at[d - 1], 68 + j, cross_sem.at[d - 1], (row, owner * 2 + core))
    @pl.when(here(SOLVE_23))
    def _():
        for q in range(2):
            send(SOLVE_23, x_full.at[q], x_in, 36 + q, x_in_sem, (2 + q, 0))

    @pl.when(here(SOLVE_47))
    def _():
        send(SOLVE_47, x_full.at[3], x_in, 39, x_in_sem, (7, 0))

    load_own.wait()
    total = right_own[...] - total
    for d in range(3):
        arrived(cross_in.at[d], cross_sem.at[d])
        total -= cross_in[d].astype(F32)
    out[...] = total

    solved = plane_row(0, 8) & (col == 0)

    @pl.when(solved & (row < 2))
    def _():
        out[...] = x_full[0]

    @pl.when(solved & (row >= 2))
    def _():
        arrived(x_in, x_in_sem)
        out[...] = x_in[...]

    @pl.when(jnp.logical_not(is_source | here(SOLVE_0) | here(SOLVE_47)))
    def _():
        load_inv.wait()

    read_right = here(SOLVE_0) | here(SOLVE_1) | here(SOLVE_23) | here(SOLVE_47) | (low_rows & (col == 3))

    @pl.when(jnp.logical_not(read_right))
    def _():
        load_right.wait()

    buffers = [x_own, stage_f.at[0], relays.at[0]]

    def same_size(shape, dtype):
        for buffer in buffers:
            if buffer.shape == shape and buffer.dtype == dtype:
                return buffer
        if shape == panel.shape[1:]:
            return panel.at[0]
        return part(0, 0, shape[1] // quarter - 1)

    for when, s, shape, dtype in pending:

        @pl.when(here(when) if isinstance(when, tuple) else when() if callable(when) else when)
        def _(s=s, shape=shape, dtype=dtype):
            ref = same_size(shape, dtype)
            remote(ref, ref, s, x_sem, sibling).wait_send()


def body(lower, slab, inverses):
    row_blocks, _, order, _, _, _ = lower.shape
    width = slab.shape[3]
    vmem = pltpu.VMEM
    dma = pltpu.SemaphoreType.DMA
    scratch = [
        vmem((row_blocks, order, order), BF16),
        vmem((order, order), F32),
        vmem((4, 2, order, order), BF16),
        vmem((5, order, order), BF16),
        vmem((order, width), F32),
        vmem((order, width), F32),
        vmem((order, width), BF16),
        vmem((4, order, width), BF16),
        vmem((4, order, width), F32),
        vmem((order, width), F32),
        vmem((4, order, width), F32),
        vmem((4, order, width), BF16),
        vmem((2, order, width), F32),
        vmem((2, order, width), BF16),
        vmem((2, order // 4, width), BF16),
        vmem((4, order, width), BF16),
        vmem((4, order, width), BF16),
        vmem((3, order, width), BF16),
        vmem((3, order, width), BF16),
        dma((5,)),
        dma((72,)),
        dma,
        dma,
        dma,
        pltpu.SemaphoreType.REGULAR,
        dma((2,)),
        dma((4, 2, 4)),
        dma((5,)),
        dma((4,)),
        dma((4,)),
        dma((4,)),
        dma((3,)),
    ]
    result = pl.pallas_call(
        kernel,
        name="window_solve",
        out_shape=jax.ShapeDtypeStruct((order, width), F32),
        in_specs=[pl.BlockSpec(memory_space=pltpu.HBM)] * 3,
        out_specs=pl.BlockSpec(memory_space=pltpu.VMEM),
        scratch_shapes=scratch,
        compiler_params=pltpu.CompilerParams(
            collective_id=0, has_side_effects=True, vmem_limit_bytes=53 << 20
        ),
    )(
        lower.reshape(row_blocks, order, order),
        slab.reshape(row_blocks, order, width),
        inverses.reshape(order, order),
    )
    return result.reshape(1, 1, order, width)


def solution(mesh):
    in_specs = (
        P(None, "row", None, None, "col", None),
        P(None, "row", None, None),
        P(None, "col", None, None),
    )
    out_specs = P("col", "row", None, None)
    return jax.shard_map(body, mesh=mesh, in_specs=in_specs, out_specs=out_specs, check_vma=False)
```

```python
import jax
import jax.numpy as jnp
from jax import lax
from jax.experimental import pallas as pl
from jax.experimental.pallas import tpu as pltpu
from jax.sharding import PartitionSpec as P

MESH = pl.DeviceIdType.MESH
F32 = jnp.float32
BF16 = jnp.bfloat16

N_Z, N_Y, N_X = 8, 4, 4
SOLVE_0 = (0, 0)
SOLVE_1 = (1, 0)
SOLVE_23 = (2, 1)
SOLVE_47 = (6, 4)
HIGH = tuple((0, b) for b in range(4))
LOW = tuple((1, b) for b in range(4))
INVERSE_SENDS = (
    ((1, 1), SOLVE_1, 0, HIGH + LOW),
    ((9, 2), SOLVE_23, 0, (HIGH[0], HIGH[3])),
    ((25, 2), SOLVE_23, 0, (HIGH[1], HIGH[2])),
    ((12, 3), SOLVE_23, 1, (HIGH[0], HIGH[3])),
    ((28, 3), SOLVE_23, 1, (HIGH[1], HIGH[2])),
    ((6, 5), SOLVE_47, 1, HIGH),
    ((14, 6), SOLVE_47, 2, HIGH),
    ((30, 7), SOLVE_47, 3, HIGH),
)
BLOCK_SENDS = (
    ((3, 1), SOLVE_23, 0),
    ((3, 2), SOLVE_23, 1),
    ((5, 4), SOLVE_47, 0),
    ((6, 5), SOLVE_47, 1),
    ((7, 4), SOLVE_47, 2),
    ((7, 5), SOLVE_47, 3),
    ((7, 6), SOLVE_47, 4),
    *(((5, c), (4, c), 0) for c in (2, 3)),
    *(((6, c), (7, c), 0) for c in (2, 3)),
)


def special_pairs():
    pairs = {(s, t) for s, t, _, _ in INVERSE_SENDS} | {(s, t) for s, t, _ in BLOCK_SENDS}
    pairs |= {(SOLVE_0, (z, 0)) for z in (1, 2, 3)} | {(SOLVE_1, (z, 1)) for z in (0, 1, 2, 4, 5)}
    pairs |= {((r, 1), (4 if r < 6 else 7, 3)) for r in range(4, 8)}
    pairs |= {((3, 0), (4, 0)), ((0, 1), (5, 0))} | {((0, 1), (r, c)) for r in (6, 7) for c in (0, 1)}
    pairs |= {((3, 0), SOLVE_23)}
    pairs |= {(SOLVE_23, (r, c)) for c in (2, 3) for r in (4, 7)}
    pairs |= {(SOLVE_23, (2, c)) for c in range(8) if c != 1}
    pairs |= {(SOLVE_47, (6, c)) for c in range(8) if c != 4}
    pairs |= {((4, 3), (7, 3))} | {((r, 3), SOLVE_47) for r in (4, 7)} | {((r, 0), (r, 3)) for r in (4, 7)} | {((r, 1), (r, 3)) for r in (4, 7)}
    pairs |= {(SOLVE_47, (r, 0)) for r in range(4, 8)}
    return sorted({tuple(sorted(p)) for p in pairs})


def kernel(
    lower, slab, inverses, out,
    panel, inv, inv_parts, blocks, right, right_own, x_own, x_stage, x_full, x_in,
    acc_f, acc_b, stage_f, stage_b, relays, pair_out, pair_in, sums, cross_in,
    load_sem, send_sem, x_sem, x_in_sem, side_sem, go_sem, relay_sem, inv_sem, block_sem, acc_f_sem, acc_b_sem, pair_sem, cross_sem,
):
    row = lax.axis_index("row")
    col = lax.axis_index("col")
    y, z = row // N_Z, row % N_Z
    x, core = col // 2, col % 2
    half = panel.shape[1] // 2
    quarter = half // 2
    width = x_own.shape[1]

    def here(device):
        return (row == device[0]) & (col == device[1])

    def plane_row(r0, r1):
        return (row >= r0) & (row < r1)

    root_z = col
    sibling = (row, col + 1 - 2 * core)
    pending = []

    def remote(src, dst, s, recv, device):
        return pltpu.make_async_remote_copy(
            src_ref=src, dst_ref=dst, send_sem=send_sem.at[s], recv_sem=recv, device_id=device, device_id_type=MESH
        )

    def send(when, src, dst, s, recv, device):
        remote(src, dst, s, recv, device).start()
        pending.append((when, s, src.shape, src.dtype))

    def arrived(dst, recv):
        remote(dst, dst, 0, recv, sibling).wait_recv()

    load_first = pltpu.make_async_copy(lower.at[0], panel.at[0], load_sem.at[0])
    load_rest = pltpu.make_async_copy(lower.at[pl.ds(1, 7)], panel.at[pl.ds(1, 7)], load_sem.at[1])
    load_inv = pltpu.make_async_copy(inverses, inv, load_sem.at[2])
    load_right = pltpu.make_async_copy(slab.at[0], right, load_sem.at[3])
    load_own = pltpu.make_async_copy(slab.at[col], right_own, load_sem.at[4])
    load_inv.start()
    load_right.start()
    load_first.start()

    def clear_slot(slot):
        inv_parts[slot] = jnp.zeros(inv_parts.shape[1:], BF16)

    @pl.when(here(SOLVE_1))
    def _():
        clear_slot(0)

    @pl.when(here(SOLVE_23))
    def _():
        clear_slot(0)
        clear_slot(1)

    @pl.when(here(SOLVE_47))
    def _():
        clear_slot(1)
        clear_slot(2)
        clear_slot(3)

    barrier = pltpu.get_barrier_semaphore()

    def greet(device):
        pl.semaphore_signal(barrier, inc=1, device_id=device, device_id_type=MESH)

    greet(sibling)
    for d in range(1, N_X):
        greet((row, (x + d) % N_X * 2 + core))
    count = jnp.int32(N_X)
    is_root = (z == root_z) & (col < 2)
    in_other = (col < 2) & (y != 0)

    @pl.when(is_root & in_other)
    def _():
        for d in range(1, N_Z):
            greet((y * N_Z + (z + d) % N_Z, col))

    @pl.when(jnp.logical_not(is_root) & in_other)
    def _():
        greet((y * N_Z + root_z, col))

    count += jnp.where(in_other, jnp.where(is_root, N_Z - 1, 1), 0)
    is_relay = (z == 2) | (z == 6)
    relay_z = jnp.where(col < 4, 2, 6)

    @pl.when(is_relay)
    def _():
        for k in range(2, 8):

            @pl.when((core == k % 2) & (z == (2 if k < 4 else 6)))
            def _(k=k):
                for d in range(1, N_Z):
                    greet((y * N_Z + (z + d) % N_Z, k))

                @pl.when(col != k)
                def _():
                    greet((row, k))

    count += jnp.where(z == 2, N_Z - 1 + jnp.where(x == 1, 0, 1), 0)
    count += jnp.where(z == 6, 2 * (N_Z - 1) + jnp.where(x >= 2, 1, 2), 0)

    @pl.when(col >= 2)
    def _():
        for q in range(N_X):

            @pl.when((z != relay_z) | (q != x))
            def _(q=q):
                greet((y * N_Z + relay_z, 2 * q + core))

    count += jnp.where(col >= 2, jnp.where(z == jnp.where(col < 4, 2, 6), N_X - 1, N_X), 0)
    in_line = is_root | is_relay

    @pl.when(in_line & (y == 0))
    def _():
        for d in range(1, N_Y):
            greet((d * N_Z + z, col))

    @pl.when(in_line & (y != 0))
    def _():
        greet((z, col))

    count += jnp.where(in_line, jnp.where(y == 0, N_Y - 1, 1), 0)
    partners = {}
    for a, b in special_pairs():
        partners.setdefault(a, []).append(b)
        partners.setdefault(b, []).append(a)
    for device, others in partners.items():
        count += jnp.where(here(device), len(others), 0)

        @pl.when(here(device))
        def _(others=others):
            for other in others:
                greet(other)

    def split_inverse(slot):
        value = inv[...]
        high = value.astype(BF16)
        inv_parts[slot, 0] = high
        inv_parts[slot, 1] = (value - high.astype(F32)).astype(BF16)

    def part(slot, piece, b):
        return inv_parts.at[slot, piece, pl.ds(b * quarter, quarter), pl.ds(0, (b + 1) * quarter)]

    def inverse_arrived(slot, parts=HIGH):
        for piece, b in parts:
            arrived(part(slot, piece, b), inv_sem.at[slot, piece, b])

    def solve(slot, total, low_part=False):
        high = total.astype(BF16)
        low = (total - high.astype(F32)).astype(BF16)
        both = jnp.concatenate([high, low], axis=1)

        def times(rows, depth):
            done = jnp.dot(inv_parts[slot, 0, rows, :depth], both[:depth], preferred_element_type=F32)
            if low_part:
                done += jnp.dot(inv_parts[slot, 1, rows, :depth], both[:depth], preferred_element_type=F32)
            return done

        whole = jnp.concatenate([times(slice(0, half), half), times(slice(half, 2 * half), 2 * half)], axis=0)
        return whole[:, :width] + whole[:, width:]

    def product(block, value):
        return jnp.dot(block, value, preferred_element_type=F32)

    is_source = here(INVERSE_SENDS[0][0])
    for source, _, _, _ in INVERSE_SENDS[1:]:
        is_source |= here(source)

    @pl.when(is_source)
    def _():
        load_inv.wait()
        split_inverse(0)

    @pl.when(here(SOLVE_0))
    def _():
        load_inv.wait()
        split_inverse(0)
        load_right.wait()
        value = solve(0, right[...], low_part=True)
        x_own[...] = value.astype(BF16)
        x_full[0] = value

    pl.semaphore_wait(barrier, count)

    load_rest.start()
    load_own.start()

    for source, solver, slot in BLOCK_SENDS:

        @pl.when(here(source))
        def _(source=source, solver=solver, slot=slot):
            send(source, lower.at[0], blocks.at[slot], 0, block_sem.at[slot], solver)

    for source, solver, slot, pieces in INVERSE_SENDS:

        @pl.when(here(source))
        def _(source=source, solver=solver, slot=slot, pieces=pieces):
            for piece, b in pieces:
                s = 1 + piece * 4 + b
                send(source, part(0, piece, b), part(slot, piece, b), s, inv_sem.at[slot, piece, b], solver)

    column_root = [SOLVE_0, (1, 1)]
    in_plane = [(1, 3, 2), ()]

    def spread_from_root(c):
        when = column_root[c]
        root_row = column_root[c][0]
        for i, target in enumerate(in_plane[c][:1]):
            send(when, x_own, x_own, 9 + i, x_sem, (target, c))
        if c == 0:
            send(when, x_own, x_stage.at[0], 19, side_sem, (0, 1))
        for d in (2, 1, 3):
            send(when, x_own, x_own, 15 + d, x_sem, (d * N_Z + root_row, c))
        for i, target in enumerate(in_plane[c]):
            if i > 0:
                send(when, x_own, x_own, 9 + i, x_sem, (target, c))

    @pl.when(here(SOLVE_0))
    def _():
        spread_from_root(0)

    @pl.when(here(SOLVE_1))
    def _():
        load_right.wait()
        load_first.wait()
        inverse_arrived(0, HIGH + LOW)
        arrived(x_own, x_sem)
        value = solve(0, right[...] - product(panel[0], x_own[...]), low_part=True)
        x_stage[0] = value.astype(BF16)
        x_full[0] = value
        send(SOLVE_1, x_stage.at[0], x_own, 9, x_sem, (2, 1))
        send(SOLVE_1, x_stage.at[0], x_own, 10, x_sem, (4, 1))
        for i, target in enumerate((5, 0, 1)):
            send(SOLVE_1, x_stage.at[0], x_own, 11 + i, x_sem, (target, 1))

    def rows_of(c, r0, r1):
        return plane_row(r0, r1) & (col == c)

    @pl.when(here((2, 0)))
    def _():
        load_first.wait()
        arrived(x_own, x_sem)
        stage_f[0] = product(panel[0], x_own[...])
        send((2, 0), stage_f.at[0], acc_f.at[0], 19, acc_f_sem.at[0], sibling)

    @pl.when(here((3, 0)))
    def _():
        load_right.wait()
        load_first.wait()
        arrived(x_own, x_sem)
        stage_b[0] = (right[...] - product(panel[0], x_own[...])).astype(BF16)
        send((3, 0), stage_b.at[0], acc_b.at[0], 19, acc_b_sem.at[0], SOLVE_23)
        send((3, 0), x_own, x_own, 9, x_sem, (4, 0))

    @pl.when(here((0, 1)))
    def _():
        arrived(x_stage.at[0], side_sem)
        for i, r in enumerate((5, 6, 7)):
            send((0, 1), x_stage.at[0], x_own, 9 + i, x_sem, (r, 0))
        arrived(x_own, x_sem)
        for i, r in enumerate((6, 7)):
            send((0, 1), x_own, x_own, 12 + i, x_sem, (r, 1))

    low_0 = rows_of(0, 4, 8)
    low_1 = rows_of(1, 4, 8)

    @pl.when(low_0)
    def _():
        load_first.wait()
        arrived(x_own, x_sem)
        stage_f[0] = product(panel[0], x_own[...])
        send(low_0, stage_f.at[0], acc_f.at[0], 18, acc_f_sem.at[0], sibling)

    @pl.when(low_1)
    def _():
        load_first.wait()
        arrived(x_own, x_sem)
        load_right.wait()
        arrived(acc_f.at[0], acc_f_sem.at[0])
        stage_b[0] = (right[...] - acc_f[0] - product(panel[0], x_own[...])).astype(BF16)

    for r, target, slot in ((4, 4, 0), (5, 4, 1), (6, 7, 1), (7, 7, 0)):

        @pl.when(here((r, 1)))
        def _(r=r, target=target, slot=slot):
            send((r, 1), stage_b.at[0], acc_b.at[slot], 19, acc_b_sem.at[slot], (target, 3))

    def scatter(when, slot, k, s):
        solver = SOLVE_23 if k < 4 else SOLVE_47
        for q in range(N_X):
            device = (solver[0], 2 * q + k % 2)
            if device != solver:
                rows = pl.ds(q * quarter, quarter)
                send(when, x_stage.at[slot, rows], relays.at[max(k // 2 - 2, 0)], s + q, relay_sem.at[max(k // 2 - 2, 0)], device)

    own_rows = pl.ds(pl.multiple_of(x * quarter, quarter), quarter)
    other_planes = [(d * N_Z + z, col) for d in range(1, N_Y)]
    other_z = [y * N_Z + (z + d) % N_Z for d in (2, 3, 4, 5, 1, 6, 7)]

    def relay_quarter(k):
        solver = SOLVE_23 if k < 4 else SOLVE_47
        slot = max(k // 2 - 2, 0)
        piece = relays.at[slot]
        first = 40 + 12 * slot

        place = lambda: (z == solver[0]) & (core == k % 2)

        @pl.when(place())
        def _():
            @pl.when(here(solver))
            def _():
                q = solver[1] // 2
                relays[slot] = x_stage[k - 2 if k < 4 else k - 4, q * quarter : (q + 1) * quarter]

            @pl.when(jnp.logical_not(here(solver)))
            def _():
                arrived(piece, relay_sem.at[slot])

            @pl.when(y == 0)
            def _():
                for i, device in enumerate(other_planes):
                    send(lambda: place() & (y == 0), piece, piece, first + i, relay_sem.at[slot], device)

            for i, target in enumerate(other_z):
                direct = (lambda target=target: (y != 0) | ((target != 4) & (target != 7))) if k < 4 else (lambda: True)

                @pl.when(direct())
                def _(i=i, target=target, direct=direct):
                    wanted = lambda: place() & direct()
                    send(wanted, piece, x_own.at[own_rows], first + 3 + i, x_sem, (target, k))

            @pl.when(col == k)
            def _():
                x_own[own_rows] = relays[slot]

            @pl.when(col != k)
            def _():
                send(lambda: place() & (col != k), piece, x_own.at[own_rows], first + 10, x_sem, (row, k))

    @pl.when(here(SOLVE_23))
    def _():
        when = SOLVE_23
        load_right.wait()
        load_first.wait()
        arrived(acc_f.at[0], acc_f_sem.at[0])
        arrived(x_own, x_sem)
        total = right[...] - acc_f[0] - product(panel[0], x_own[...])
        inverse_arrived(0)
        value = solve(0, total)
        x_stage[0] = value.astype(BF16)
        x_full[0] = value
        for i, r in enumerate((4, 7)):
            send(when, x_stage.at[0], x_own, 20 + i, x_sem, (r, 2))
        scatter(when, 0, 2, 26)
        arrived(blocks.at[0], block_sem.at[0])
        arrived(acc_b.at[0], acc_b_sem.at[0])
        stage_f[0] = acc_b[0].astype(F32) - product(blocks[0], x_own[...])
        arrived(blocks.at[1], block_sem.at[1])
        total = stage_f[0] - product(blocks[1], x_stage[0])
        inverse_arrived(1)
        value = solve(1, total)
        x_stage[1] = value.astype(BF16)
        x_full[1] = value
        for i, r in enumerate((4, 7)):
            send(when, x_stage.at[1], x_own, 23 + i, x_sem, (r, 3))
        scatter(when, 1, 3, 29)
        send(when, x_own, x_own, 33, x_sem, (3, 1))

    low_rows = (row == 4) | (row == 7)
    low_2 = low_rows & (col == 2)

    @pl.when(low_2)
    def _():
        load_first.wait()
        arrived(x_own, x_sem)
        stage_f[0] = product(panel[0], x_own[...])
        send(low_2, stage_f.at[0], acc_f.at[0], 18, acc_f_sem.at[0], sibling)
        arrived(blocks.at[0], block_sem.at[0])
        stage_f[1] = product(blocks[0], x_own[...])
        send(low_2, stage_f.at[1], acc_f.at[1], 19, acc_f_sem.at[1], sibling)

    for r, rows in ((4, (4, 5)), (7, (6, 7))):

        @pl.when(here((r, 3)))
        def _(r=r, rows=rows):
            load_first.wait()
            for i, target in enumerate(rows):
                j = 0 if target == r else 1
                if j == 1:
                    arrived(blocks.at[0], block_sem.at[0])
                arrived(acc_b.at[j], acc_b_sem.at[j])
                arrived(acc_f.at[j], acc_f_sem.at[j])
                stage_f[j] = acc_b[j].astype(F32) - acc_f[j]
                if i == 0:
                    arrived(x_own, x_sem)
                    for c in (0, 1):
                        pl.semaphore_signal(go_sem, inc=1, device_id=(r, c), device_id_type=MESH)
                block = panel[0] if target == r else blocks[0]
                stage_b[i] = (stage_f[j] - product(block, x_own[...])).astype(BF16)
                if target == 6:
                    pl.semaphore_wait(go_sem, 1)
                send((r, 3), stage_b.at[i], acc_b.at[target - 4], 18 + i, acc_b_sem.at[target - 4], SOLVE_47)
                if target == 5:
                    pl.semaphore_signal(go_sem, inc=1, device_id=(7, 3), device_id_type=MESH)

    @pl.when(here(SOLVE_47))
    def _():
        when = SOLVE_47
        load_inv.wait()
        split_inverse(0)
        load_first.wait()
        load_right.wait()
        place = {(1, 0): blocks.at[0], (2, 0): panel.at[0], (2, 1): blocks.at[1]}
        place |= {(3, 0): blocks.at[2], (3, 1): blocks.at[3], (3, 2): blocks.at[4]}
        for slot in range(5):
            arrived(blocks.at[slot], block_sem.at[slot])
        for slot in range(1, 4):
            inverse_arrived(slot)
        for q in range(4):
            for j in range(q - 1):
                done = product(place[q, j][...], x_stage[j])
                acc_f[q] = done if j == 0 else acc_f[q] + done
            arrived(acc_b.at[q], acc_b_sem.at[q])
            total = acc_b[q].astype(F32)
            if q > 1:
                total -= acc_f[q]
            if q > 0:
                total -= product(place[q, q - 1][...], x_stage[q - 1])
            value = solve(q, total)
            x_stage[q] = value.astype(BF16)
            x_full[q] = value
            scatter(when, q, 4 + q, 20 + 4 * q)
            if q < 2:
                send(when, x_full.at[q], x_in, 36 + q, x_in_sem, (4 + q, 0))
        send(when, x_full.at[2], x_in, 38, x_in_sem, (6, 0))
    for k in range(2, 8):
        relay_quarter(k)

    waited = rows_of(0, 0, 8) | here((0, 1)) | low_1 | (low_rows & (col < 4)) | here(SOLVE_23)

    @pl.when(jnp.logical_not(waited) & (col < 2))
    def _():
        arrived(x_own, x_sem)

    @pl.when(jnp.logical_not(waited) & (col >= 2))
    def _():
        @pl.when(z != relay_z)
        def _():
            arrived(x_own, x_sem)

        @pl.when(z == relay_z)
        def _():
            arrived(x_own.at[pl.ds(0, 3 * quarter)], x_sem)

    @pl.when(here(column_root[1]))
    def _():
        spread_from_root(1)

    relay = is_root & (y != 0)
    peers = [(i, (y * N_Z + (z + d) % N_Z, col)) for i, d in enumerate((4, 3, 5, 2, 6, 1, 7))]

    @pl.when(relay)
    def _():
        for i, peer in peers:
            send(relay, x_own, x_own, 9 + i, x_sem, peer)

    always = row >= 0
    waited_first = rows_of(0, 2, 8) | low_1 | (low_rows & (col < 4))
    waited_first = waited_first | here(SOLVE_1) | here(SOLVE_23) | here(SOLVE_47)

    @pl.when(jnp.logical_not(waited_first))
    def _():
        load_first.wait()

    load_rest.wait()
    value = x_own[...]
    distances = (2, 1, 3, 0)
    owners = [(x + d) % N_X for d in distances]
    for j, owner in enumerate(owners):
        pair_out[j] = product(panel[2 * owner + 1 - core], value).astype(BF16)
        send(always, pair_out.at[j], pair_in.at[j], 64 + j, pair_sem.at[j], sibling)

    @pl.when(low_rows & (col < 2))
    def _():
        pl.semaphore_wait(go_sem, 1)

    for j, (d, owner) in enumerate(zip(distances, owners)):
        total = product(panel[2 * owner + core], value)
        arrived(pair_in.at[j], pair_sem.at[j])
        total = total + pair_in[j].astype(F32)
        if d > 0:
            sums[j] = total.astype(BF16)
            send(always, sums.at[j], cross_in.at[d - 1], 68 + j, cross_sem.at[d - 1], (row, owner * 2 + core))
    @pl.when(here(SOLVE_23))
    def _():
        for q in range(2):
            send(SOLVE_23, x_full.at[q], x_in, 36 + q, x_in_sem, (2 + q, 0))

    @pl.when(here(SOLVE_47))
    def _():
        send(SOLVE_47, x_full.at[3], x_in, 39, x_in_sem, (7, 0))

    load_own.wait()
    total = right_own[...] - total
    for d in range(3):
        arrived(cross_in.at[d], cross_sem.at[d])
        total -= cross_in[d].astype(F32)
    out[...] = total

    solved = plane_row(0, 8) & (col == 0)

    @pl.when(solved & (row < 2))
    def _():
        out[...] = x_full[0]

    @pl.when(solved & (row >= 2))
    def _():
        arrived(x_in, x_in_sem)
        out[...] = x_in[...]

    @pl.when(jnp.logical_not(is_source | here(SOLVE_0) | here(SOLVE_47)))
    def _():
        load_inv.wait()

    read_right = here((3, 0)) | here(SOLVE_0) | here(SOLVE_1) | here(SOLVE_23) | here(SOLVE_47) | low_1

    @pl.when(jnp.logical_not(read_right))
    def _():
        load_right.wait()

    buffers = [x_own, stage_f.at[0], relays.at[0]]

    def same_size(shape, dtype):
        for buffer in buffers:
            if buffer.shape == shape and buffer.dtype == dtype:
                return buffer
        if shape == panel.shape[1:]:
            return panel.at[0]
        return part(0, 0, shape[1] // quarter - 1)

    for when, s, shape, dtype in pending:

        @pl.when(here(when) if isinstance(when, tuple) else when() if callable(when) else when)
        def _(s=s, shape=shape, dtype=dtype):
            ref = same_size(shape, dtype)
            remote(ref, ref, s, x_sem, sibling).wait_send()


def body(lower, slab, inverses):
    row_blocks, _, order, _, _, _ = lower.shape
    width = slab.shape[3]
    vmem = pltpu.VMEM
    dma = pltpu.SemaphoreType.DMA
    scratch = [
        vmem((row_blocks, order, order), BF16),
        vmem((order, order), F32),
        vmem((4, 2, order, order), BF16),
        vmem((5, order, order), BF16),
        vmem((order, width), F32),
        vmem((order, width), F32),
        vmem((order, width), BF16),
        vmem((4, order, width), BF16),
        vmem((4, order, width), F32),
        vmem((order, width), F32),
        vmem((4, order, width), F32),
        vmem((4, order, width), BF16),
        vmem((2, order, width), F32),
        vmem((2, order, width), BF16),
        vmem((2, order // 4, width), BF16),
        vmem((4, order, width), BF16),
        vmem((4, order, width), BF16),
        vmem((3, order, width), BF16),
        vmem((3, order, width), BF16),
        dma((5,)),
        dma((72,)),
        dma,
        dma,
        dma,
        pltpu.SemaphoreType.REGULAR,
        dma((2,)),
        dma((4, 2, 4)),
        dma((5,)),
        dma((4,)),
        dma((4,)),
        dma((4,)),
        dma((3,)),
    ]
    result = pl.pallas_call(
        kernel,
        name="window_solve",
        out_shape=jax.ShapeDtypeStruct((order, width), F32),
        in_specs=[pl.BlockSpec(memory_space=pltpu.HBM)] * 3,
        out_specs=pl.BlockSpec(memory_space=pltpu.VMEM),
        scratch_shapes=scratch,
        compiler_params=pltpu.CompilerParams(
            collective_id=0, has_side_effects=True, vmem_limit_bytes=53 << 20
        ),
    )(
        lower.reshape(row_blocks, order, order),
        slab.reshape(row_blocks, order, width),
        inverses.reshape(order, order),
    )
    return result.reshape(1, 1, order, width)


def solution(mesh):
    in_specs = (
        P(None, "row", None, None, "col", None),
        P(None, "row", None, None),
        P(None, "col", None, None),
    )
    out_specs = P("col", "row", None, None)
    return jax.shard_map(body, mesh=mesh, in_specs=in_specs, out_specs=out_specs, check_vma=False)
```

```python
import jax
import jax.numpy as jnp
from jax import lax
from jax.experimental import pallas as pl
from jax.experimental.pallas import tpu as pltpu
from jax.sharding import PartitionSpec as P

MESH = pl.DeviceIdType.MESH
F32 = jnp.float32
BF16 = jnp.bfloat16

N_Z, N_Y, N_X = 8, 4, 4
SOLVE_0 = (0, 0)
SOLVE_1 = (1, 0)
SOLVE_23 = (2, 1)
SOLVE_47 = (6, 4)
HIGH = tuple((0, b) for b in range(4))
LOW = tuple((1, b) for b in range(4))
INVERSE_SENDS = (
    ((1, 1), SOLVE_1, 0, HIGH + LOW),
    ((9, 2), SOLVE_23, 0, (HIGH[0], HIGH[3])),
    ((25, 2), SOLVE_23, 0, (HIGH[1], HIGH[2])),
    ((12, 3), SOLVE_23, 1, (HIGH[0], HIGH[3])),
    ((28, 3), SOLVE_23, 1, (HIGH[1], HIGH[2])),
    ((6, 5), SOLVE_47, 1, HIGH),
    ((14, 6), SOLVE_47, 2, HIGH),
    ((30, 7), SOLVE_47, 3, HIGH),
)
BLOCK_SENDS = (
    ((3, 1), SOLVE_23, 0),
    ((3, 2), SOLVE_23, 1),
    ((5, 4), SOLVE_47, 0),
    ((6, 5), SOLVE_47, 1),
    ((7, 4), SOLVE_47, 2),
    ((7, 5), SOLVE_47, 3),
    ((7, 6), SOLVE_47, 4),
    *(((5, c), (4, c), 0) for c in (2, 3)),
    *(((6, c), (7, c), 0) for c in (2, 3)),
)


def special_pairs():
    pairs = {(s, t) for s, t, _, _ in INVERSE_SENDS} | {(s, t) for s, t, _ in BLOCK_SENDS}
    pairs |= {(SOLVE_0, (z, 0)) for z in (1, 2, 3)} | {(SOLVE_1, (z, 1)) for z in (0, 1, 2, 4, 5)}
    pairs |= {((r, 1), (4 if r < 6 else 7, 3)) for r in range(4, 8)}
    pairs |= {((3, 0), (4, 0)), ((0, 1), (5, 0))} | {((0, 1), (r, c)) for r in (6, 7) for c in (0, 1)}
    pairs |= {((3, 0), SOLVE_23)}
    pairs |= {(SOLVE_23, (r, c)) for c in (2, 3) for r in (4, 7)}
    pairs |= {(SOLVE_23, (2, c)) for c in range(8) if c != 1}
    pairs |= {(SOLVE_47, (6, c)) for c in range(8) if c != 4}
    pairs |= {((4, 3), (7, 3))} | {((r, 3), SOLVE_47) for r in (4, 7)} | {((r, 0), (r, 3)) for r in (4, 7)} | {((r, 1), (r, 3)) for r in (4, 7)}
    pairs |= {(SOLVE_47, (r, 0)) for r in range(4, 8)}
    return sorted({tuple(sorted(p)) for p in pairs})


def kernel(
    lower, slab, inverses, out,
    first, panel, inv, inv_parts, blocks, right, right_own, x_own, x_stage, x_full, x_in,
    acc_f, acc_b, stage_f, stage_b, relays, x_mate, ours, sums, cross_in,
    load_sem, send_sem, x_sem, x_in_sem, side_sem, go_sem, relay_sem, inv_sem, block_sem, acc_f_sem, acc_b_sem, mate_sem, cross_sem,
):
    row = lax.axis_index("row")
    col = lax.axis_index("col")
    y, z = row // N_Z, row % N_Z
    x, core = col // 2, col % 2
    half = first.shape[0] // 2
    quarter = half // 2
    width = x_own.shape[1]

    def here(device):
        return (row == device[0]) & (col == device[1])

    def plane_row(r0, r1):
        return (row >= r0) & (row < r1)

    root_z = col
    sibling = (row, col + 1 - 2 * core)
    pending = []
    relay_waits = {}

    def remote(src, dst, s, recv, device):
        return pltpu.make_async_remote_copy(
            src_ref=src, dst_ref=dst, send_sem=send_sem.at[s], recv_sem=recv, device_id=device, device_id_type=MESH
        )

    def send(when, src, dst, s, recv, device):
        remote(src, dst, s, recv, device).start()
        if when is not None:
            pending.append((when, s, src.shape, src.dtype))

    def arrived(dst, recv):
        remote(dst, dst, 0, recv, sibling).wait_recv()

    load_first = pltpu.make_async_copy(lower.at[0, 0], first, load_sem.at[0])
    load_ours = pltpu.make_async_copy(lower.at[:, core], panel.at[0], load_sem.at[1])
    load_inv = pltpu.make_async_copy(inverses, inv, load_sem.at[2])
    load_right = pltpu.make_async_copy(slab.at[0], right, load_sem.at[3])
    load_own = pltpu.make_async_copy(slab.at[col], right_own, load_sem.at[4])
    load_inv.start()
    load_right.start()
    load_first.start()

    def clear_slot(slot):
        inv_parts[slot] = jnp.zeros(inv_parts.shape[1:], BF16)

    @pl.when(here(SOLVE_1))
    def _():
        clear_slot(0)

    @pl.when(here(SOLVE_23))
    def _():
        clear_slot(0)
        clear_slot(1)

    @pl.when(here(SOLVE_47))
    def _():
        clear_slot(1)
        clear_slot(2)
        clear_slot(3)

    barrier = pltpu.get_barrier_semaphore()

    def greet(device):
        pl.semaphore_signal(barrier, inc=1, device_id=device, device_id_type=MESH)

    greet(sibling)
    for d in range(1, N_X):
        greet((row, (x + d) % N_X * 2 + core))
    count = jnp.int32(N_X)
    is_root = (z == root_z) & (col < 2)
    in_other = (col < 2) & (y != 0)

    @pl.when(is_root & in_other)
    def _():
        for d in range(1, N_Z):
            greet((y * N_Z + (z + d) % N_Z, col))

    @pl.when(jnp.logical_not(is_root) & in_other)
    def _():
        greet((y * N_Z + root_z, col))

    count += jnp.where(in_other, jnp.where(is_root, N_Z - 1, 1), 0)
    is_relay = (z == 2) | (z == 6)
    relay_z = jnp.where(col < 4, 2, 6)

    @pl.when(is_relay)
    def _():
        for k in range(2, 8):

            @pl.when((core == k % 2) & (z == (2 if k < 4 else 6)))
            def _(k=k):
                for d in range(1, N_Z):
                    greet((y * N_Z + (z + d) % N_Z, k))

                @pl.when(col != k)
                def _():
                    greet((row, k))

    count += jnp.where(z == 2, N_Z - 1 + jnp.where(x == 1, 0, 1), 0)
    count += jnp.where(z == 6, 2 * (N_Z - 1) + jnp.where(x >= 2, 1, 2), 0)

    @pl.when(col >= 2)
    def _():
        for q in range(N_X):

            @pl.when((z != relay_z) | (q != x))
            def _(q=q):
                greet((y * N_Z + relay_z, 2 * q + core))

    count += jnp.where(col >= 2, jnp.where(z == jnp.where(col < 4, 2, 6), N_X - 1, N_X), 0)
    in_line = is_root | is_relay

    @pl.when(in_line & (y == 0))
    def _():
        for d in range(1, N_Y):
            greet((d * N_Z + z, col))

    @pl.when(in_line & (y != 0))
    def _():
        greet((z, col))

    count += jnp.where(in_line, jnp.where(y == 0, N_Y - 1, 1), 0)
    partners = {}
    for a, b in special_pairs():
        partners.setdefault(a, []).append(b)
        partners.setdefault(b, []).append(a)
    by_row = {}
    for device, others in partners.items():
        count += jnp.where(here(device), len(others), 0)
        by_row.setdefault(device[0], []).append((device[1], others))

    def greet_row(r):
        @pl.when(row == r)
        def _():
            for c, others in by_row[r]:

                @pl.when(col == c)
                def _(others=others):
                    for other in others:
                        greet(other)

    @pl.when(y == 0)
    def _():
        for r in by_row:
            if r < N_Z:
                greet_row(r)

    @pl.when(y != 0)
    def _():
        for r in by_row:
            if r >= N_Z:
                greet_row(r)

    def split_inverse(slot):
        value = inv[...]
        high = value.astype(BF16)
        inv_parts[slot, 0] = high
        inv_parts[slot, 1] = (value - high.astype(F32)).astype(BF16)

    def part(slot, piece, b):
        return inv_parts.at[slot, piece, pl.ds(b * quarter, quarter), pl.ds(0, (b + 1) * quarter)]

    def inverse_arrived(slot, parts=HIGH):
        for piece, b in parts:
            arrived(part(slot, piece, b), inv_sem.at[slot, piece, b])

    def solve(slot, total, low_part=False):
        high = total.astype(BF16)
        low = (total - high.astype(F32)).astype(BF16)
        both = jnp.concatenate([high, low], axis=1)

        def times(rows, depth):
            done = jnp.dot(inv_parts[slot, 0, rows, :depth], both[:depth], preferred_element_type=F32)
            if low_part:
                done += jnp.dot(inv_parts[slot, 1, rows, :depth], both[:depth], preferred_element_type=F32)
            return done

        whole = jnp.concatenate([times(slice(0, half), half), times(slice(half, 2 * half), 2 * half)], axis=0)
        return whole[:, :width] + whole[:, width:]

    def product(block, value):
        return jnp.dot(block, value, preferred_element_type=F32)

    is_source = here(INVERSE_SENDS[0][0])
    for source, _, _, _ in INVERSE_SENDS[1:]:
        is_source |= here(source)

    @pl.when(is_source)
    def _():
        load_inv.wait()
        split_inverse(0)

    @pl.when(here(SOLVE_0))
    def _():
        load_inv.wait()
        split_inverse(0)
        load_right.wait()
        value = solve(0, right[...], low_part=True)
        x_own[...] = value.astype(BF16)
        x_full[0] = value

    pl.semaphore_wait(barrier, count)

    load_ours.start()
    load_own.start()

    for source, solver, slot in BLOCK_SENDS:

        @pl.when(here(source))
        def _(source=source, solver=solver, slot=slot):
            send(source, lower.at[0, 0], blocks.at[slot], 0, block_sem.at[slot], solver)

    for source, solver, slot, pieces in INVERSE_SENDS:

        @pl.when(here(source))
        def _(source=source, solver=solver, slot=slot, pieces=pieces):
            for piece, b in pieces:
                s = 1 + piece * 4 + b
                send(source, part(0, piece, b), part(slot, piece, b), s, inv_sem.at[slot, piece, b], solver)

    remote(lower.at[:, 1 - core], panel.at[1], 65, mate_sem.at[1], sibling).start()

    column_root = [SOLVE_0, (1, 1)]
    in_plane = [(1, 3, 2), ()]

    def spread_from_root(c):
        when = column_root[c]
        root_row = column_root[c][0]
        for i, target in enumerate(in_plane[c][:1]):
            send(when, x_own, x_own, 9 + i, x_sem, (target, c))
        if c == 0:
            send(when, x_own, x_stage.at[0], 19, side_sem, (0, 1))
        for d in (2, 1, 3):
            send(when, x_own, x_own, 15 + d, x_sem, (d * N_Z + root_row, c))
        for i, target in enumerate(in_plane[c]):
            if i > 0:
                send(when, x_own, x_own, 9 + i, x_sem, (target, c))

    @pl.when(here(SOLVE_0))
    def _():
        spread_from_root(0)

    @pl.when(here(SOLVE_1))
    def _():
        load_right.wait()
        load_first.wait()
        inverse_arrived(0, HIGH + LOW)
        arrived(x_own, x_sem)
        value = solve(0, right[...] - product(first[...], x_own[...]), low_part=True)
        x_stage[0] = value.astype(BF16)
        x_full[0] = value
        send(SOLVE_1, x_stage.at[0], x_own, 9, x_sem, (2, 1))
        send(SOLVE_1, x_stage.at[0], x_own, 10, x_sem, (4, 1))
        for i, target in enumerate((5, 0, 1)):
            send(SOLVE_1, x_stage.at[0], x_own, 11 + i, x_sem, (target, 1))

    def rows_of(c, r0, r1):
        return plane_row(r0, r1) & (col == c)

    @pl.when(here((2, 0)))
    def _():
        load_first.wait()
        arrived(x_own, x_sem)
        stage_f[0] = product(first[...], x_own[...])
        send((2, 0), stage_f.at[0], acc_f.at[0], 19, acc_f_sem.at[0], sibling)

    @pl.when(here((3, 0)))
    def _():
        load_right.wait()
        load_first.wait()
        arrived(x_own, x_sem)
        stage_b[0] = (right[...] - product(first[...], x_own[...])).astype(BF16)
        send((3, 0), stage_b.at[0], acc_b.at[0], 19, acc_b_sem.at[0], SOLVE_23)
        send((3, 0), x_own, x_own, 9, x_sem, (4, 0))

    @pl.when(here((0, 1)))
    def _():
        arrived(x_stage.at[0], side_sem)
        for i, r in enumerate((5, 6, 7)):
            send((0, 1), x_stage.at[0], x_own, 9 + i, x_sem, (r, 0))
        arrived(x_own, x_sem)
        for i, r in enumerate((6, 7)):
            send((0, 1), x_own, x_own, 12 + i, x_sem, (r, 1))

    low_0 = rows_of(0, 4, 8)
    low_1 = rows_of(1, 4, 8)

    @pl.when(low_0)
    def _():
        load_first.wait()
        arrived(x_own, x_sem)
        stage_f[0] = product(first[...], x_own[...])
        send(low_0, stage_f.at[0], acc_f.at[0], 18, acc_f_sem.at[0], sibling)

    @pl.when(low_1)
    def _():
        load_first.wait()
        arrived(x_own, x_sem)
        load_right.wait()
        arrived(acc_f.at[0], acc_f_sem.at[0])
        stage_b[0] = (right[...] - acc_f[0] - product(first[...], x_own[...])).astype(BF16)

    for r, target, slot in ((4, 4, 0), (5, 4, 1), (6, 7, 1), (7, 7, 0)):

        @pl.when(here((r, 1)))
        def _(r=r, target=target, slot=slot):
            send((r, 1), stage_b.at[0], acc_b.at[slot], 19, acc_b_sem.at[slot], (target, 3))

    def scatter(when, slot, k, s):
        solver = SOLVE_23 if k < 4 else SOLVE_47
        for q in range(N_X):
            device = (solver[0], 2 * q + k % 2)
            if device != solver:
                rows = pl.ds(q * quarter, quarter)
                send(when, x_stage.at[slot, rows], relays.at[max(k // 2 - 2, 0)], s + q, relay_sem.at[max(k // 2 - 2, 0)], device)

    own_rows = pl.ds(pl.multiple_of(x * quarter, quarter), quarter)
    other_planes = [(d * N_Z + z, col) for d in range(1, N_Y)]
    other_z = [y * N_Z + (z + d) % N_Z for d in (2, 3, 4, 5, 1, 6, 7)]

    def relay_quarter(k):
        solver = SOLVE_23 if k < 4 else SOLVE_47
        slot = max(k // 2 - 2, 0)
        piece = relays.at[slot]
        base = 40 + 12 * slot
        waits = relay_waits.setdefault(k, [])

        place = lambda: (z == solver[0]) & (core == k % 2)

        @pl.when(place())
        def _():
            @pl.when(here(solver))
            def _():
                q = solver[1] // 2
                relays[slot] = x_stage[k - 2 if k < 4 else k - 4, q * quarter : (q + 1) * quarter]

            @pl.when(jnp.logical_not(here(solver)))
            def _():
                arrived(piece, relay_sem.at[slot])

            @pl.when(y == 0)
            def _():
                for i, device in enumerate(other_planes):
                    send(None, piece, piece, base + i, relay_sem.at[slot], device)
                    waits.append((lambda: y == 0, base + i))

            for i, target in enumerate(other_z):
                direct = (lambda target=target: (y != 0) | ((target != 4) & (target != 7))) if k < 4 else (lambda: True)

                @pl.when(direct())
                def _(i=i, target=target, direct=direct):
                    waits.append((direct, base + 3 + i))
                    send(None, piece, x_own.at[own_rows], base + 3 + i, x_sem, (target, k))

            @pl.when(col == k)
            def _():
                x_own[own_rows] = relays[slot]

            @pl.when(col != k)
            def _():
                waits.append((lambda: col != k, base + 10))
                send(None, piece, x_own.at[own_rows], base + 10, x_sem, (row, k))

    @pl.when(here(SOLVE_23))
    def _():
        when = SOLVE_23
        load_right.wait()
        load_first.wait()
        arrived(acc_f.at[0], acc_f_sem.at[0])
        arrived(x_own, x_sem)
        total = right[...] - acc_f[0] - product(first[...], x_own[...])
        inverse_arrived(0)
        value = solve(0, total)
        x_stage[0] = value.astype(BF16)
        x_full[0] = value
        for i, r in enumerate((4, 7)):
            send(when, x_stage.at[0], x_own, 20 + i, x_sem, (r, 2))
        scatter(when, 0, 2, 26)
        arrived(blocks.at[0], block_sem.at[0])
        arrived(acc_b.at[0], acc_b_sem.at[0])
        stage_f[0] = acc_b[0].astype(F32) - product(blocks[0], x_own[...])
        arrived(blocks.at[1], block_sem.at[1])
        total = stage_f[0] - product(blocks[1], x_stage[0])
        inverse_arrived(1)
        value = solve(1, total)
        x_stage[1] = value.astype(BF16)
        x_full[1] = value
        for i, r in enumerate((4, 7)):
            send(when, x_stage.at[1], x_own, 23 + i, x_sem, (r, 3))
        scatter(when, 1, 3, 29)
        send(when, x_own, x_own, 33, x_sem, (3, 1))

    low_rows = (row == 4) | (row == 7)
    low_2 = low_rows & (col == 2)

    @pl.when(low_2)
    def _():
        load_first.wait()
        arrived(x_own, x_sem)
        stage_f[0] = product(first[...], x_own[...])
        send(low_2, stage_f.at[0], acc_f.at[0], 18, acc_f_sem.at[0], sibling)
        arrived(blocks.at[0], block_sem.at[0])
        stage_f[1] = product(blocks[0], x_own[...])
        send(low_2, stage_f.at[1], acc_f.at[1], 19, acc_f_sem.at[1], sibling)

    for r, rows in ((4, (4, 5)), (7, (6, 7))):

        @pl.when(here((r, 3)))
        def _(r=r, rows=rows):
            load_first.wait()
            for i, target in enumerate(rows):
                j = 0 if target == r else 1
                if j == 1:
                    arrived(blocks.at[0], block_sem.at[0])
                arrived(acc_b.at[j], acc_b_sem.at[j])
                arrived(acc_f.at[j], acc_f_sem.at[j])
                stage_f[j] = acc_b[j].astype(F32) - acc_f[j]
                if i == 0:
                    arrived(x_own, x_sem)
                    for c in (0, 1):
                        pl.semaphore_signal(go_sem, inc=1, device_id=(r, c), device_id_type=MESH)
                block = first[...] if target == r else blocks[0]
                stage_b[i] = (stage_f[j] - product(block, x_own[...])).astype(BF16)
                if target == 6:
                    pl.semaphore_wait(go_sem, 1)
                send((r, 3), stage_b.at[i], acc_b.at[target - 4], 18 + i, acc_b_sem.at[target - 4], SOLVE_47)
                if target == 5:
                    pl.semaphore_signal(go_sem, inc=1, device_id=(7, 3), device_id_type=MESH)

    @pl.when(here(SOLVE_47))
    def _():
        when = SOLVE_47
        load_inv.wait()
        split_inverse(0)
        load_first.wait()
        load_right.wait()
        place = {(1, 0): blocks.at[0], (2, 0): first, (2, 1): blocks.at[1]}
        place |= {(3, 0): blocks.at[2], (3, 1): blocks.at[3], (3, 2): blocks.at[4]}
        for slot in range(5):
            arrived(blocks.at[slot], block_sem.at[slot])
        for slot in range(1, 4):
            inverse_arrived(slot)
        for q in range(4):
            for j in range(q - 1):
                done = product(place[q, j][...], x_stage[j])
                acc_f[q] = done if j == 0 else acc_f[q] + done
            arrived(acc_b.at[q], acc_b_sem.at[q])
            total = acc_b[q].astype(F32)
            if q > 1:
                total -= acc_f[q]
            if q > 0:
                total -= product(place[q, q - 1][...], x_stage[q - 1])
            value = solve(q, total)
            x_stage[q] = value.astype(BF16)
            x_full[q] = value
            scatter(when, q, 4 + q, 20 + 4 * q)
            if q < 2:
                send(when, x_full.at[q], x_in, 36 + q, x_in_sem, (4 + q, 0))
        send(when, x_full.at[2], x_in, 38, x_in_sem, (6, 0))
    for k in range(2, 8):
        relay_quarter(k)

    waited = rows_of(0, 0, 8) | here((0, 1)) | low_1 | (low_rows & (col < 4)) | here(SOLVE_23)

    @pl.when(jnp.logical_not(waited) & (col < 2))
    def _():
        arrived(x_own, x_sem)

    @pl.when(jnp.logical_not(waited) & (col >= 2))
    def _():
        @pl.when(z != relay_z)
        def _():
            arrived(x_own, x_sem)

        @pl.when(z == relay_z)
        def _():
            arrived(x_own.at[pl.ds(0, 3 * quarter)], x_sem)

    @pl.when(here(column_root[1]))
    def _():
        spread_from_root(1)

    relay = is_root & (y != 0)
    peers = [(i, (y * N_Z + (z + d) % N_Z, col)) for i, d in enumerate((4, 3, 5, 2, 6, 1, 7))]

    @pl.when(relay)
    def _():
        for i, peer in peers:
            send(relay, x_own, x_own, 9 + i, x_sem, peer)

    always = row >= 0
    waited_first = rows_of(0, 2, 8) | low_1 | (low_rows & (col < 4))
    waited_first = waited_first | here(SOLVE_1) | here(SOLVE_23) | here(SOLVE_47)

    @pl.when(jnp.logical_not(waited_first))
    def _():
        load_first.wait()

    send(always, x_own, x_mate, 64, mate_sem.at[0], sibling)
    load_ours.wait()
    half_panel = panel[0].reshape(4 * 2 * half, 2 * half)
    ours[...] = product(half_panel, x_own[...]).reshape(4, 2 * half, width)
    arrived(panel.at[1], mate_sem.at[1])
    arrived(x_mate, mate_sem.at[0])

    @pl.when(low_rows & (col < 2))
    def _():
        pl.semaphore_wait(go_sem, 1)

    value = x_mate[...]
    for j, d in enumerate((2, 1, 3, 0)):
        owner = (x + d) % N_X
        total = ours[owner] + product(panel[1, owner], value)
        if d > 0:
            sums[j] = total.astype(BF16)
            send(always, sums.at[j], cross_in.at[d - 1], 68 + j, cross_sem.at[d - 1], (row, owner * 2 + core))
    @pl.when(here(SOLVE_23))
    def _():
        for q in range(2):
            send(SOLVE_23, x_full.at[q], x_in, 36 + q, x_in_sem, (2 + q, 0))

    @pl.when(here(SOLVE_47))
    def _():
        send(SOLVE_47, x_full.at[3], x_in, 39, x_in_sem, (7, 0))

    load_own.wait()
    total = right_own[...] - total
    for d in range(3):
        arrived(cross_in.at[d], cross_sem.at[d])
        total -= cross_in[d].astype(F32)
    out[...] = total

    solved = plane_row(0, 8) & (col == 0)

    @pl.when(solved & (row < 2))
    def _():
        out[...] = x_full[0]

    @pl.when(solved & (row >= 2))
    def _():
        arrived(x_in, x_in_sem)
        out[...] = x_in[...]

    @pl.when(jnp.logical_not(is_source | here(SOLVE_0) | here(SOLVE_47)))
    def _():
        load_inv.wait()

    read_right = here((3, 0)) | here(SOLVE_0) | here(SOLVE_1) | here(SOLVE_23) | here(SOLVE_47) | low_1

    @pl.when(jnp.logical_not(read_right))
    def _():
        load_right.wait()

    buffers = [x_own, stage_f.at[0], relays.at[0]]

    def same_size(shape, dtype):
        for buffer in buffers:
            if buffer.shape == shape and buffer.dtype == dtype:
                return buffer
        if shape == first.shape:
            return first
        return part(0, 0, shape[1] // quarter - 1)

    remote(panel.at[1], panel.at[1], 65, mate_sem.at[1], sibling).wait_send()

    def sent(s, shape, dtype):
        ref = same_size(shape, dtype)
        remote(ref, ref, s, x_sem, sibling).wait_send()

    groups = {}
    for when, s, shape, dtype in pending:
        if isinstance(when, tuple):
            groups.setdefault(when[0], {}).setdefault(when[1], []).append((s, shape, dtype))
        elif when is always:
            sent(s, shape, dtype)

    def sent_in_row(r):
        @pl.when(row == r)
        def _():
            for c, copies in groups[r].items():

                @pl.when(col == c)
                def _(copies=copies):
                    for copy in copies:
                        sent(*copy)

    @pl.when(y == 0)
    def _():
        for r in groups:
            if r < N_Z:
                sent_in_row(r)
        for when, s, shape, dtype in pending:
            if not isinstance(when, tuple) and when is not always and when is not relay:

                @pl.when(when)
                def _(s=s, shape=shape, dtype=dtype):
                    sent(s, shape, dtype)

    @pl.when(y != 0)
    def _():
        for r in groups:
            if r >= N_Z:
                sent_in_row(r)

        @pl.when(relay)
        def _():
            for when, s, shape, dtype in pending:
                if when is relay:
                    sent(s, shape, dtype)

    @pl.when(is_relay)
    def _():
        for k, waits in relay_waits.items():

            @pl.when((core == k % 2) & (z == (2 if k < 4 else 6)))
            def _(waits=waits):
                for wanted, s in waits:

                    @pl.when(wanted())
                    def _(s=s):
                        remote(relays.at[0], relays.at[0], s, x_sem, sibling).wait_send()


def body(lower, slab, inverses):
    row_blocks, _, order, _, _, _ = lower.shape
    width = slab.shape[3]
    vmem = pltpu.VMEM
    dma = pltpu.SemaphoreType.DMA
    scratch = [
        vmem((order, order), BF16),
        vmem((2, row_blocks // 2, order, order), BF16),
        vmem((order, order), F32),
        vmem((4, 2, order, order), BF16),
        vmem((5, order, order), BF16),
        vmem((order, width), F32),
        vmem((order, width), F32),
        vmem((order, width), BF16),
        vmem((4, order, width), BF16),
        vmem((4, order, width), F32),
        vmem((order, width), F32),
        vmem((4, order, width), F32),
        vmem((4, order, width), BF16),
        vmem((2, order, width), F32),
        vmem((2, order, width), BF16),
        vmem((2, order // 4, width), BF16),
        vmem((order, width), BF16),
        vmem((4, order, width), F32),
        vmem((3, order, width), BF16),
        vmem((3, order, width), BF16),
        dma((5,)),
        dma((72,)),
        dma,
        dma,
        dma,
        pltpu.SemaphoreType.REGULAR,
        dma((2,)),
        dma((4, 2, 4)),
        dma((5,)),
        dma((4,)),
        dma((4,)),
        dma((2,)),
        dma((3,)),
    ]
    result = pl.pallas_call(
        kernel,
        name="window_solve",
        out_shape=jax.ShapeDtypeStruct((order, width), F32),
        in_specs=[pl.BlockSpec(memory_space=pltpu.HBM)] * 3,
        out_specs=pl.BlockSpec(memory_space=pltpu.VMEM),
        scratch_shapes=scratch,
        compiler_params=pltpu.CompilerParams(
            collective_id=0, has_side_effects=True, vmem_limit_bytes=53 << 20
        ),
    )(
        lower.reshape(row_blocks // 2, 2, order, order),
        slab.reshape(row_blocks, order, width),
        inverses.reshape(order, order),
    )
    return result.reshape(1, 1, order, width)


def solution(mesh):
    in_specs = (
        P(None, "row", None, None, "col", None),
        P(None, "row", None, None),
        P(None, "col", None, None),
    )
    out_specs = P("col", "row", None, None)
    return jax.shard_map(body, mesh=mesh, in_specs=in_specs, out_specs=out_specs, check_vma=False)
```

```python
import jax
import jax.numpy as jnp
from jax import lax
from jax.experimental import pallas as pl
from jax.experimental.pallas import tpu as pltpu
from jax.sharding import PartitionSpec as P

MESH = pl.DeviceIdType.MESH
F32 = jnp.float32
BF16 = jnp.bfloat16

N_Z, N_Y, N_X = 8, 4, 4
SOLVE_0 = (0, 0)
SOLVE_1 = (1, 0)
SOLVE_23 = (2, 1)
SOLVE_47 = (6, 4)
HIGH = tuple((0, b) for b in range(4))
LOW = tuple((1, b) for b in range(4))
INVERSE_SENDS = (
    ((1, 1), SOLVE_1, 0, HIGH + LOW),
    ((9, 2), SOLVE_23, 0, (HIGH[0], HIGH[3])),
    ((25, 2), SOLVE_23, 0, (HIGH[1], HIGH[2])),
    ((12, 3), SOLVE_23, 1, (HIGH[0], HIGH[3])),
    ((28, 3), SOLVE_23, 1, (HIGH[1], HIGH[2])),
    ((6, 5), SOLVE_47, 1, HIGH),
    ((14, 6), SOLVE_47, 2, HIGH),
    ((30, 7), SOLVE_47, 3, HIGH),
)
BLOCK_SENDS = (
    ((3, 1), SOLVE_23, 0),
    ((3, 2), SOLVE_23, 1),
    ((5, 4), SOLVE_47, 0),
    ((6, 5), SOLVE_47, 1),
    ((7, 4), SOLVE_47, 2),
    ((7, 5), SOLVE_47, 3),
    ((7, 6), SOLVE_47, 4),
    *(((5, c), (4, c), 0) for c in (2, 3)),
    *(((6, c), (7, c), 0) for c in (2, 3)),
)


def special_pairs():
    pairs = {(s, t) for s, t, _, _ in INVERSE_SENDS} | {(s, t) for s, t, _ in BLOCK_SENDS}
    pairs |= {(SOLVE_0, (z, 0)) for z in (1, 2, 3)} | {(SOLVE_1, (z, 1)) for z in (0, 1, 2, 4, 5)}
    pairs |= {((r, 1), (4 if r < 6 else 7, 3)) for r in range(4, 8)}
    pairs |= {((3, 0), (4, 0)), ((0, 1), (5, 0))} | {((0, 1), (r, c)) for r in (6, 7) for c in (0, 1)}
    pairs |= {((3, 0), SOLVE_23)}
    pairs |= {(SOLVE_23, (r, c)) for c in (2, 3) for r in (4, 7)}
    pairs |= {(SOLVE_23, (2, c)) for c in range(8) if c != 1}
    pairs |= {(SOLVE_47, (6, c)) for c in range(8) if c != 4}
    pairs |= {((4, 3), (7, 3))} | {((r, 3), SOLVE_47) for r in (4, 7)} | {((r, 0), (r, 3)) for r in (4, 7)} | {((r, 1), (r, 3)) for r in (4, 7)}
    pairs |= {(SOLVE_47, (r, 0)) for r in range(4, 8)}
    return sorted({tuple(sorted(p)) for p in pairs})


def kernel(
    lower, slab, inverses, out,
    first, panel, inv, inv_parts, blocks, right, right_own, x_own, x_stage, x_full, x_in,
    acc_f, acc_b, stage_f, stage_b, relays, x_mate, ours, sums, cross_in,
    load_sem, send_sem, x_sem, x_in_sem, side_sem, go_sem, relay_sem, inv_sem, block_sem, acc_f_sem, acc_b_sem, mate_sem, cross_sem,
):
    row = lax.axis_index("row")
    col = lax.axis_index("col")
    y, z = row // N_Z, row % N_Z
    x, core = col // 2, col % 2
    half = first.shape[0] // 2
    quarter = half // 2
    width = x_own.shape[1]

    def here(device):
        return (row == device[0]) & (col == device[1])

    def plane_row(r0, r1):
        return (row >= r0) & (row < r1)

    root_z = col
    sibling = (row, col + 1 - 2 * core)
    pending = []
    relay_waits = {}

    def remote(src, dst, s, recv, device):
        return pltpu.make_async_remote_copy(
            src_ref=src, dst_ref=dst, send_sem=send_sem.at[s], recv_sem=recv, device_id=device, device_id_type=MESH
        )

    def send(when, src, dst, s, recv, device):
        remote(src, dst, s, recv, device).start()
        if when is not None:
            pending.append((when, s, src.shape, src.dtype))

    def arrived(dst, recv):
        remote(dst, dst, 0, recv, sibling).wait_recv()

    load_first = pltpu.make_async_copy(lower.at[0, 0], first, load_sem.at[0])
    load_ours = pltpu.make_async_copy(lower.at[:, core], panel.at[0], load_sem.at[1])
    load_inv = pltpu.make_async_copy(inverses, inv, load_sem.at[2])
    load_right = pltpu.make_async_copy(slab.at[0], right, load_sem.at[3])
    load_own = pltpu.make_async_copy(slab.at[col], right_own, load_sem.at[4])
    load_inv.start()
    load_right.start()
    load_first.start()

    def clear_slot(slot):
        inv_parts[slot] = jnp.zeros(inv_parts.shape[1:], BF16)

    @pl.when(here(SOLVE_1))
    def _():
        clear_slot(0)

    @pl.when(here(SOLVE_23))
    def _():
        clear_slot(0)
        clear_slot(1)

    @pl.when(here(SOLVE_47))
    def _():
        clear_slot(1)
        clear_slot(2)
        clear_slot(3)

    barrier = pltpu.get_barrier_semaphore()

    def greet(device):
        pl.semaphore_signal(barrier, inc=1, device_id=device, device_id_type=MESH)

    greet(sibling)
    for d in range(1, N_X):
        greet((row, (x + d) % N_X * 2 + core))
    count = jnp.int32(N_X)
    is_root = (z == root_z) & (col < 2)
    in_other = (col < 2) & (y != 0)

    @pl.when(is_root & in_other)
    def _():
        for d in range(1, N_Z):
            greet((y * N_Z + (z + d) % N_Z, col))

    @pl.when(jnp.logical_not(is_root) & in_other)
    def _():
        greet((y * N_Z + root_z, col))

    count += jnp.where(in_other, jnp.where(is_root, N_Z - 1, 1), 0)
    is_relay = (z == 2) | (z == 6)
    relay_z = jnp.where(col < 4, 2, 6)

    @pl.when(is_relay)
    def _():
        for k in range(2, 8):

            @pl.when((core == k % 2) & (z == (2 if k < 4 else 6)))
            def _(k=k):
                for d in range(1, N_Z):
                    greet((y * N_Z + (z + d) % N_Z, k))

                @pl.when(col != k)
                def _():
                    greet((row, k))

    count += jnp.where(z == 2, N_Z - 1 + jnp.where(x == 1, 0, 1), 0)
    count += jnp.where(z == 6, 2 * (N_Z - 1) + jnp.where(x >= 2, 1, 2), 0)

    @pl.when(col >= 2)
    def _():
        for q in range(N_X):

            @pl.when((z != relay_z) | (q != x))
            def _(q=q):
                greet((y * N_Z + relay_z, 2 * q + core))

    count += jnp.where(col >= 2, jnp.where(z == jnp.where(col < 4, 2, 6), N_X - 1, N_X), 0)
    in_line = is_root | is_relay

    @pl.when(in_line & (y == 0))
    def _():
        for d in range(1, N_Y):
            greet((d * N_Z + z, col))

    @pl.when(in_line & (y != 0))
    def _():
        greet((z, col))

    count += jnp.where(in_line, jnp.where(y == 0, N_Y - 1, 1), 0)
    partners = {}
    for a, b in special_pairs():
        partners.setdefault(a, []).append(b)
        partners.setdefault(b, []).append(a)
    by_row = {}
    for device, others in partners.items():
        count += jnp.where(here(device), len(others), 0)
        by_row.setdefault(device[0], []).append((device[1], others))

    def greet_row(r):
        @pl.when(row == r)
        def _():
            for c, others in by_row[r]:

                @pl.when(col == c)
                def _(others=others):
                    for other in others:
                        greet(other)

    @pl.when(y == 0)
    def _():
        for r in by_row:
            if r < N_Z:
                greet_row(r)

    @pl.when(y != 0)
    def _():
        for r in by_row:
            if r >= N_Z:
                greet_row(r)

    def split_inverse(slot):
        value = inv[...]
        high = value.astype(BF16)
        inv_parts[slot, 0] = high
        inv_parts[slot, 1] = (value - high.astype(F32)).astype(BF16)

    def part(slot, piece, b):
        return inv_parts.at[slot, piece, pl.ds(b * quarter, quarter), pl.ds(0, (b + 1) * quarter)]

    def inverse_arrived(slot, parts=HIGH):
        for piece, b in parts:
            arrived(part(slot, piece, b), inv_sem.at[slot, piece, b])

    def solve(slot, total, low_part=False):
        high = total.astype(BF16)
        low = (total - high.astype(F32)).astype(BF16)
        both = jnp.concatenate([high, low], axis=1)

        whole = product(inv_parts[slot, 0], both)
        if low_part:
            whole += product(inv_parts[slot, 1], both)
        return whole[:, :width] + whole[:, width:]

    def product(block, value):
        return jnp.dot(block, value, preferred_element_type=F32)

    is_source = here(INVERSE_SENDS[0][0])
    for source, _, _, _ in INVERSE_SENDS[1:]:
        is_source |= here(source)

    @pl.when(is_source)
    def _():
        load_inv.wait()
        split_inverse(0)

    @pl.when(here(SOLVE_0))
    def _():
        load_inv.wait()
        split_inverse(0)
        load_right.wait()
        value = solve(0, right[...], low_part=True)
        x_own[...] = value.astype(BF16)
        x_full[0] = value

    pl.semaphore_wait(barrier, count)

    load_ours.start()
    load_own.start()

    for source, solver, slot in BLOCK_SENDS:

        @pl.when(here(source))
        def _(source=source, solver=solver, slot=slot):
            send(source, lower.at[0, 0], blocks.at[slot], 0, block_sem.at[slot], solver)

    for source, solver, slot, pieces in INVERSE_SENDS:

        @pl.when(here(source))
        def _(source=source, solver=solver, slot=slot, pieces=pieces):
            for piece, b in pieces:
                s = 1 + piece * 4 + b
                send(source, part(0, piece, b), part(slot, piece, b), s, inv_sem.at[slot, piece, b], solver)

    remote(lower.at[:, 1 - core], panel.at[1], 65, mate_sem.at[1], sibling).start()

    column_root = [SOLVE_0, (1, 1)]
    in_plane = [(1, 3, 2), ()]

    def spread_from_root(c):
        when = column_root[c]
        root_row = column_root[c][0]
        for i, target in enumerate(in_plane[c][:1]):
            send(when, x_own, x_own, 9 + i, x_sem, (target, c))
        if c == 0:
            send(when, x_own, x_stage.at[0], 19, side_sem, (0, 1))
        for d in (2, 1, 3):
            send(when, x_own, x_own, 15 + d, x_sem, (d * N_Z + root_row, c))
        for i, target in enumerate(in_plane[c]):
            if i > 0:
                send(when, x_own, x_own, 9 + i, x_sem, (target, c))

    @pl.when(here(SOLVE_0))
    def _():
        spread_from_root(0)

    @pl.when(here(SOLVE_1))
    def _():
        load_right.wait()
        load_first.wait()
        inverse_arrived(0, HIGH + LOW)
        arrived(x_own, x_sem)
        value = solve(0, right[...] - product(first[...], x_own[...]), low_part=True)
        x_stage[0] = value.astype(BF16)
        x_full[0] = value
        send(SOLVE_1, x_stage.at[0], x_own, 9, x_sem, (2, 1))
        send(SOLVE_1, x_stage.at[0], x_own, 10, x_sem, (4, 1))
        for i, target in enumerate((5, 0, 1)):
            send(SOLVE_1, x_stage.at[0], x_own, 11 + i, x_sem, (target, 1))

    def rows_of(c, r0, r1):
        return plane_row(r0, r1) & (col == c)

    @pl.when(here((2, 0)))
    def _():
        load_first.wait()
        arrived(x_own, x_sem)
        stage_f[0] = product(first[...], x_own[...])
        send((2, 0), stage_f.at[0], acc_f.at[0], 19, acc_f_sem.at[0], sibling)

    @pl.when(here((3, 0)))
    def _():
        load_right.wait()
        load_first.wait()
        arrived(x_own, x_sem)
        stage_b[0] = (right[...] - product(first[...], x_own[...])).astype(BF16)
        send((3, 0), stage_b.at[0], acc_b.at[0], 19, acc_b_sem.at[0], SOLVE_23)
        send((3, 0), x_own, x_own, 9, x_sem, (4, 0))

    @pl.when(here((0, 1)))
    def _():
        arrived(x_stage.at[0], side_sem)
        for i, r in enumerate((5, 6, 7)):
            send((0, 1), x_stage.at[0], x_own, 9 + i, x_sem, (r, 0))
        arrived(x_own, x_sem)
        for i, r in enumerate((6, 7)):
            send((0, 1), x_own, x_own, 12 + i, x_sem, (r, 1))

    low_0 = rows_of(0, 4, 8)
    low_1 = rows_of(1, 4, 8)

    @pl.when(low_0)
    def _():
        load_first.wait()
        arrived(x_own, x_sem)
        stage_f[0] = product(first[...], x_own[...])
        send(low_0, stage_f.at[0], acc_f.at[0], 18, acc_f_sem.at[0], sibling)

    @pl.when(low_1)
    def _():
        load_first.wait()
        arrived(x_own, x_sem)
        load_right.wait()
        arrived(acc_f.at[0], acc_f_sem.at[0])
        stage_b[0] = (right[...] - acc_f[0] - product(first[...], x_own[...])).astype(BF16)

    for r, target, slot in ((4, 4, 0), (5, 4, 1), (6, 7, 1), (7, 7, 0)):

        @pl.when(here((r, 1)))
        def _(r=r, target=target, slot=slot):
            send((r, 1), stage_b.at[0], acc_b.at[slot], 19, acc_b_sem.at[slot], (target, 3))

    def scatter(when, slot, k, s):
        solver = SOLVE_23 if k < 4 else SOLVE_47
        for q in range(N_X):
            device = (solver[0], 2 * q + k % 2)
            if device != solver:
                rows = pl.ds(q * quarter, quarter)
                send(when, x_stage.at[slot, rows], relays.at[max(k // 2 - 2, 0)], s + q, relay_sem.at[max(k // 2 - 2, 0)], device)

    own_rows = pl.ds(pl.multiple_of(x * quarter, quarter), quarter)
    other_planes = [(d * N_Z + z, col) for d in range(1, N_Y)]
    other_z = [y * N_Z + (z + d) % N_Z for d in (2, 3, 4, 5, 1, 6, 7)]

    def relay_quarter(k):
        solver = SOLVE_23 if k < 4 else SOLVE_47
        slot = max(k // 2 - 2, 0)
        piece = relays.at[slot]
        base = 40 + 12 * slot
        waits = relay_waits.setdefault(k, [])

        place = lambda: (z == solver[0]) & (core == k % 2)

        @pl.when(place())
        def _():
            @pl.when(here(solver))
            def _():
                q = solver[1] // 2
                relays[slot] = x_stage[k - 2 if k < 4 else k - 4, q * quarter : (q + 1) * quarter]

            @pl.when(jnp.logical_not(here(solver)))
            def _():
                arrived(piece, relay_sem.at[slot])

            @pl.when(y == 0)
            def _():
                for i, device in enumerate(other_planes):
                    send(None, piece, piece, base + i, relay_sem.at[slot], device)
                    waits.append((lambda: y == 0, base + i))

            for i, target in enumerate(other_z):
                direct = (lambda target=target: (y != 0) | ((target != 4) & (target != 7))) if k < 4 else (lambda: True)

                @pl.when(direct())
                def _(i=i, target=target, direct=direct):
                    waits.append((direct, base + 3 + i))
                    send(None, piece, x_own.at[own_rows], base + 3 + i, x_sem, (target, k))

            @pl.when(col == k)
            def _():
                x_own[own_rows] = relays[slot]

            @pl.when(col != k)
            def _():
                waits.append((lambda: col != k, base + 10))
                send(None, piece, x_own.at[own_rows], base + 10, x_sem, (row, k))

    @pl.when(here(SOLVE_23))
    def _():
        when = SOLVE_23
        load_right.wait()
        load_first.wait()
        arrived(acc_f.at[0], acc_f_sem.at[0])
        arrived(x_own, x_sem)
        total = right[...] - acc_f[0] - product(first[...], x_own[...])
        inverse_arrived(0)
        value = solve(0, total)
        x_stage[0] = value.astype(BF16)
        x_full[0] = value
        for i, r in enumerate((4, 7)):
            send(when, x_stage.at[0], x_own, 20 + i, x_sem, (r, 2))
        scatter(when, 0, 2, 26)
        for slot in range(2):
            arrived(blocks.at[slot], block_sem.at[slot])
        arrived(acc_b.at[0], acc_b_sem.at[0])
        total = acc_b[0].astype(F32) - (product(blocks[0], x_own[...]) + product(blocks[1], x_stage[0]))
        inverse_arrived(1)
        value = solve(1, total)
        x_stage[1] = value.astype(BF16)
        x_full[1] = value
        for i, r in enumerate((4, 7)):
            send(when, x_stage.at[1], x_own, 23 + i, x_sem, (r, 3))
        scatter(when, 1, 3, 29)
        send(when, x_own, x_own, 33, x_sem, (3, 1))

    low_rows = (row == 4) | (row == 7)
    low_2 = low_rows & (col == 2)

    @pl.when(low_2)
    def _():
        load_first.wait()
        arrived(x_own, x_sem)
        stage_f[0] = product(first[...], x_own[...])
        send(low_2, stage_f.at[0], acc_f.at[0], 18, acc_f_sem.at[0], sibling)
        arrived(blocks.at[0], block_sem.at[0])
        stage_f[1] = product(blocks[0], x_own[...])
        send(low_2, stage_f.at[1], acc_f.at[1], 19, acc_f_sem.at[1], sibling)

    for r, rows in ((4, (4, 5)), (7, (6, 7))):

        @pl.when(here((r, 3)))
        def _(r=r, rows=rows):
            load_first.wait()
            for i, target in enumerate(rows):
                j = 0 if target == r else 1
                if j == 1:
                    arrived(blocks.at[0], block_sem.at[0])
                arrived(acc_b.at[j], acc_b_sem.at[j])
                arrived(acc_f.at[j], acc_f_sem.at[j])
                stage_f[j] = acc_b[j].astype(F32) - acc_f[j]
                if i == 0:
                    arrived(x_own, x_sem)
                    for c in (0, 1):
                        pl.semaphore_signal(go_sem, inc=1, device_id=(r, c), device_id_type=MESH)
                block = first[...] if target == r else blocks[0]
                stage_b[i] = (stage_f[j] - product(block, x_own[...])).astype(BF16)
                send((r, 3), stage_b.at[i], acc_b.at[target - 4], 18 + i, acc_b_sem.at[target - 4], SOLVE_47)

    @pl.when(here(SOLVE_47))
    def _():
        when = SOLVE_47
        load_inv.wait()
        split_inverse(0)
        load_first.wait()
        load_right.wait()
        place = {(1, 0): blocks.at[0], (2, 0): first, (2, 1): blocks.at[1]}
        place |= {(3, 0): blocks.at[2], (3, 1): blocks.at[3], (3, 2): blocks.at[4]}
        for slot in range(5):
            arrived(blocks.at[slot], block_sem.at[slot])
        for slot in range(1, 4):
            inverse_arrived(slot)
        for q in range(4):
            arrived(acc_b.at[q], acc_b_sem.at[q])
            total = acc_b[q].astype(F32)
            if q > 0:
                total -= acc_f[q]
            value = solve(q, total)
            x_stage[q] = value.astype(BF16)
            x_full[q] = value
            scatter(when, q, 4 + q, 20 + 4 * q)
            if q < 2:
                send(when, x_full.at[q], x_in, 36 + q, x_in_sem, (4 + q, 0))
            for r in range(q + 1, 4):
                done = product(place[r, q][...], x_stage[q])
                acc_f[r] = done if q == 0 else acc_f[r] + done
        send(when, x_full.at[2], x_in, 38, x_in_sem, (6, 0))
    for k in range(2, 8):
        relay_quarter(k)

    waited = rows_of(0, 0, 8) | here((0, 1)) | low_1 | (low_rows & (col < 4)) | here(SOLVE_23)

    @pl.when(jnp.logical_not(waited) & (col < 2))
    def _():
        arrived(x_own, x_sem)

    @pl.when(jnp.logical_not(waited) & (col >= 2))
    def _():
        @pl.when(z != relay_z)
        def _():
            arrived(x_own, x_sem)

        @pl.when(z == relay_z)
        def _():
            arrived(x_own.at[pl.ds(0, 3 * quarter)], x_sem)

    @pl.when(here(column_root[1]))
    def _():
        spread_from_root(1)

    relay = is_root & (y != 0)
    peers = [(i, (y * N_Z + (z + d) % N_Z, col)) for i, d in enumerate((4, 3, 5, 2, 6, 1, 7))]

    @pl.when(relay)
    def _():
        for i, peer in peers:
            send(relay, x_own, x_own, 9 + i, x_sem, peer)

    always = row >= 0
    waited_first = rows_of(0, 2, 8) | low_1 | (low_rows & (col < 4))
    waited_first = waited_first | here(SOLVE_1) | here(SOLVE_23) | here(SOLVE_47)

    @pl.when(jnp.logical_not(waited_first))
    def _():
        load_first.wait()

    send(always, x_own, x_mate, 64, mate_sem.at[0], sibling)
    load_ours.wait()
    half_panel = panel[0].reshape(4 * 2 * half, 2 * half)
    ours[...] = product(half_panel, x_own[...]).reshape(4, 2 * half, width)
    arrived(panel.at[1], mate_sem.at[1])
    arrived(x_mate, mate_sem.at[0])

    @pl.when(low_rows & (col < 2))
    def _():
        pl.semaphore_wait(go_sem, 1)

    value = x_mate[...]
    for j, d in enumerate((2, 1, 3, 0)):
        owner = (x + d) % N_X
        total = ours[owner] + product(panel[1, owner], value)
        if d > 0:
            sums[j] = total.astype(BF16)
            send(always, sums.at[j], cross_in.at[d - 1], 68 + j, cross_sem.at[d - 1], (row, owner * 2 + core))
    @pl.when(here(SOLVE_23))
    def _():
        for q in range(2):
            send(SOLVE_23, x_full.at[q], x_in, 36 + q, x_in_sem, (2 + q, 0))

    @pl.when(here(SOLVE_47))
    def _():
        send(SOLVE_47, x_full.at[3], x_in, 39, x_in_sem, (7, 0))

    load_own.wait()
    total = right_own[...] - total
    for d in range(3):
        arrived(cross_in.at[d], cross_sem.at[d])
        total -= cross_in[d].astype(F32)
    out[...] = total

    solved = plane_row(0, 8) & (col == 0)

    @pl.when(solved & (row < 2))
    def _():
        out[...] = x_full[0]

    @pl.when(solved & (row >= 2))
    def _():
        arrived(x_in, x_in_sem)
        out[...] = x_in[...]

    @pl.when(jnp.logical_not(is_source | here(SOLVE_0) | here(SOLVE_47)))
    def _():
        load_inv.wait()

    read_right = here((3, 0)) | here(SOLVE_0) | here(SOLVE_1) | here(SOLVE_23) | here(SOLVE_47) | low_1

    @pl.when(jnp.logical_not(read_right))
    def _():
        load_right.wait()

    buffers = [x_own, stage_f.at[0], relays.at[0]]

    def same_size(shape, dtype):
        for buffer in buffers:
            if buffer.shape == shape and buffer.dtype == dtype:
                return buffer
        if shape == first.shape:
            return first
        return part(0, 0, shape[1] // quarter - 1)

    remote(panel.at[1], panel.at[1], 65, mate_sem.at[1], sibling).wait_send()

    def sent(s, shape, dtype):
        ref = same_size(shape, dtype)
        remote(ref, ref, s, x_sem, sibling).wait_send()

    groups = {}
    for when, s, shape, dtype in pending:
        if isinstance(when, tuple):
            groups.setdefault(when[0], {}).setdefault(when[1], []).append((s, shape, dtype))
        elif when is always:
            sent(s, shape, dtype)

    def sent_in_row(r):
        @pl.when(row == r)
        def _():
            for c, copies in groups[r].items():

                @pl.when(col == c)
                def _(copies=copies):
                    for copy in copies:
                        sent(*copy)

    @pl.when(y == 0)
    def _():
        for r in groups:
            if r < N_Z:
                sent_in_row(r)
        for when, s, shape, dtype in pending:
            if not isinstance(when, tuple) and when is not always and when is not relay:

                @pl.when(when)
                def _(s=s, shape=shape, dtype=dtype):
                    sent(s, shape, dtype)

    @pl.when(y != 0)
    def _():
        for r in groups:
            if r >= N_Z:
                sent_in_row(r)

        @pl.when(relay)
        def _():
            for when, s, shape, dtype in pending:
                if when is relay:
                    sent(s, shape, dtype)

    @pl.when(is_relay)
    def _():
        for k, waits in relay_waits.items():

            @pl.when((core == k % 2) & (z == (2 if k < 4 else 6)))
            def _(waits=waits):
                for wanted, s in waits:

                    @pl.when(wanted())
                    def _(s=s):
                        remote(relays.at[0], relays.at[0], s, x_sem, sibling).wait_send()


def body(lower, slab, inverses):
    row_blocks, _, order, _, _, _ = lower.shape
    width = slab.shape[3]
    vmem = pltpu.VMEM
    dma = pltpu.SemaphoreType.DMA
    scratch = [
        vmem((order, order), BF16),
        vmem((2, row_blocks // 2, order, order), BF16),
        vmem((order, order), F32),
        vmem((4, 2, order, order), BF16),
        vmem((5, order, order), BF16),
        vmem((order, width), F32),
        vmem((order, width), F32),
        vmem((order, width), BF16),
        vmem((4, order, width), BF16),
        vmem((4, order, width), F32),
        vmem((order, width), F32),
        vmem((4, order, width), F32),
        vmem((4, order, width), BF16),
        vmem((2, order, width), F32),
        vmem((2, order, width), BF16),
        vmem((2, order // 4, width), BF16),
        vmem((order, width), BF16),
        vmem((4, order, width), F32),
        vmem((3, order, width), BF16),
        vmem((3, order, width), BF16),
        dma((5,)),
        dma((72,)),
        dma,
        dma,
        dma,
        pltpu.SemaphoreType.REGULAR,
        dma((2,)),
        dma((4, 2, 4)),
        dma((5,)),
        dma((4,)),
        dma((4,)),
        dma((2,)),
        dma((3,)),
    ]
    result = pl.pallas_call(
        kernel,
        name="window_solve",
        out_shape=jax.ShapeDtypeStruct((order, width), F32),
        in_specs=[pl.BlockSpec(memory_space=pltpu.HBM)] * 3,
        out_specs=pl.BlockSpec(memory_space=pltpu.VMEM),
        scratch_shapes=scratch,
        compiler_params=pltpu.CompilerParams(
            collective_id=0, has_side_effects=True, vmem_limit_bytes=53 << 20
        ),
    )(
        lower.reshape(row_blocks // 2, 2, order, order),
        slab.reshape(row_blocks, order, width),
        inverses.reshape(order, order),
    )
    return result.reshape(1, 1, order, width)


def solution(mesh):
    in_specs = (
        P(None, "row", None, None, "col", None),
        P(None, "row", None, None),
        P(None, "col", None, None),
    )
    out_specs = P("col", "row", None, None)
    return jax.shard_map(body, mesh=mesh, in_specs=in_specs, out_specs=out_specs, check_vma=False)
```

```python
import jax
import jax.numpy as jnp
from jax import lax
from jax.experimental import pallas as pl
from jax.experimental.pallas import tpu as pltpu
from jax.sharding import PartitionSpec as P

MESH = pl.DeviceIdType.MESH
F32 = jnp.float32
BF16 = jnp.bfloat16

N_Z, N_Y, N_X = 8, 4, 4
SOLVE_0 = (0, 0)
SOLVE_1 = (1, 0)
SOLVE_23 = (2, 1)
SOLVE_47 = (6, 4)
HIGH = tuple((0, b) for b in range(4))
LOW = tuple((1, b) for b in range(4))
INVERSE_SENDS = (
    ((1, 1), SOLVE_1, 0, HIGH + LOW),
    ((9, 2), SOLVE_23, 0, (HIGH[0], HIGH[3])),
    ((25, 2), SOLVE_23, 0, (HIGH[1], HIGH[2])),
    ((12, 3), SOLVE_23, 1, (HIGH[0], HIGH[3])),
    ((28, 3), SOLVE_23, 1, (HIGH[1], HIGH[2])),
    ((6, 5), SOLVE_47, 1, HIGH),
    ((14, 6), SOLVE_47, 2, HIGH),
    ((30, 7), SOLVE_47, 3, HIGH),
)
BLOCK_SENDS = (
    ((3, 1), SOLVE_23, 0),
    ((3, 2), SOLVE_23, 1),
    ((5, 4), SOLVE_47, 0),
    ((6, 5), SOLVE_47, 1),
    ((7, 4), SOLVE_47, 2),
    ((7, 5), SOLVE_47, 3),
    ((7, 6), SOLVE_47, 4),
    *(((5, c), (4, c), 0) for c in (2, 3)),
    *(((6, c), (7, c), 0) for c in (2, 3)),
)


def special_pairs():
    pairs = {(s, t) for s, t, _, _ in INVERSE_SENDS} | {(s, t) for s, t, _ in BLOCK_SENDS}
    pairs |= {(SOLVE_0, (z, 0)) for z in (1, 2, 3)} | {(SOLVE_1, (z, 1)) for z in (0, 1, 2, 4, 5)}
    pairs |= {((r, 1), (4 if r < 6 else 7, 3)) for r in range(4, 8)}
    pairs |= {((3, 0), (4, 0)), ((0, 1), (5, 0))} | {((0, 1), (r, c)) for r in (6, 7) for c in (0, 1)}
    pairs |= {((3, 0), SOLVE_23)}
    pairs |= {(SOLVE_23, (r, c)) for c in (2, 3) for r in (4, 7)}
    pairs |= {(SOLVE_23, (2, c)) for c in range(8) if c != 1}
    pairs |= {(SOLVE_47, (6, c)) for c in range(8) if c != 4}
    pairs |= {((4, 3), (7, 3))} | {((r, 3), SOLVE_47) for r in (4, 7)} | {((r, 0), (r, 3)) for r in (4, 7)} | {((r, 1), (r, 3)) for r in (4, 7)}
    pairs |= {(SOLVE_47, (r, 0)) for r in range(4, 8)}
    return sorted({tuple(sorted(p)) for p in pairs})


def kernel(
    lower, slab, inverses, out,
    first, panel, inv, inv_parts, blocks, right, right_own, x_own, x_stage, x_full, x_in,
    acc_f, acc_b, stage_f, stage_b, relays, x_mate, ours, sums, cross_in,
    load_sem, send_sem, x_sem, x_in_sem, side_sem, go_sem, relay_sem, inv_sem, block_sem, acc_f_sem, acc_b_sem, mate_sem, cross_sem,
):
    row = lax.axis_index("row")
    col = lax.axis_index("col")
    y, z = row // N_Z, row % N_Z
    x, core = col // 2, col % 2
    half = first.shape[0] // 2
    quarter = half // 2
    width = x_own.shape[1]

    def here(device):
        return (row == device[0]) & (col == device[1])

    def plane_row(r0, r1):
        return (row >= r0) & (row < r1)

    root_z = col
    sibling = (row, col + 1 - 2 * core)
    pending = []
    relay_waits = {}

    def remote(src, dst, s, recv, device):
        return pltpu.make_async_remote_copy(
            src_ref=src, dst_ref=dst, send_sem=send_sem.at[s], recv_sem=recv, device_id=device, device_id_type=MESH
        )

    def send(when, src, dst, s, recv, device):
        remote(src, dst, s, recv, device).start()
        if when is not None:
            pending.append((when, s, src.shape, src.dtype))

    def arrived(dst, recv):
        remote(dst, dst, 0, recv, sibling).wait_recv()

    load_first = pltpu.make_async_copy(lower.at[0, 0], first, load_sem.at[0])
    load_ours = pltpu.make_async_copy(lower.at[:, core], panel.at[0], load_sem.at[1])
    load_inv = pltpu.make_async_copy(inverses, inv, load_sem.at[2])
    load_right = pltpu.make_async_copy(slab.at[0], right, load_sem.at[3])
    load_own = pltpu.make_async_copy(slab.at[col], right_own, load_sem.at[4])
    load_inv.start()
    load_right.start()
    load_first.start()

    def clear_slot(slot):
        inv_parts[slot] = jnp.zeros(inv_parts.shape[1:], BF16)

    @pl.when(here(SOLVE_1))
    def _():
        clear_slot(0)

    @pl.when(here(SOLVE_23))
    def _():
        clear_slot(0)
        clear_slot(1)

    @pl.when(here(SOLVE_47))
    def _():
        clear_slot(1)
        clear_slot(2)
        clear_slot(3)

    barrier = pltpu.get_barrier_semaphore()

    def greet(device):
        pl.semaphore_signal(barrier, inc=1, device_id=device, device_id_type=MESH)

    count = jnp.int32(0)
    partners = {}
    for a, b in special_pairs():
        partners.setdefault(a, []).append(b)
        partners.setdefault(b, []).append(a)
    by_row = {}
    for device, others in partners.items():
        count += jnp.where(here(device), len(others), 0)
        by_row.setdefault(device[0], []).append((device[1], others))

    def greet_row(r):
        @pl.when(row == r)
        def _():
            for c, others in by_row[r]:

                @pl.when(col == c)
                def _(others=others):
                    for other in others:
                        greet(other)

    @pl.when(y == 0)
    def _():
        for r in by_row:
            if r < N_Z:
                greet_row(r)

    @pl.when(y != 0)
    def _():
        for r in by_row:
            if r >= N_Z:
                greet_row(r)

    greet(sibling)
    for d in range(1, N_X):
        greet((row, (x + d) % N_X * 2 + core))
    count += N_X
    is_root = (z == root_z) & (col < 2)
    in_other = (col < 2) & (y != 0)

    @pl.when(is_root & in_other)
    def _():
        for d in range(1, N_Z):
            greet((y * N_Z + (z + d) % N_Z, col))

    @pl.when(jnp.logical_not(is_root) & in_other)
    def _():
        greet((y * N_Z + root_z, col))

    count += jnp.where(in_other, jnp.where(is_root, N_Z - 1, 1), 0)
    is_relay = (z == 2) | (z == 6)
    relay_z = jnp.where(col < 4, 2, 6)

    @pl.when(is_relay)
    def _():
        for k in range(2, 8):

            @pl.when((core == k % 2) & (z == (2 if k < 4 else 6)))
            def _(k=k):
                for d in range(1, N_Z):
                    greet((y * N_Z + (z + d) % N_Z, k))

                @pl.when(col != k)
                def _():
                    greet((row, k))

    count += jnp.where(z == 2, N_Z - 1 + jnp.where(x == 1, 0, 1), 0)
    count += jnp.where(z == 6, 2 * (N_Z - 1) + jnp.where(x >= 2, 1, 2), 0)

    @pl.when(col >= 2)
    def _():
        for q in range(N_X):

            @pl.when((z != relay_z) | (q != x))
            def _(q=q):
                greet((y * N_Z + relay_z, 2 * q + core))

    count += jnp.where(col >= 2, jnp.where(z == jnp.where(col < 4, 2, 6), N_X - 1, N_X), 0)
    in_line = is_root | is_relay

    @pl.when(in_line & (y == 0))
    def _():
        for d in range(1, N_Y):
            greet((d * N_Z + z, col))

    @pl.when(in_line & (y != 0))
    def _():
        greet((z, col))

    count += jnp.where(in_line, jnp.where(y == 0, N_Y - 1, 1), 0)
    def split_inverse(slot):
        value = inv[...]
        high = value.astype(BF16)
        inv_parts[slot, 0] = high
        inv_parts[slot, 1] = (value - high.astype(F32)).astype(BF16)

    def part(slot, piece, b):
        return inv_parts.at[slot, piece, pl.ds(b * quarter, quarter), pl.ds(0, (b + 1) * quarter)]

    def inverse_arrived(slot, parts=HIGH):
        for piece, b in parts:
            arrived(part(slot, piece, b), inv_sem.at[slot, piece, b])

    def solve(slot, total, low_part=False):
        high = total.astype(BF16)
        low = (total - high.astype(F32)).astype(BF16)
        both = jnp.concatenate([high, low], axis=1)

        whole = product(inv_parts[slot, 0], both)
        if low_part:
            whole += product(inv_parts[slot, 1], both)
        return whole[:, :width] + whole[:, width:]

    def product(block, value):
        return jnp.dot(block, value, preferred_element_type=F32)

    is_source = here(INVERSE_SENDS[0][0])
    for source, _, _, _ in INVERSE_SENDS[1:]:
        is_source |= here(source)

    @pl.when(is_source)
    def _():
        load_inv.wait()
        split_inverse(0)

    @pl.when(here(SOLVE_0))
    def _():
        load_inv.wait()
        split_inverse(0)
        load_right.wait()
        value = solve(0, right[...], low_part=True)
        x_own[...] = value.astype(BF16)
        x_full[0] = value

    pl.semaphore_wait(barrier, count)

    load_ours.start()
    load_own.start()

    for source, solver, slot in BLOCK_SENDS:

        @pl.when(here(source))
        def _(source=source, solver=solver, slot=slot):
            send(source, lower.at[0, 0], blocks.at[slot], 0, block_sem.at[slot], solver)

    for source, solver, slot, pieces in INVERSE_SENDS:

        @pl.when(here(source))
        def _(source=source, solver=solver, slot=slot, pieces=pieces):
            for piece, b in pieces:
                s = 1 + piece * 4 + b
                send(source, part(0, piece, b), part(slot, piece, b), s, inv_sem.at[slot, piece, b], solver)

    remote(lower.at[:, 1 - core], panel.at[1], 65, mate_sem.at[1], sibling).start()

    column_root = [SOLVE_0, (1, 1)]
    in_plane = [(1, 3, 2), ()]

    def spread_from_root(c):
        when = column_root[c]
        root_row = column_root[c][0]
        for i, target in enumerate(in_plane[c][:1]):
            send(when, x_own, x_own, 9 + i, x_sem, (target, c))
        if c == 0:
            send(when, x_own, x_stage.at[0], 19, side_sem, (0, 1))
        for i, target in enumerate(in_plane[c]):
            if i > 0:
                send(when, x_own, x_own, 9 + i, x_sem, (target, c))
        for d in (2, 1, 3):
            send(when, x_own, x_own, 15 + d, x_sem, (d * N_Z + root_row, c))

    @pl.when(here(SOLVE_0))
    def _():
        spread_from_root(0)

    @pl.when(here(SOLVE_1))
    def _():
        load_right.wait()
        load_first.wait()
        inverse_arrived(0, HIGH + LOW)
        arrived(x_own, x_sem)
        value = solve(0, right[...] - product(first[...], x_own[...]), low_part=True)
        x_stage[0] = value.astype(BF16)
        x_full[0] = value
        send(SOLVE_1, x_stage.at[0], x_own, 9, x_sem, (2, 1))
        send(SOLVE_1, x_stage.at[0], x_own, 10, x_sem, (4, 1))
        for i, target in enumerate((5, 0, 1)):
            send(SOLVE_1, x_stage.at[0], x_own, 11 + i, x_sem, (target, 1))

    def rows_of(c, r0, r1):
        return plane_row(r0, r1) & (col == c)

    @pl.when(here((2, 0)))
    def _():
        load_first.wait()
        arrived(x_own, x_sem)
        stage_f[0] = product(first[...], x_own[...])
        send((2, 0), stage_f.at[0], acc_f.at[0], 19, acc_f_sem.at[0], sibling)

    @pl.when(here((3, 0)))
    def _():
        load_right.wait()
        load_first.wait()
        arrived(x_own, x_sem)
        stage_b[0] = (right[...] - product(first[...], x_own[...])).astype(BF16)
        send((3, 0), stage_b.at[0], acc_b.at[0], 19, acc_b_sem.at[0], SOLVE_23)
        send((3, 0), x_own, x_own, 9, x_sem, (4, 0))

    @pl.when(here((0, 1)))
    def _():
        arrived(x_stage.at[0], side_sem)
        for i, r in enumerate((5, 6, 7)):
            send((0, 1), x_stage.at[0], x_own, 9 + i, x_sem, (r, 0))
        arrived(x_own, x_sem)
        for i, r in enumerate((6, 7)):
            send((0, 1), x_own, x_own, 12 + i, x_sem, (r, 1))

    low_0 = rows_of(0, 4, 8)
    low_1 = rows_of(1, 4, 8)

    @pl.when(low_0)
    def _():
        load_first.wait()
        arrived(x_own, x_sem)
        stage_f[0] = product(first[...], x_own[...])
        send(low_0, stage_f.at[0], acc_f.at[0], 18, acc_f_sem.at[0], sibling)

    @pl.when(low_1)
    def _():
        load_first.wait()
        arrived(x_own, x_sem)
        load_right.wait()
        arrived(acc_f.at[0], acc_f_sem.at[0])
        stage_b[0] = (right[...] - acc_f[0] - product(first[...], x_own[...])).astype(BF16)

    for r, target, slot in ((4, 4, 0), (5, 4, 1), (6, 7, 1), (7, 7, 0)):

        @pl.when(here((r, 1)))
        def _(r=r, target=target, slot=slot):
            send((r, 1), stage_b.at[0], acc_b.at[slot], 19, acc_b_sem.at[slot], (target, 3))

    def scatter(when, slot, k, s):
        solver = SOLVE_23 if k < 4 else SOLVE_47
        for q in range(N_X):
            device = (solver[0], 2 * q + k % 2)
            if device != solver:
                rows = pl.ds(q * quarter, quarter)
                send(when, x_stage.at[slot, rows], relays.at[max(k // 2 - 2, 0)], s + q, relay_sem.at[max(k // 2 - 2, 0)], device)

    own_rows = pl.ds(pl.multiple_of(x * quarter, quarter), quarter)
    other_planes = [(d * N_Z + z, col) for d in range(1, N_Y)]
    other_z = [y * N_Z + (z + d) % N_Z for d in (2, 3, 4, 5, 1, 6, 7)]

    def relay_quarter(k):
        solver = SOLVE_23 if k < 4 else SOLVE_47
        slot = max(k // 2 - 2, 0)
        piece = relays.at[slot]
        base = 40 + 12 * slot
        waits = relay_waits.setdefault(k, [])

        place = lambda: (z == solver[0]) & (core == k % 2)

        @pl.when(place())
        def _():
            @pl.when(here(solver))
            def _():
                q = solver[1] // 2
                relays[slot] = x_stage[k - 2 if k < 4 else k - 4, q * quarter : (q + 1) * quarter]

            @pl.when(jnp.logical_not(here(solver)))
            def _():
                arrived(piece, relay_sem.at[slot])

            @pl.when(y == 0)
            def _():
                for i, device in enumerate(other_planes):
                    send(None, piece, piece, base + i, relay_sem.at[slot], device)
                    waits.append((lambda: y == 0, base + i))

            for i, target in enumerate(other_z):
                direct = (lambda target=target: (y != 0) | ((target != 4) & (target != 7))) if k < 4 else (lambda: True)

                @pl.when(direct())
                def _(i=i, target=target, direct=direct):
                    waits.append((direct, base + 3 + i))
                    send(None, piece, x_own.at[own_rows], base + 3 + i, x_sem, (target, k))

            @pl.when(col == k)
            def _():
                x_own[own_rows] = relays[slot]

            @pl.when(col != k)
            def _():
                waits.append((lambda: col != k, base + 10))
                send(None, piece, x_own.at[own_rows], base + 10, x_sem, (row, k))

    @pl.when(here(SOLVE_23))
    def _():
        when = SOLVE_23
        load_right.wait()
        load_first.wait()
        arrived(acc_f.at[0], acc_f_sem.at[0])
        arrived(x_own, x_sem)
        total = right[...] - acc_f[0] - product(first[...], x_own[...])
        inverse_arrived(0)
        value = solve(0, total)
        x_stage[0] = value.astype(BF16)
        x_full[0] = value
        for i, r in enumerate((4, 7)):
            send(when, x_stage.at[0], x_own, 20 + i, x_sem, (r, 2))
        scatter(when, 0, 2, 26)
        for slot in range(2):
            arrived(blocks.at[slot], block_sem.at[slot])
        arrived(acc_b.at[0], acc_b_sem.at[0])
        total = acc_b[0].astype(F32) - (product(blocks[0], x_own[...]) + product(blocks[1], x_stage[0]))
        inverse_arrived(1)
        value = solve(1, total)
        x_stage[1] = value.astype(BF16)
        x_full[1] = value
        for i, r in enumerate((4, 7)):
            send(when, x_stage.at[1], x_own, 23 + i, x_sem, (r, 3))
        scatter(when, 1, 3, 29)
        send(when, x_own, x_own, 33, x_sem, (3, 1))

    low_rows = (row == 4) | (row == 7)
    low_2 = low_rows & (col == 2)

    @pl.when(low_2)
    def _():
        load_first.wait()
        arrived(x_own, x_sem)
        stage_f[0] = product(first[...], x_own[...])
        send(low_2, stage_f.at[0], acc_f.at[0], 18, acc_f_sem.at[0], sibling)
        arrived(blocks.at[0], block_sem.at[0])
        stage_f[1] = product(blocks[0], x_own[...])
        send(low_2, stage_f.at[1], acc_f.at[1], 19, acc_f_sem.at[1], sibling)

    for r, rows in ((4, (4, 5)), (7, (6, 7))):

        @pl.when(here((r, 3)))
        def _(r=r, rows=rows):
            load_first.wait()
            for i, target in enumerate(rows):
                j = 0 if target == r else 1
                if j == 1:
                    arrived(blocks.at[0], block_sem.at[0])
                arrived(acc_b.at[j], acc_b_sem.at[j])
                arrived(acc_f.at[j], acc_f_sem.at[j])
                stage_f[j] = acc_b[j].astype(F32) - acc_f[j]
                if i == 0:
                    arrived(x_own, x_sem)
                    for c in (0, 1):
                        pl.semaphore_signal(go_sem, inc=1, device_id=(r, c), device_id_type=MESH)
                block = first[...] if target == r else blocks[0]
                stage_b[i] = (stage_f[j] - product(block, x_own[...])).astype(BF16)
                send((r, 3), stage_b.at[i], acc_b.at[target - 4], 18 + i, acc_b_sem.at[target - 4], SOLVE_47)

    @pl.when(here(SOLVE_47))
    def _():
        when = SOLVE_47
        load_inv.wait()
        split_inverse(0)
        load_first.wait()
        load_right.wait()
        place = {(1, 0): blocks.at[0], (2, 0): first, (2, 1): blocks.at[1]}
        place |= {(3, 0): blocks.at[2], (3, 1): blocks.at[3], (3, 2): blocks.at[4]}
        for slot in range(5):
            arrived(blocks.at[slot], block_sem.at[slot])
        for slot in range(1, 4):
            inverse_arrived(slot)
        for q in range(4):
            arrived(acc_b.at[q], acc_b_sem.at[q])
            total = acc_b[q].astype(F32)
            if q > 0:
                total -= acc_f[q]
            value = solve(q, total)
            x_stage[q] = value.astype(BF16)
            x_full[q] = value
            scatter(when, q, 4 + q, 20 + 4 * q)
            if q < 2:
                send(when, x_full.at[q], x_in, 36 + q, x_in_sem, (4 + q, 0))
            for r in range(q + 1, 4):
                done = product(place[r, q][...], x_stage[q])
                acc_f[r] = done if q == 0 else acc_f[r] + done
        send(when, x_full.at[2], x_in, 38, x_in_sem, (6, 0))
    for k in range(2, 8):
        relay_quarter(k)

    waited = rows_of(0, 0, 8) | here((0, 1)) | low_1 | (low_rows & (col < 4)) | here(SOLVE_23)

    @pl.when(jnp.logical_not(waited) & (col < 2))
    def _():
        arrived(x_own, x_sem)

    @pl.when(jnp.logical_not(waited) & (col >= 2))
    def _():
        @pl.when(z != relay_z)
        def _():
            arrived(x_own, x_sem)

        @pl.when(z == relay_z)
        def _():
            arrived(x_own.at[pl.ds(0, 3 * quarter)], x_sem)

    @pl.when(here(column_root[1]))
    def _():
        spread_from_root(1)

    relay = is_root & (y != 0)
    peers = [(i, (y * N_Z + (z + d) % N_Z, col)) for i, d in enumerate((4, 3, 5, 2, 6, 1, 7))]

    @pl.when(relay)
    def _():
        for i, peer in peers:
            send(relay, x_own, x_own, 9 + i, x_sem, peer)

    always = row >= 0
    waited_first = rows_of(0, 2, 8) | low_1 | (low_rows & (col < 4))
    waited_first = waited_first | here(SOLVE_1) | here(SOLVE_23) | here(SOLVE_47)

    @pl.when(jnp.logical_not(waited_first))
    def _():
        load_first.wait()

    send(always, x_own, x_mate, 64, mate_sem.at[0], sibling)
    load_ours.wait()
    half_panel = panel[0].reshape(4 * 2 * half, 2 * half)
    ours[...] = product(half_panel, x_own[...]).reshape(4, 2 * half, width)
    arrived(panel.at[1], mate_sem.at[1])
    arrived(x_mate, mate_sem.at[0])

    @pl.when(low_rows & (col < 2))
    def _():
        pl.semaphore_wait(go_sem, 1)

    value = x_mate[...]
    for j, d in enumerate((2, 1, 3, 0)):
        owner = (x + d) % N_X
        total = ours[owner] + product(panel[1, owner], value)
        if d > 0:
            sums[j] = total.astype(BF16)
            send(always, sums.at[j], cross_in.at[d - 1], 68 + j, cross_sem.at[d - 1], (row, owner * 2 + core))
    @pl.when(here(SOLVE_23))
    def _():
        for q in range(2):
            send(SOLVE_23, x_full.at[q], x_in, 36 + q, x_in_sem, (2 + q, 0))

    @pl.when(here(SOLVE_47))
    def _():
        send(SOLVE_47, x_full.at[3], x_in, 39, x_in_sem, (7, 0))

    load_own.wait()
    total = right_own[...] - total
    for d in range(3):
        arrived(cross_in.at[d], cross_sem.at[d])
        total -= cross_in[d].astype(F32)
    out[...] = total

    solved = plane_row(0, 8) & (col == 0)

    @pl.when(solved & (row < 2))
    def _():
        out[...] = x_full[0]

    @pl.when(solved & (row >= 2))
    def _():
        arrived(x_in, x_in_sem)
        out[...] = x_in[...]

    @pl.when(jnp.logical_not(is_source | here(SOLVE_0) | here(SOLVE_47)))
    def _():
        load_inv.wait()

    read_right = here((3, 0)) | here(SOLVE_0) | here(SOLVE_1) | here(SOLVE_23) | here(SOLVE_47) | low_1

    @pl.when(jnp.logical_not(read_right))
    def _():
        load_right.wait()

    buffers = [x_own, stage_f.at[0], relays.at[0]]

    def same_size(shape, dtype):
        for buffer in buffers:
            if buffer.shape == shape and buffer.dtype == dtype:
                return buffer
        if shape == first.shape:
            return first
        return part(0, 0, shape[1] // quarter - 1)

    remote(panel.at[1], panel.at[1], 65, mate_sem.at[1], sibling).wait_send()

    def sent(s, shape, dtype):
        ref = same_size(shape, dtype)
        remote(ref, ref, s, x_sem, sibling).wait_send()

    groups = {}
    for when, s, shape, dtype in pending:
        if isinstance(when, tuple):
            groups.setdefault(when[0], {}).setdefault(when[1], []).append((s, shape, dtype))
        elif when is always:
            sent(s, shape, dtype)

    def sent_in_row(r):
        @pl.when(row == r)
        def _():
            for c, copies in groups[r].items():

                @pl.when(col == c)
                def _(copies=copies):
                    for copy in copies:
                        sent(*copy)

    @pl.when(y == 0)
    def _():
        for r in groups:
            if r < N_Z:
                sent_in_row(r)
        for when, s, shape, dtype in pending:
            if not isinstance(when, tuple) and when is not always and when is not relay:

                @pl.when(when)
                def _(s=s, shape=shape, dtype=dtype):
                    sent(s, shape, dtype)

    @pl.when(y != 0)
    def _():
        for r in groups:
            if r >= N_Z:
                sent_in_row(r)

        @pl.when(relay)
        def _():
            for when, s, shape, dtype in pending:
                if when is relay:
                    sent(s, shape, dtype)

    @pl.when(is_relay)
    def _():
        for k, waits in relay_waits.items():

            @pl.when((core == k % 2) & (z == (2 if k < 4 else 6)))
            def _(waits=waits):
                for wanted, s in waits:

                    @pl.when(wanted())
                    def _(s=s):
                        remote(relays.at[0], relays.at[0], s, x_sem, sibling).wait_send()


def body(lower, slab, inverses):
    row_blocks, _, order, _, _, _ = lower.shape
    width = slab.shape[3]
    vmem = pltpu.VMEM
    dma = pltpu.SemaphoreType.DMA
    scratch = [
        vmem((order, order), BF16),
        vmem((2, row_blocks // 2, order, order), BF16),
        vmem((order, order), F32),
        vmem((4, 2, order, order), BF16),
        vmem((5, order, order), BF16),
        vmem((order, width), F32),
        vmem((order, width), F32),
        vmem((order, width), BF16),
        vmem((4, order, width), BF16),
        vmem((4, order, width), F32),
        vmem((order, width), F32),
        vmem((4, order, width), F32),
        vmem((4, order, width), BF16),
        vmem((2, order, width), F32),
        vmem((2, order, width), BF16),
        vmem((2, order // 4, width), BF16),
        vmem((order, width), BF16),
        vmem((4, order, width), F32),
        vmem((3, order, width), BF16),
        vmem((3, order, width), BF16),
        dma((5,)),
        dma((72,)),
        dma,
        dma,
        dma,
        pltpu.SemaphoreType.REGULAR,
        dma((2,)),
        dma((4, 2, 4)),
        dma((5,)),
        dma((4,)),
        dma((4,)),
        dma((2,)),
        dma((3,)),
    ]
    result = pl.pallas_call(
        kernel,
        name="window_solve",
        out_shape=jax.ShapeDtypeStruct((order, width), F32),
        in_specs=[pl.BlockSpec(memory_space=pltpu.HBM)] * 3,
        out_specs=pl.BlockSpec(memory_space=pltpu.VMEM),
        scratch_shapes=scratch,
        compiler_params=pltpu.CompilerParams(
            collective_id=0, has_side_effects=True, vmem_limit_bytes=53 << 20
        ),
    )(
        lower.reshape(row_blocks // 2, 2, order, order),
        slab.reshape(row_blocks, order, width),
        inverses.reshape(order, order),
    )
    return result.reshape(1, 1, order, width)


def solution(mesh):
    in_specs = (
        P(None, "row", None, None, "col", None),
        P(None, "row", None, None),
        P(None, "col", None, None),
    )
    out_specs = P("col", "row", None, None)
    return jax.shard_map(body, mesh=mesh, in_specs=in_specs, out_specs=out_specs, check_vma=False)
```

```python
import jax
import jax.numpy as jnp
from jax import lax
from jax.experimental import pallas as pl
from jax.experimental.pallas import tpu as pltpu
from jax.sharding import PartitionSpec as P

MESH = pl.DeviceIdType.MESH
F32 = jnp.float32
BF16 = jnp.bfloat16

N_Z, N_Y, N_X = 8, 4, 4
SOLVE_0 = (0, 0)
SOLVE_1 = (1, 0)
SOLVE_23 = (2, 1)
SOLVE_47 = (6, 4)
HIGH = tuple((0, b) for b in range(4))
LOW = tuple((1, b) for b in range(4))
INVERSE_SENDS = (
    ((1, 1), SOLVE_1, 0, HIGH + LOW),
    ((9, 2), SOLVE_23, 0, (HIGH[0], HIGH[3])),
    ((25, 2), SOLVE_23, 0, (HIGH[1], HIGH[2])),
    ((12, 3), SOLVE_23, 1, (HIGH[0], HIGH[3])),
    ((28, 3), SOLVE_23, 1, (HIGH[1], HIGH[2])),
    ((6, 5), SOLVE_47, 1, HIGH),
    ((14, 6), SOLVE_47, 2, HIGH),
    ((30, 7), SOLVE_47, 3, HIGH),
)
BLOCK_SENDS = (
    ((3, 1), SOLVE_23, 0),
    ((3, 2), SOLVE_23, 1),
    ((5, 4), SOLVE_47, 0),
    ((6, 5), SOLVE_47, 1),
    ((7, 4), SOLVE_47, 2),
    ((7, 5), SOLVE_47, 3),
    ((7, 6), SOLVE_47, 4),
    *(((5, c), (4, c), 0) for c in (2, 3)),
    *(((6, c), (7, c), 0) for c in (2, 3)),
)


def special_pairs():
    pairs = {(s, t) for s, t, _, _ in INVERSE_SENDS} | {(s, t) for s, t, _ in BLOCK_SENDS}
    pairs |= {(SOLVE_0, (z, 0)) for z in (1, 2, 3)} | {(SOLVE_1, (z, 1)) for z in (0, 1, 2, 4, 5)}
    pairs |= {((r, 1), (4 if r < 6 else 7, 3)) for r in range(4, 8)}
    pairs |= {((3, 0), (4, 0)), ((0, 1), (5, 0))} | {((0, 1), (r, c)) for r in (6, 7) for c in (0, 1)}
    pairs |= {((3, 0), SOLVE_23)}
    pairs |= {(SOLVE_23, (r, c)) for c in (2, 3) for r in (4, 7)}
    pairs |= {(SOLVE_23, (2, c)) for c in range(8) if c != 1}
    pairs |= {(SOLVE_47, (6, c)) for c in range(8) if c != 4}
    pairs |= {((4, 3), (7, 3))} | {((r, 3), SOLVE_47) for r in (4, 7)} | {((r, 0), (r, 3)) for r in (4, 7)} | {((r, 1), (r, 3)) for r in (4, 7)}
    pairs |= {(SOLVE_47, (r, 0)) for r in range(4, 8)}
    return sorted({tuple(sorted(p)) for p in pairs})


def kernel(
    lower, slab, inverses, out,
    first, panel, inv, inv_parts, blocks, right, right_own, x_own, x_stage, x_full, x_in,
    acc_f, acc_b, stage_f, stage_b, relays, x_mate, ours, sums, cross_in,
    load_sem, send_sem, x_sem, x_in_sem, side_sem, relay_sem, inv_sem, block_sem, acc_f_sem, acc_b_sem, mate_sem, cross_sem,
):
    row = lax.axis_index("row")
    col = lax.axis_index("col")
    y, z = row // N_Z, row % N_Z
    x, core = col // 2, col % 2
    half = first.shape[0] // 2
    quarter = half // 2
    width = x_own.shape[1]

    def here(device):
        return (row == device[0]) & (col == device[1])

    def plane_row(r0, r1):
        return (row >= r0) & (row < r1)

    root_z = col
    sibling = (row, col + 1 - 2 * core)
    pending = []
    relay_waits = {}

    def remote(src, dst, s, recv, device):
        return pltpu.make_async_remote_copy(
            src_ref=src, dst_ref=dst, send_sem=send_sem.at[s], recv_sem=recv, device_id=device, device_id_type=MESH
        )

    def send(when, src, dst, s, recv, device):
        remote(src, dst, s, recv, device).start()
        if when is not None:
            pending.append((when, s, src.shape, src.dtype))

    def arrived(dst, recv):
        remote(dst, dst, 0, recv, sibling).wait_recv()

    load_first = pltpu.make_async_copy(lower.at[0, 0], first, load_sem.at[0])
    load_ours = pltpu.make_async_copy(lower.at[:, core], panel.at[0], load_sem.at[1])
    load_inv = pltpu.make_async_copy(inverses, inv, load_sem.at[2])
    load_right = pltpu.make_async_copy(slab.at[0], right, load_sem.at[3])
    load_own = pltpu.make_async_copy(slab.at[col], right_own, load_sem.at[4])
    load_inv.start()
    load_right.start()
    load_first.start()

    def clear_slot(slot):
        inv_parts[slot] = jnp.zeros(inv_parts.shape[1:], BF16)

    @pl.when(here(SOLVE_1))
    def _():
        clear_slot(0)

    @pl.when(here(SOLVE_23))
    def _():
        clear_slot(0)
        clear_slot(1)

    @pl.when(here(SOLVE_47))
    def _():
        clear_slot(1)
        clear_slot(2)
        clear_slot(3)

    barrier = pltpu.get_barrier_semaphore()

    def greet(device):
        pl.semaphore_signal(barrier, inc=1, device_id=device, device_id_type=MESH)

    count = jnp.int32(0)
    partners = {}
    for a, b in special_pairs():
        partners.setdefault(a, []).append(b)
        partners.setdefault(b, []).append(a)
    by_row = {}
    for device, others in partners.items():
        count += jnp.where(here(device), len(others), 0)
        by_row.setdefault(device[0], []).append((device[1], others))

    def greet_row(r):
        @pl.when(row == r)
        def _():
            for c, others in by_row[r]:

                @pl.when(col == c)
                def _(others=others):
                    for other in others:
                        greet(other)

    @pl.when(y == 0)
    def _():
        for r in by_row:
            if r < N_Z:
                greet_row(r)

    @pl.when(y != 0)
    def _():
        for r in by_row:
            if r >= N_Z:
                greet_row(r)

    greet(sibling)
    for d in range(1, N_X):
        greet((row, (x + d) % N_X * 2 + core))
    count += N_X
    is_root = (z == root_z) & (col < 2)
    in_other = (col < 2) & (y != 0)

    @pl.when(is_root & in_other)
    def _():
        for d in range(1, N_Z):
            greet((y * N_Z + (z + d) % N_Z, col))

    @pl.when(jnp.logical_not(is_root) & in_other)
    def _():
        greet((y * N_Z + root_z, col))

    count += jnp.where(in_other, jnp.where(is_root, N_Z - 1, 1), 0)
    is_relay = (z == 2) | (z == 6)
    relay_z = jnp.where(col < 4, 2, 6)

    @pl.when(is_relay)
    def _():
        for k in range(2, 8):

            @pl.when((core == k % 2) & (z == (2 if k < 4 else 6)))
            def _(k=k):
                for d in range(1, N_Z):
                    greet((y * N_Z + (z + d) % N_Z, k))

                @pl.when(col != k)
                def _():
                    greet((row, k))

    count += jnp.where(z == 2, N_Z - 1 + jnp.where(x == 1, 0, 1), 0)
    count += jnp.where(z == 6, 2 * (N_Z - 1) + jnp.where(x >= 2, 1, 2), 0)

    @pl.when(col >= 2)
    def _():
        for q in range(N_X):

            @pl.when((z != relay_z) | (q != x))
            def _(q=q):
                greet((y * N_Z + relay_z, 2 * q + core))

    count += jnp.where(col >= 2, jnp.where(z == jnp.where(col < 4, 2, 6), N_X - 1, N_X), 0)
    in_line = is_root | is_relay

    @pl.when(in_line & (y == 0))
    def _():
        for d in range(1, N_Y):
            greet((d * N_Z + z, col))

    @pl.when(in_line & (y != 0))
    def _():
        greet((z, col))

    count += jnp.where(in_line, jnp.where(y == 0, N_Y - 1, 1), 0)
    def split_inverse(slot):
        value = inv[...]
        high = value.astype(BF16)
        inv_parts[slot, 0] = high
        inv_parts[slot, 1] = (value - high.astype(F32)).astype(BF16)

    def part(slot, piece, b):
        return inv_parts.at[slot, piece, pl.ds(b * quarter, quarter), pl.ds(0, (b + 1) * quarter)]

    def inverse_arrived(slot, parts=HIGH):
        for piece, b in parts:
            arrived(part(slot, piece, b), inv_sem.at[slot, piece, b])

    def solve(slot, total, low_part=False):
        high = total.astype(BF16)
        low = (total - high.astype(F32)).astype(BF16)
        both = jnp.concatenate([high, low], axis=1)

        whole = product(inv_parts[slot, 0], both)
        if low_part:
            whole += product(inv_parts[slot, 1], both)
        return whole[:, :width] + whole[:, width:]

    def product(block, value):
        return jnp.dot(block, value, preferred_element_type=F32)

    is_source = here(INVERSE_SENDS[0][0])
    for source, _, _, _ in INVERSE_SENDS[1:]:
        is_source |= here(source)

    @pl.when(is_source)
    def _():
        load_inv.wait()
        split_inverse(0)

    @pl.when(here(SOLVE_0))
    def _():
        load_inv.wait()
        split_inverse(0)
        load_right.wait()
        value = solve(0, right[...], low_part=True)
        x_own[...] = value.astype(BF16)
        x_full[0] = value

    pl.semaphore_wait(barrier, count)

    load_ours.start()
    load_own.start()

    for source, solver, slot in BLOCK_SENDS:

        @pl.when(here(source))
        def _(source=source, solver=solver, slot=slot):
            send(source, lower.at[0, 0], blocks.at[slot], 0, block_sem.at[slot], solver)

    for source, solver, slot, pieces in INVERSE_SENDS:

        @pl.when(here(source))
        def _(source=source, solver=solver, slot=slot, pieces=pieces):
            for piece, b in pieces:
                s = 1 + piece * 4 + b
                send(source, part(0, piece, b), part(slot, piece, b), s, inv_sem.at[slot, piece, b], solver)

    remote(lower.at[:, 1 - core], panel.at[1], 65, mate_sem.at[1], sibling).start()

    column_root = [SOLVE_0, (1, 1)]
    in_plane = [(1, 3, 2), ()]

    def spread_from_root(c):
        when = column_root[c]
        root_row = column_root[c][0]
        for i, target in enumerate(in_plane[c][:1]):
            send(when, x_own, x_own, 9 + i, x_sem, (target, c))
        if c == 0:
            send(when, x_own, x_stage.at[0], 19, side_sem, (0, 1))
        for i, target in enumerate(in_plane[c]):
            if i > 0:
                send(when, x_own, x_own, 9 + i, x_sem, (target, c))
        for d in (2, 1, 3):
            send(when, x_own, x_own, 15 + d, x_sem, (d * N_Z + root_row, c))

    @pl.when(here(SOLVE_0))
    def _():
        spread_from_root(0)

    @pl.when(here(SOLVE_1))
    def _():
        load_right.wait()
        load_first.wait()
        inverse_arrived(0, HIGH + LOW)
        arrived(x_own, x_sem)
        value = solve(0, right[...] - product(first[...], x_own[...]), low_part=True)
        x_stage[0] = value.astype(BF16)
        x_full[0] = value
        send(SOLVE_1, x_stage.at[0], x_own, 9, x_sem, (2, 1))
        send(SOLVE_1, x_stage.at[0], x_own, 10, x_sem, (4, 1))
        for i, target in enumerate((5, 0, 1)):
            send(SOLVE_1, x_stage.at[0], x_own, 11 + i, x_sem, (target, 1))

    def rows_of(c, r0, r1):
        return plane_row(r0, r1) & (col == c)

    @pl.when(here((2, 0)))
    def _():
        load_first.wait()
        arrived(x_own, x_sem)
        stage_f[0] = product(first[...], x_own[...])
        send((2, 0), stage_f.at[0], acc_f.at[0], 19, acc_f_sem.at[0], sibling)

    @pl.when(here((3, 0)))
    def _():
        load_right.wait()
        load_first.wait()
        arrived(x_own, x_sem)
        stage_b[0] = (right[...] - product(first[...], x_own[...])).astype(BF16)
        send((3, 0), stage_b.at[0], acc_b.at[0], 19, acc_b_sem.at[0], SOLVE_23)
        send((3, 0), x_own, x_own, 9, x_sem, (4, 0))

    @pl.when(here((0, 1)))
    def _():
        arrived(x_stage.at[0], side_sem)
        for i, r in enumerate((5, 6, 7)):
            send((0, 1), x_stage.at[0], x_own, 9 + i, x_sem, (r, 0))
        arrived(x_own, x_sem)
        for i, r in enumerate((6, 7)):
            send((0, 1), x_own, x_own, 12 + i, x_sem, (r, 1))

    low_0 = rows_of(0, 4, 8)
    low_1 = rows_of(1, 4, 8)

    @pl.when(low_0)
    def _():
        load_first.wait()
        arrived(x_own, x_sem)
        stage_f[0] = product(first[...], x_own[...])
        send(low_0, stage_f.at[0], acc_f.at[0], 18, acc_f_sem.at[0], sibling)

    @pl.when(low_1)
    def _():
        load_first.wait()
        arrived(x_own, x_sem)
        load_right.wait()
        arrived(acc_f.at[0], acc_f_sem.at[0])
        stage_b[0] = (right[...] - acc_f[0] - product(first[...], x_own[...])).astype(BF16)

    for r, target, slot in ((4, 4, 0), (5, 4, 1), (6, 7, 1), (7, 7, 0)):

        @pl.when(here((r, 1)))
        def _(r=r, target=target, slot=slot):
            send((r, 1), stage_b.at[0], acc_b.at[slot], 19, acc_b_sem.at[slot], (target, 3))

    def scatter(when, slot, k, s):
        solver = SOLVE_23 if k < 4 else SOLVE_47
        for q in range(N_X):
            device = (solver[0], 2 * q + k % 2)
            if device != solver:
                rows = pl.ds(q * quarter, quarter)
                send(when, x_stage.at[slot, rows], relays.at[max(k // 2 - 2, 0)], s + q, relay_sem.at[max(k // 2 - 2, 0)], device)

    own_rows = pl.ds(pl.multiple_of(x * quarter, quarter), quarter)
    other_planes = [(d * N_Z + z, col) for d in range(1, N_Y)]
    other_z = [y * N_Z + (z + d) % N_Z for d in (2, 3, 4, 5, 1, 6, 7)]

    def relay_quarter(k):
        solver = SOLVE_23 if k < 4 else SOLVE_47
        slot = max(k // 2 - 2, 0)
        piece = relays.at[slot]
        base = 40 + 12 * slot
        waits = relay_waits.setdefault(k, [])

        place = lambda: (z == solver[0]) & (core == k % 2)

        @pl.when(place())
        def _():
            @pl.when(here(solver))
            def _():
                q = solver[1] // 2
                relays[slot] = x_stage[k - 2 if k < 4 else k - 4, q * quarter : (q + 1) * quarter]

            @pl.when(jnp.logical_not(here(solver)))
            def _():
                arrived(piece, relay_sem.at[slot])

            @pl.when(y == 0)
            def _():
                for i, device in enumerate(other_planes):
                    send(None, piece, piece, base + i, relay_sem.at[slot], device)
                    waits.append((lambda: y == 0, base + i))

            for i, target in enumerate(other_z):
                direct = (lambda target=target: (y != 0) | ((target != 4) & (target != 7))) if k < 4 else (lambda: True)

                @pl.when(direct())
                def _(i=i, target=target, direct=direct):
                    waits.append((direct, base + 3 + i))
                    send(None, piece, x_own.at[own_rows], base + 3 + i, x_sem, (target, k))

            @pl.when(col == k)
            def _():
                x_own[own_rows] = relays[slot]

            @pl.when(col != k)
            def _():
                waits.append((lambda: col != k, base + 10))
                send(None, piece, x_own.at[own_rows], base + 10, x_sem, (row, k))

    @pl.when(here(SOLVE_23))
    def _():
        when = SOLVE_23
        load_right.wait()
        load_first.wait()
        arrived(acc_f.at[0], acc_f_sem.at[0])
        arrived(x_own, x_sem)
        total = right[...] - acc_f[0] - product(first[...], x_own[...])
        inverse_arrived(0)
        value = solve(0, total)
        x_stage[0] = value.astype(BF16)
        x_full[0] = value
        for i, r in enumerate((4, 7)):
            send(when, x_stage.at[0], x_own, 20 + i, x_sem, (r, 2))
        scatter(when, 0, 2, 26)
        for slot in range(2):
            arrived(blocks.at[slot], block_sem.at[slot])
        arrived(acc_b.at[0], acc_b_sem.at[0])
        total = acc_b[0].astype(F32) - (product(blocks[0], x_own[...]) + product(blocks[1], x_stage[0]))
        inverse_arrived(1)
        value = solve(1, total)
        x_stage[1] = value.astype(BF16)
        x_full[1] = value
        for i, r in enumerate((4, 7)):
            send(when, x_stage.at[1], x_own, 23 + i, x_sem, (r, 3))
        scatter(when, 1, 3, 29)
        send(when, x_own, x_own, 33, x_sem, (3, 1))

    low_rows = (row == 4) | (row == 7)
    low_2 = low_rows & (col == 2)

    @pl.when(low_2)
    def _():
        load_first.wait()
        arrived(x_own, x_sem)
        stage_f[0] = product(first[...], x_own[...])
        send(low_2, stage_f.at[0], acc_f.at[0], 18, acc_f_sem.at[0], sibling)
        arrived(blocks.at[0], block_sem.at[0])
        stage_f[1] = product(blocks[0], x_own[...])
        send(low_2, stage_f.at[1], acc_f.at[1], 19, acc_f_sem.at[1], sibling)

    for r, rows in ((4, (4, 5)), (7, (6, 7))):

        @pl.when(here((r, 3)))
        def _(r=r, rows=rows):
            load_first.wait()
            for i, target in enumerate(rows):
                j = 0 if target == r else 1
                if j == 1:
                    arrived(blocks.at[0], block_sem.at[0])
                arrived(acc_b.at[j], acc_b_sem.at[j])
                arrived(acc_f.at[j], acc_f_sem.at[j])
                stage_f[j] = acc_b[j].astype(F32) - acc_f[j]
                if i == 0:
                    arrived(x_own, x_sem)
                block = first[...] if target == r else blocks[0]
                stage_b[i] = (stage_f[j] - product(block, x_own[...])).astype(BF16)
                send((r, 3), stage_b.at[i], acc_b.at[target - 4], 18 + i, acc_b_sem.at[target - 4], SOLVE_47)

    @pl.when(here(SOLVE_47))
    def _():
        when = SOLVE_47
        load_inv.wait()
        split_inverse(0)
        load_first.wait()
        load_right.wait()
        place = {(1, 0): blocks.at[0], (2, 0): first, (2, 1): blocks.at[1]}
        place |= {(3, 0): blocks.at[2], (3, 1): blocks.at[3], (3, 2): blocks.at[4]}
        for slot in range(5):
            arrived(blocks.at[slot], block_sem.at[slot])
        for slot in range(1, 4):
            inverse_arrived(slot)
        for q in range(4):
            arrived(acc_b.at[q], acc_b_sem.at[q])
            total = acc_b[q].astype(F32)
            if q > 0:
                total -= acc_f[q]
            value = solve(q, total)
            x_stage[q] = value.astype(BF16)
            x_full[q] = value
            scatter(when, q, 4 + q, 20 + 4 * q)
            if q < 2:
                send(when, x_full.at[q], x_in, 36 + q, x_in_sem, (4 + q, 0))
            for r in range(q + 1, 4):
                done = product(place[r, q][...], x_stage[q])
                acc_f[r] = done if q == 0 else acc_f[r] + done
        send(when, x_full.at[2], x_in, 38, x_in_sem, (6, 0))
    for k in range(2, 8):
        relay_quarter(k)

    waited = rows_of(0, 0, 8) | here((0, 1)) | low_1 | (low_rows & (col < 4)) | here(SOLVE_23)

    @pl.when(jnp.logical_not(waited) & (col < 2))
    def _():
        arrived(x_own, x_sem)

    @pl.when(jnp.logical_not(waited) & (col >= 2))
    def _():
        @pl.when(z != relay_z)
        def _():
            arrived(x_own, x_sem)

        @pl.when(z == relay_z)
        def _():
            arrived(x_own.at[pl.ds(0, 3 * quarter)], x_sem)

    @pl.when(here(column_root[1]))
    def _():
        spread_from_root(1)

    relay = is_root & (y != 0)
    peers = [(i, (y * N_Z + (z + d) % N_Z, col)) for i, d in enumerate((4, 3, 5, 2, 6, 1, 7))]

    @pl.when(relay)
    def _():
        for i, peer in peers:
            send(relay, x_own, x_own, 9 + i, x_sem, peer)

    always = row >= 0
    waited_first = rows_of(0, 2, 8) | low_1 | (low_rows & (col < 4))
    waited_first = waited_first | here(SOLVE_1) | here(SOLVE_23) | here(SOLVE_47)

    @pl.when(jnp.logical_not(waited_first))
    def _():
        load_first.wait()

    send(always, x_own, x_mate, 64, mate_sem.at[0], sibling)
    load_ours.wait()
    half_panel = panel[0].reshape(4 * 2 * half, 2 * half)
    ours[...] = product(half_panel, x_own[...]).reshape(4, 2 * half, width)
    arrived(panel.at[1], mate_sem.at[1])
    arrived(x_mate, mate_sem.at[0])

    value = x_mate[...]
    for j, d in enumerate((2, 1, 3, 0)):
        owner = (x + d) % N_X
        total = ours[owner] + product(panel[1, owner], value)
        if d > 0:
            sums[j] = total.astype(BF16)
            send(always, sums.at[j], cross_in.at[d - 1], 68 + j, cross_sem.at[d - 1], (row, owner * 2 + core))
    @pl.when(here(SOLVE_23))
    def _():
        for q in range(2):
            send(SOLVE_23, x_full.at[q], x_in, 36 + q, x_in_sem, (2 + q, 0))

    @pl.when(here(SOLVE_47))
    def _():
        send(SOLVE_47, x_full.at[3], x_in, 39, x_in_sem, (7, 0))

    load_own.wait()
    total = right_own[...] - total
    for d in range(3):
        arrived(cross_in.at[d], cross_sem.at[d])
        total -= cross_in[d].astype(F32)
    out[...] = total

    solved = plane_row(0, 8) & (col == 0)

    @pl.when(solved & (row < 2))
    def _():
        out[...] = x_full[0]

    @pl.when(solved & (row >= 2))
    def _():
        arrived(x_in, x_in_sem)
        out[...] = x_in[...]

    @pl.when(jnp.logical_not(is_source | here(SOLVE_0) | here(SOLVE_47)))
    def _():
        load_inv.wait()

    read_right = here((3, 0)) | here(SOLVE_0) | here(SOLVE_1) | here(SOLVE_23) | here(SOLVE_47) | low_1

    @pl.when(jnp.logical_not(read_right))
    def _():
        load_right.wait()

    buffers = [x_own, stage_f.at[0], relays.at[0]]

    def same_size(shape, dtype):
        for buffer in buffers:
            if buffer.shape == shape and buffer.dtype == dtype:
                return buffer
        if shape == first.shape:
            return first
        return part(0, 0, shape[1] // quarter - 1)

    remote(panel.at[1], panel.at[1], 65, mate_sem.at[1], sibling).wait_send()

    def sent(s, shape, dtype):
        ref = same_size(shape, dtype)
        remote(ref, ref, s, x_sem, sibling).wait_send()

    groups = {}
    for when, s, shape, dtype in pending:
        if isinstance(when, tuple):
            groups.setdefault(when[0], {}).setdefault(when[1], []).append((s, shape, dtype))
        elif when is always:
            sent(s, shape, dtype)

    def sent_in_row(r):
        @pl.when(row == r)
        def _():
            for c, copies in groups[r].items():

                @pl.when(col == c)
                def _(copies=copies):
                    for copy in copies:
                        sent(*copy)

    @pl.when(y == 0)
    def _():
        for r in groups:
            if r < N_Z:
                sent_in_row(r)
        for when, s, shape, dtype in pending:
            if not isinstance(when, tuple) and when is not always and when is not relay:

                @pl.when(when)
                def _(s=s, shape=shape, dtype=dtype):
                    sent(s, shape, dtype)

    @pl.when(y != 0)
    def _():
        for r in groups:
            if r >= N_Z:
                sent_in_row(r)

        @pl.when(relay)
        def _():
            for when, s, shape, dtype in pending:
                if when is relay:
                    sent(s, shape, dtype)

    @pl.when(is_relay)
    def _():
        for k, waits in relay_waits.items():

            @pl.when((core == k % 2) & (z == (2 if k < 4 else 6)))
            def _(waits=waits):
                for wanted, s in waits:

                    @pl.when(wanted())
                    def _(s=s):
                        remote(relays.at[0], relays.at[0], s, x_sem, sibling).wait_send()


def body(lower, slab, inverses):
    row_blocks, _, order, _, _, _ = lower.shape
    width = slab.shape[3]
    vmem = pltpu.VMEM
    dma = pltpu.SemaphoreType.DMA
    scratch = [
        vmem((order, order), BF16),
        vmem((2, row_blocks // 2, order, order), BF16),
        vmem((order, order), F32),
        vmem((4, 2, order, order), BF16),
        vmem((5, order, order), BF16),
        vmem((order, width), F32),
        vmem((order, width), F32),
        vmem((order, width), BF16),
        vmem((4, order, width), BF16),
        vmem((4, order, width), F32),
        vmem((order, width), F32),
        vmem((4, order, width), F32),
        vmem((4, order, width), BF16),
        vmem((2, order, width), F32),
        vmem((2, order, width), BF16),
        vmem((2, order // 4, width), BF16),
        vmem((order, width), BF16),
        vmem((4, order, width), F32),
        vmem((3, order, width), BF16),
        vmem((3, order, width), BF16),
        dma((5,)),
        dma((72,)),
        dma,
        dma,
        dma,
        dma((2,)),
        dma((4, 2, 4)),
        dma((5,)),
        dma((4,)),
        dma((4,)),
        dma((2,)),
        dma((3,)),
    ]
    result = pl.pallas_call(
        kernel,
        name="window_solve",
        out_shape=jax.ShapeDtypeStruct((order, width), F32),
        in_specs=[pl.BlockSpec(memory_space=pltpu.HBM)] * 3,
        out_specs=pl.BlockSpec(memory_space=pltpu.VMEM),
        scratch_shapes=scratch,
        compiler_params=pltpu.CompilerParams(
            collective_id=0, has_side_effects=True, vmem_limit_bytes=53 << 20
        ),
    )(
        lower.reshape(row_blocks // 2, 2, order, order),
        slab.reshape(row_blocks, order, width),
        inverses.reshape(order, order),
    )
    return result.reshape(1, 1, order, width)


def solution(mesh):
    in_specs = (
        P(None, "row", None, None, "col", None),
        P(None, "row", None, None),
        P(None, "col", None, None),
    )
    out_specs = P("col", "row", None, None)
    return jax.shard_map(body, mesh=mesh, in_specs=in_specs, out_specs=out_specs, check_vma=False)
```
